32 devices in a mesh: grp: 2 (over y), tok: 4 (over z), fac: 2 (over x), sub: 2 (over core).
Axes of the slice: x: 2, y: 2, z: 4, core: 2. Of those that a mesh axis runs over, the one named last changes fastest.
Arguments:
- activations: bfloat16 [1024, 5120], P(('grp', 'tok')), parts along dimension 0, may hold values from -6 to 6
- gradients: bfloat16 [1024, 13824], P(('grp', 'tok')), parts along dimension 0, may hold values from -6 to 6
- tok_class: int32 [1024, 1], P('grp'), parts along dimension 0, may hold values from 0 to 1; in each aligned block of 64 rows (0 to 63, 64 to 127, ...) at most 40 rows name the same one
- query_inputs: bfloat16 [1024, 5120], P('grp', 'tok'), parts along dimension 0, may hold values from -6 to 6
- query_gradients: bfloat16 [1024, 13824], P('grp', 'tok'), parts along dimension 0, may hold values from -6 to 6
- query_class: int32 [1024, 1], P('grp'), parts along dimension 0, may hold values from 0 to 1; in each aligned block of 256 rows (0 to 255, 256 to 511, ...) at most 160 rows name the same one
- basis_a: bfloat16 [2, 5120, 5120], P(None, 'tok', ('fac', 'sub')), may hold values from -0.078125 to 0.078125
- basis_g: bfloat16 [2, 13824, 13824], P(None, 'tok', ('fac', 'sub')), may hold values from -0.0546875 to 0.0546875
- eigen_a: float32 [2, 5120], P(None, ('fac', 'sub')), may hold values from 0.5 to 8
- eigen_g: float32 [2, 13824], P(None, ('fac', 'sub')), may hold values from 0.5 to 8
Outputs:
- scores: float32 [512, 1024], P('fac', ('grp', 'tok', 'sub')), parts along dimension 1
The draws below stay inside these ranges and needn't reach their ends.
There are 2 independent parts, one for each index of `grp`. The reference program is written for one: setup_inputs(seed, part) draws one part's arguments, and reference() takes and returns one part's arrays. A program takes and returns all parts, laid end to end along the dimension named above; an argument that names none is the same for every part. Nothing has to cross between parts.
Inputs may be any that keep to these rules, and one draw needn't show every extreme that they name: `tok_class`: in each half of the 128 training tokens of one index of tok no class is named by more than 40 tokens, and in every draw some class reaches that. `query_class`: the queries fall into equal blocks in order, one for each index of fac; in each block no class is named by more than 160 queries, and in every draw some class reaches that.
All inputs are finite; a program needn't handle non-finite values.
Results may differ from the reference program's by a relative error of at most 0.0003.
Values may be sent and summed in bfloat16 or wider, within the bound.
No kernel may reach another device: no remote copies, remote signals or barrier semaphores. Data moves between devices by JAX's collectives and lax.ppermute only.
A program may use at most 256 MiB of HBM per device.

```python
import math
import jax
import jax.numpy as jnp
import numpy as np
from jax import lax

D = 5120
FH = 13824
CLASSES = 2
QUERIES = 512
TOK_DEV = 128
TOKENS = 512
SLOT_CAP = 40
QUERY_CAP = 160
N_FAC = 2
N_SUB = 2


def block_scale(stream_key, extent, pieces, low, largest):
    def one(axis_at, parts):
        steps = jax.random.uniform(jax.random.fold_in(jax.random.fold_in(stream_key, 6), axis_at), (parts,), jnp.float32, low / len(pieces), largest / len(pieces))
        return jnp.repeat(jnp.exp(steps), extent[axis_at] // parts).reshape((-1,) + (1,) * (len(extent) - axis_at - 1))

    gain = one(*pieces[0])
    for cut in pieces[1:]:
        gain = gain * one(*cut)
    return gain


def shared_out(own_key, own, number, rows, number_of, top, bound, lean):
    sequence = jax.random.permutation(own_key, number_of)
    heavy_load, common = shares(number_of, rows * top, bound, lean, True), shares(number_of, rows * top, bound, lean, False)
    places = jnp.arange(number_of)

    def named(sizes, rotation):
        used = int((sizes > 0).sum())
        fixed = max(1, used // 4)
        moved = fixed + (places - fixed + rotation * (used - fixed)) % max(1, number_of - fixed)
        return jnp.zeros((number_of,), jnp.int32).at[sequence[jnp.where(places < fixed, places, moved)]].set(jnp.asarray(sizes, jnp.int32))

    sizes = jnp.where(number % 4 == 0, named(heavy_load, number // 4), named(common, number - number // 4 - 1))
    mixed = jax.random.permutation(jax.random.fold_in(own, 3), number_of)
    source_of, sink = mixed[0:number_of // 2 * 2:2], mixed[1:number_of // 2 * 2:2]
    slack = jnp.minimum(sizes[source_of] - 1, bound - sizes[sink]) // 2
    slack = jnp.where((source_of == sequence[0]) | (sink == sequence[0]) | (sizes[sink] == 0), 0, jnp.maximum(slack, 0))
    moved = jax.random.randint(jax.random.fold_in(own, 4), (number_of // 2,), 0, 1 << 20) % (slack + 1)
    sizes = sizes.at[source_of].add(-moved).at[sink].add(moved)
    items = jnp.searchsorted(jnp.cumsum(sizes), jnp.arange(rows * top), side="right").astype(jnp.int32)
    listing = items.reshape(top, rows).T
    listing = listing[jax.random.permutation(jax.random.fold_in(own, 1), rows)]
    rotation = jax.random.randint(jax.random.fold_in(own, 2), (rows, 1), 0, top)
    return jnp.take_along_axis(listing, (jnp.arange(top)[None, :] + rotation) % top, axis=1)


def shares(amount, total, limit, lean, full):
    weights = [(1 << 20) // math.isqrt(rank ** lean) + 1 for rank in range(1, amount + 1)]
    largest = limit if full else min(limit, max(-(-total // amount), total * weights[0] // sum(weights)))
    least = 1 if total - largest >= amount - 1 else 0
    given, spare = [largest] + [least] * (amount - 1), total - largest - least * (amount - 1)
    while spare > 0:
        free = [i for i in range(1, amount) if given[i] < largest] or [i for i in range(1, amount) if given[i] < limit]
        whole, left = sum([weights[i] for i in free]), spare
        for i in free:
            extra = min(limit - given[i], max(1, left * weights[i] // whole), spare)
            given[i] = given[i] + extra
            spare = spare - extra
    return np.array(given)


def bell_draw(own_key, extent, deviation, bound, shards=(), kind=jnp.bfloat16):
    drawn = deviation * jax.random.normal(own_key, extent, jnp.float32)
    if shards:
        drawn = drawn * block_scale(own_key, extent, shards, -0.22, 0.18)
    return jnp.clip(drawn, -bound, bound).astype(kind)


def setup_inputs(seed: int = 0, part: int = 0) -> dict:
    seeds = jax.random.split(jax.random.key(seed), 11)
    own_keys = jax.random.split(jax.random.fold_in(seeds[10], part), 11)
    activations = bell_draw(own_keys[0], (TOKENS, D), 1.0, 6.0, ((0, 4),))
    gradients = bell_draw(own_keys[1], (TOKENS, FH), 1.0, 6.0, ((0, 4),))
    tok_class_keys = jax.random.split(jax.random.fold_in(own_keys[2], 1), TOKENS // (TOK_DEV // N_SUB))
    tok_class_turns = jax.random.permutation(jax.random.fold_in(own_keys[2], 3), TOKENS // (TOK_DEV // N_SUB))
    tok_class = jax.vmap(lambda own, number: shared_out(jax.random.fold_in(own_keys[2], 2), own, number, TOK_DEV // N_SUB, CLASSES, 1, SLOT_CAP, 1))(tok_class_keys, tok_class_turns).reshape((TOKENS, 1))
    query_inputs = bell_draw(own_keys[3], (QUERIES, D), 1.0, 6.0, ((1, 4),))
    query_gradients = bell_draw(own_keys[4], (QUERIES, FH), 1.0, 6.0, ((1, 4),))
    query_class_keys = jax.random.split(jax.random.fold_in(own_keys[5], 1), QUERIES // (QUERIES // N_FAC))
    query_class_turns = jax.random.permutation(jax.random.fold_in(own_keys[5], 3), QUERIES // (QUERIES // N_FAC))
    query_class = jax.vmap(lambda own, number: shared_out(jax.random.fold_in(own_keys[5], 2), own, number, QUERIES // N_FAC, CLASSES, 1, QUERY_CAP, 1))(query_class_keys, query_class_turns).reshape((QUERIES, 1))
    basis_a = bell_draw(seeds[6], (CLASSES, D, D), D ** -0.5, 0.078125, ((1, 4), (2, 4)))
    basis_g = bell_draw(seeds[7], (CLASSES, FH, FH), FH ** -0.5, 0.0546875, ((1, 4), (2, 4)))
    eigen_a = jnp.clip(jnp.exp(math.log(8.0) - 2.7725887 * jax.random.uniform(seeds[8], (CLASSES, D), jnp.float32) ** block_scale(seeds[8], (CLASSES, D), ((1, 4),), -0.2, 0.2)), 0.5, 8.0)
    eigen_g = jnp.clip(jnp.exp(math.log(8.0) - 2.7725887 * jax.random.uniform(seeds[9], (CLASSES, FH), jnp.float32) ** block_scale(seeds[9], (CLASSES, FH), ((1, 4),), -0.2, 0.2)), 0.5, 8.0)
    return {"activations": activations, "gradients": gradients, "tok_class": tok_class, "query_inputs": query_inputs, "query_gradients": query_gradients, "query_class": query_class, "basis_a": basis_a, "basis_g": basis_g, "eigen_a": eigen_a, "eigen_g": eigen_g}


DAMPING = 0.25

def reference(activations, gradients, tok_class, query_inputs, query_gradients, query_class, basis_a, basis_g, eigen_a, eigen_g):
    token_ids = tok_class[:, 0]
    query_ids = query_class[:, 0]
    factor = 1.0 / math.sqrt(FH * D)
    total = jnp.zeros((QUERIES, TOKENS), jnp.float32)
    for klass in range(CLASSES):
        token_g = jnp.dot(gradients, basis_g[klass], preferred_element_type=jnp.float32)
        token_a = jnp.dot(activations, basis_a[klass], preferred_element_type=jnp.float32)
        damped_g = token_g / (eigen_g[klass] + DAMPING)[None, :]
        damped_a = token_a / (eigen_a[klass] + DAMPING)[None, :]
        query_g = jnp.dot(query_gradients, basis_g[klass], preferred_element_type=jnp.float32)
        query_a = jnp.dot(query_inputs, basis_a[klass], preferred_element_type=jnp.float32)
        side_g = jnp.dot(query_g, damped_g.T, precision=lax.Precision.HIGHEST)
        side_a = jnp.dot(query_a, damped_a.T, precision=lax.Precision.HIGHEST)
        paired = (query_ids[:, None] == klass) & (token_ids[None, :] == klass)
        total = total + jnp.where(paired, side_g * side_a * factor, jnp.zeros_like(side_g))
    return total
```

```python
import math

import jax
import jax.numpy as jnp
from jax import lax
from jax.sharding import PartitionSpec as P

D = 5120
FH = 13824
DAMPING = 0.25
CHUNKS = 8
LARGEST = 32767.0


def quantise(x):
    top = jnp.max(jnp.abs(x), axis=1, keepdims=True)
    code = jnp.ceil(8.0 * jnp.log2(jnp.maximum(top, 1e-30)))
    scaled = jnp.round(x * (LARGEST * jnp.exp2(code * -0.125)))
    return jnp.clip(scaled, -LARGEST, LARGEST).astype(jnp.int16), code.astype(jnp.int16)


def pack(x_g, x_a):
    q_g, e_g = quantise(x_g)
    q_a, e_a = quantise(x_a)
    lane = lax.broadcasted_iota(jnp.int32, (x_g.shape[0], 128), 1)
    tail = jnp.where(lane < 64, e_g, e_a)
    return jnp.concatenate([q_g, q_a, tail], axis=1)


def unpack(packet, width_g, width_a):
    both = width_g + width_a
    s_g = jnp.exp2(packet[:, both : both + 1].astype(jnp.float32) * 0.125) * (1.0 / LARGEST)
    s_a = jnp.exp2(packet[:, both + 64 : both + 65].astype(jnp.float32) * 0.125) * (1.0 / LARGEST)
    return (
        packet[:, :width_g].astype(jnp.float32) * s_g,
        packet[:, width_g:both].astype(jnp.float32) * s_a,
    )


def body(
    activations,
    gradients,
    tok_class,
    query_inputs,
    query_gradients,
    query_class,
    basis_a,
    basis_g,
    eigen_a,
    eigen_g,
):
    classes, width_g, width_a = basis_g.shape[0], basis_g.shape[2], basis_a.shape[2]
    deep_g, deep_a = basis_g.shape[1], basis_a.shape[1]
    tok_count, fac_count, sub_count = (lax.axis_size(a) for a in ("tok", "fac", "sub"))
    z, x, core = (lax.axis_index(a) for a in ("tok", "fac", "sub"))
    queries = query_inputs.shape[0]
    block = queries // fac_count
    rows = block // CHUNKS
    low, high = 3 * CHUNKS // 8, 5 * CHUNKS // 8
    tok_rows = activations.shape[0]
    half_rows = tok_rows // sub_count
    slot_cap = 5 * half_rows // 8
    share = half_rows // fac_count
    token_ids = tok_class[:, 0]
    query_ids = query_class[:, 0]

    at = (core * fac_count + x) * share
    own_g = lax.dynamic_slice_in_dim(gradients, at, share)
    own_a = lax.dynamic_slice_in_dim(activations, at, share)
    blocks = []
    for step in range(tok_count):
        to = lax.rem(z + step, tok_count)
        part = jnp.concatenate(
            [
                lax.dynamic_slice_in_dim(own_g, to * deep_g, deep_g, 1),
                lax.dynamic_slice_in_dim(own_a, to * deep_a, deep_a, 1),
            ],
            axis=1,
        )
        if step:
            part = lax.ppermute(part, "tok", [(i, (i + step) % tok_count) for i in range(tok_count)])
        blocks.append(part)
    mine = jnp.concatenate(blocks, axis=0)
    plane = [mine]
    for step in range(1, fac_count):
        plane.append(lax.ppermute(mine, "fac", [(i, (i + step) % fac_count) for i in range(fac_count)]))
    plane = jnp.concatenate(plane, axis=0)
    other = [plane]
    for step in range(1, sub_count):
        other.append(lax.ppermute(plane, "sub", [(i, (i + step) % sub_count) for i in range(sub_count)]))
    raw = jnp.concatenate(other, axis=0)

    halves = tok_count * sub_count
    ids = token_ids.reshape(halves, half_rows)
    earlier = jnp.arange(half_rows)[None, :] < jnp.arange(half_rows)[:, None]
    rank = jnp.sum(
        ((ids[:, None, :] == ids[:, :, None]) & earlier).astype(jnp.int32), axis=2
    )
    slot = ids * (halves * slot_cap) + jnp.arange(halves)[:, None] * slot_cap + rank
    from_s = lax.rem(core - jnp.arange(sub_count) + sub_count, sub_count)[:, None, None, None]
    from_f = lax.rem(x - jnp.arange(fac_count) + fac_count, fac_count)[None, :, None, None]
    from_z = lax.rem(z - jnp.arange(tok_count) + tok_count, tok_count)[None, None, :, None]
    slot = slot.reshape(tok_count, sub_count, fac_count, share)
    pick_s = from_s[:, 0, 0, 0]
    slot = jnp.take(jnp.take(jnp.take(slot, from_z[0, 0, :, 0], 0), pick_s, 1), from_f[0, :, 0, 0], 2)
    slot = slot.transpose(1, 2, 0, 3).reshape(-1)
    table = (jnp.arange(classes * halves * slot_cap)[:, None] == slot[None, :]).astype(jnp.bfloat16)
    packed = jnp.dot(table, raw, preferred_element_type=jnp.float32).astype(jnp.bfloat16)
    packed = packed.reshape(classes, halves * slot_cap, deep_g + deep_a)

    qids = query_ids.reshape(fac_count, block)
    key = qids * block + jnp.arange(block)
    place = jnp.sum((key[:, None, :] < key[:, :, None]).astype(jnp.int32), axis=2)
    first = jnp.sum((qids == 0).astype(jnp.int32), axis=1)
    order = (jnp.arange(block)[None, :, None] == place[:, None, :]).astype(jnp.bfloat16)
    order = order.reshape(fac_count, CHUNKS, rows, block)

    def ordered(features):
        return (
            jnp.einsum(
                "fjpb,fbr->jfpr",
                order,
                features.reshape(fac_count, block, features.shape[1]),
                preferred_element_type=jnp.float32,
            )
            .astype(jnp.bfloat16)
            .reshape(queries, features.shape[1])
        )

    unit = fac_count * rows
    spot = (jnp.arange(low, high)[:, None, None] * rows + jnp.arange(rows)) < first[None, :, None]
    spot = spot.reshape((high - low) * unit, 1)

    def partial(features, basis):
        sorted_rows = ordered(features)
        zero = jnp.dot(sorted_rows[: high * unit], basis[0], preferred_element_type=jnp.float32)
        one = jnp.dot(sorted_rows[low * unit :], basis[1], preferred_element_type=jnp.float32)
        middle = jnp.where(spot, zero[low * unit :], one[: (high - low) * unit])
        out = jnp.concatenate([zero[: low * unit], middle, one[(high - low) * unit :]], axis=0)
        return out.reshape(CHUNKS, unit, basis.shape[2])

    part_a = partial(query_inputs, basis_a)
    part_g = partial(query_gradients, basis_g)

    weight_g = 1.0 / (eigen_g + DAMPING)
    weight_a = 1.0 / (eigen_a + DAMPING)
    tok_g = (
        jnp.einsum("csr,crk->csk", packed[:, :, :deep_g], basis_g, preferred_element_type=jnp.float32)
        * weight_g[:, None, :]
    )
    tok_a = (
        jnp.einsum("csr,crk->csk", packed[:, :, deep_g:], basis_a, preferred_element_type=jnp.float32)
        * weight_a[:, None, :]
    )

    up = [(i, i + 1) for i in range(tok_count - 1)]
    down = [(i + 1, i) for i in range(tok_count - 1)]
    from_below, from_above = [], []
    for step in range(CHUNKS + tok_count - 2):
        for got, pairs, behind in (
            (from_below, up, z),
            (from_above, down, tok_count - 1 - z),
        ):
            chunk = jnp.clip(step - behind, 0, CHUNKS - 1)
            x_g = lax.dynamic_index_in_dim(part_g, chunk, 0, keepdims=False)
            x_a = lax.dynamic_index_in_dim(part_a, chunk, 0, keepdims=False)
            if step:
                r_g, r_a = unpack(got[-1], width_g, width_a)
                x_g, x_a = x_g + r_g, x_a + r_a
            got.append(lax.ppermute(pack(x_g, x_a), "tok", pairs))

    sides = {0: [], 1: []}
    for chunk in range(CHUNKS):
        below = jnp.zeros_like(from_below[0])
        above = jnp.zeros_like(from_above[0])
        for behind in range(1, tok_count):
            below = jnp.where(z == behind, from_below[chunk + behind - 1], below)
            above = jnp.where(tok_count - 1 - z == behind, from_above[chunk + behind - 1], above)
        b_g, b_a = unpack(below, width_g, width_a)
        a_g, a_a = unpack(above, width_g, width_a)
        full_g = part_g[chunk] + b_g + a_g
        full_a = part_a[chunk] + b_a + a_a
        for klass in range(classes):
            if (chunk < high, chunk >= low)[klass]:
                s_g = lax.dot_general(
                    full_g, tok_g[klass], (((1,), (1,)), ((), ())), precision=lax.Precision.HIGH,
                    preferred_element_type=jnp.float32,
                )
                s_a = lax.dot_general(
                    full_a, tok_a[klass], (((1,), (1,)), ((), ())), precision=lax.Precision.HIGH,
                    preferred_element_type=jnp.float32,
                )
                sides[klass].append(jnp.stack([s_g, s_a]).reshape(2, fac_count, rows, halves, slot_cap))
    pieces = jnp.stack([jnp.concatenate(sides[k], axis=2) for k in range(classes)])
    pieces = pieces.transpose(4, 2, 0, 1, 3, 5).reshape(
        tok_count, sub_count, fac_count, classes, 2, high * rows, slot_cap
    )
    pieces = pieces.transpose(0, 2, 1, 3, 4, 5, 6).reshape(
        tok_count * fac_count * sub_count, classes, 2, high * rows, slot_cap
    )
    side = lax.psum_scatter(pieces, ("tok", "fac", "sub"), scatter_dimension=0, tiled=True)[0]
    scores = side[:, 0] * side[:, 1] * (1.0 / math.sqrt(FH * D))

    own_place = lax.dynamic_index_in_dim(place, x, 0, keepdims=False)
    own_first = lax.dynamic_index_in_dim(first, x, 0, keepdims=False)
    at_row = jnp.arange(high * rows)
    out = jnp.zeros((block, half_rows), jnp.float32)
    half = z * sub_count + core
    own_rank = lax.dynamic_index_in_dim(rank, half, 0, keepdims=False)
    own_ids = lax.dynamic_index_in_dim(ids, half, 0, keepdims=False)
    for klass in range(classes):
        row = at_row + (0, low * rows)[klass]
        of_class = (row < own_first) if klass == 0 else (row >= own_first)
        to_query = ((own_place[:, None] == row[None, :]) & of_class[None, :]).astype(jnp.float32)
        to_token = (
            (own_rank[None, :] == jnp.arange(slot_cap)[:, None]) & (own_ids[None, :] == klass)
        ).astype(jnp.float32)
        by_query = jnp.dot(to_query, scores[klass], precision=lax.Precision.HIGHEST)
        out = out + jnp.dot(by_query, to_token, precision=lax.Precision.HIGHEST)
    return out


def solution(mesh):
    placed = (
        P(("grp", "tok"), None),
        P(("grp", "tok"), None),
        P("grp", None),
        P("grp", "tok"),
        P("grp", "tok"),
        P("grp", None),
        P(None, "tok", ("fac", "sub")),
        P(None, "tok", ("fac", "sub")),
        P(None, ("fac", "sub")),
        P(None, ("fac", "sub")),
    )
    return jax.shard_map(
        body, mesh=mesh, in_specs=placed, out_specs=P("fac", ("grp", "tok", "sub")), check_vma=False
    )
```

```python
import functools
import math

import jax
import jax.numpy as jnp
from jax import lax
from jax.experimental import pallas as pl
from jax.experimental.pallas import tpu as pltpu
from jax.sharding import PartitionSpec as P

D = 5120
FH = 13824
DAMPING = 0.25
CHUNKS = 8
LARGEST = 32760.0
LANES = 128
TILE = 512
MIB = 1 << 20
F32 = jnp.float32
BF16 = jnp.bfloat16
FINE = 8.0 / math.log(2.0)
LAST_GROUP = 2


def up_to(n, m):
    return -(-n // m) * m


def params(mib):
    return pltpu.CompilerParams(vmem_limit_bytes=mib * MIB)


def query_kernel(fac, rows, place_ref, spot_ref, feat_ref, basis_ref, out_ref, sorted_ref):
    block = place_ref.shape[1]
    unit = fac * rows
    low, high = 3 * CHUNKS // 8 * unit, 5 * CHUNKS // 8 * unit

    @pl.when(pl.program_id(0) == 0)
    def _():
        for f in range(fac):
            order = lax.broadcasted_iota(jnp.int32, (block, block), 0) == place_ref[f : f + 1, :]
            moved = jnp.dot(
                order.astype(F32).astype(BF16),
                feat_ref[f * block : (f + 1) * block, :],
                preferred_element_type=F32,
            ).astype(BF16)
            for j in range(CHUNKS):
                sorted_ref[j * unit + f * rows : j * unit + (f + 1) * rows, :] = moved[
                    j * rows : (j + 1) * rows, :
                ]

    zero = jnp.dot(sorted_ref[:high, :], basis_ref[0], preferred_element_type=F32)
    one = jnp.dot(sorted_ref[low:, :], basis_ref[1], preferred_element_type=F32)
    out_ref[:low, :] = zero[:low]
    out_ref[low:high, :] = jnp.where(spot_ref[...] > 0, zero[low:], one[: high - low])
    out_ref[high:, :] = one[high - low :]


def query_coords(place, spot, features, basis, fac, rows):
    queries, deep = features.shape
    width = basis.shape[2]
    tile = min(TILE, width)
    return pl.pallas_call(
        functools.partial(query_kernel, fac, rows),
        grid=(pl.cdiv(width, tile),),
        in_specs=[
            pl.BlockSpec(place.shape, lambda i: (0, 0)),
            pl.BlockSpec(spot.shape, lambda i: (0, 0)),
            pl.BlockSpec((queries, deep), lambda i: (0, 0)),
            pl.BlockSpec((2, deep, tile), lambda i: (0, 0, i)),
        ],
        out_specs=pl.BlockSpec((queries, tile), lambda i: (0, i)),
        out_shape=jax.ShapeDtypeStruct((queries, width), F32),
        scratch_shapes=[pltpu.VMEM((queries, deep), BF16)],
        compiler_params=params(48),
        name="query_coords",
    )(place, spot, features, basis)


def token_kernel(start, deep, slots, slot_ref, *refs):
    count = len(refs) - 6
    raws, (weight_ref, basis_ref, high_ref, low_ref, raw_ref, packed_ref) = refs[:count], refs[count:]

    @pl.when(pl.program_id(0) == 0)
    def _():
        size = raws[0].shape[0]
        for i, ref in enumerate(raws):
            raw_ref[i * size : (i + 1) * size, :] = ref[:, start : start + deep]
        tokens = raw_ref.shape[0]
        for klass in range(2):
            table = (
                lax.broadcasted_iota(jnp.int32, (slots, tokens), 0) + klass * slots == slot_ref[...]
            )
            packed_ref[klass] = jnp.dot(
                table.astype(F32).astype(BF16), raw_ref[...], preferred_element_type=F32
            ).astype(BF16)

    for klass in range(2):
        coords = (
            jnp.dot(packed_ref[klass], basis_ref[klass], preferred_element_type=F32)
            * weight_ref[klass : klass + 1, :]
        )
        high = coords.astype(BF16)
        high_ref[klass] = high
        low_ref[klass] = (coords - high.astype(F32)).astype(BF16)


def token_coords(slot, raws, weight, basis, start, slots):
    deep, width = basis.shape[1:]
    tokens = slot.shape[1]
    tile = min(TILE, width)
    out = jax.ShapeDtypeStruct((2, slots, width), BF16)
    return pl.pallas_call(
        functools.partial(token_kernel, start, deep, slots),
        grid=(pl.cdiv(width, tile),),
        in_specs=[pl.BlockSpec(slot.shape, lambda i: (0, 0))]
        + [pl.BlockSpec(raw.shape, lambda i: (0, 0)) for raw in raws]
        + [
            pl.BlockSpec((2, tile), lambda i: (0, i)),
            pl.BlockSpec((2, deep, tile), lambda i: (0, 0, i)),
        ],
        out_specs=[pl.BlockSpec((2, slots, tile), lambda i: (0, 0, i))] * 2,
        out_shape=[out, out],
        scratch_shapes=[pltpu.VMEM((tokens, deep), BF16), pltpu.VMEM((2, slots, deep), BF16)],
        compiler_params=params(56),
        name="token_coords",
    )(slot, *raws, weight, basis)


def scaled(x):
    top = jnp.max(jnp.abs(x), axis=1, keepdims=True)
    code = jnp.ceil(jnp.log(jnp.maximum(top, 1e-30)) * FINE)
    return lax.round(x * (LARGEST * jnp.exp(code * (-1.0 / FINE))), lax.RoundingMethod.TO_NEAREST_EVEN), code


def narrow(x):
    return x.astype(jnp.int32).astype(jnp.int16)


def wide(x):
    return x.astype(jnp.int32).astype(F32)


def read_packet(ref, width_g, width_a):
    start = up_to(width_g, LANES)
    tail = start + up_to(width_a, LANES)
    code = wide(ref[:, tail : tail + LANES])
    step = jnp.exp(code * (1.0 / FINE)) * (1.0 / LARGEST)
    return (
        wide(ref[:, :width_g]) * step[:, 0:1],
        wide(ref[:, start : start + width_a]) * step[:, LANES - 1 : LANES],
    )


def stage_kernel(first, chunk_ref, part_g_ref, part_a_ref, *refs):
    del chunk_ref
    out_ref = refs[-1]
    width_g, width_a = part_g_ref.shape[1], part_a_ref.shape[1]
    start = up_to(width_g, LANES)
    tail = start + up_to(width_a, LANES)
    x_g, x_a = part_g_ref[...], part_a_ref[...]
    if not first:
        r_g, r_a = read_packet(refs[0], width_g, width_a)
        x_g, x_a = x_g + r_g, x_a + r_a
    q_g, code_g = scaled(x_g)
    q_a, code_a = scaled(x_a)
    if start != width_g or tail != start + width_a:
        out_ref[...] = jnp.zeros_like(out_ref)
    out_ref[:, :width_g] = narrow(q_g)
    out_ref[:, start : start + width_a] = narrow(q_a)
    lane = lax.broadcasted_iota(jnp.int32, (x_g.shape[0], LANES), 1)
    out_ref[:, tail:] = narrow(jnp.where(lane < LANES // 2, code_g, code_a))


def stage(chunk, part_g, part_a, received):
    queries, width_g = part_g.shape
    width_a = part_a.shape[1]
    unit = queries // CHUNKS
    size = unit // 2
    packet = up_to(width_g, LANES) + up_to(width_a, LANES) + LANES
    per = unit // size
    got = [] if received is None else [received]
    return pl.pallas_call(
        functools.partial(stage_kernel, received is None),
        grid_spec=pltpu.PrefetchScalarGridSpec(
            num_scalar_prefetch=1,
            grid=(per,),
            in_specs=[
                pl.BlockSpec((size, width_g), lambda i, c: (c[0] * per + i, 0)),
                pl.BlockSpec((size, width_a), lambda i, c: (c[0] * per + i, 0)),
            ]
            + [pl.BlockSpec((size, packet), lambda i, c: (i, 0)) for _ in got],
            out_specs=pl.BlockSpec((size, packet), lambda i, c: (i, 0)),
        ),
        out_shape=jax.ShapeDtypeStruct((unit, packet), jnp.int16),
        compiler_params=params(24),
        name="running_sum",
    )(chunk, part_g, part_a, *got)


def side_kernel(hops, unit, z_ref, part_g_ref, part_a_ref, *refs):
    below, above = refs[:hops], refs[hops : 2 * hops]
    gh_ref, gl_ref, ah_ref, al_ref, out_ref, x_g, x_a, below_ref, above_ref, sems = refs[2 * hops :]
    width_g, width_a = part_g_ref.shape[1], part_a_ref.shape[1]

    @pl.when((pl.program_id(0) == 0) & (pl.program_id(1) == 0))
    def _():
        for k in range(hops):
            cut = (z_ref[0] <= 1) if k == 0 else (z_ref[0] == k + 1)

            @pl.when(cut)
            def _():
                pltpu.make_async_copy(below[k], below_ref, sems.at[0]).start()

            cut = (z_ref[1] <= 1) if k == 0 else (z_ref[1] == k + 1)

            @pl.when(cut)
            def _():
                pltpu.make_async_copy(above[k], above_ref, sems.at[1]).start()

        pltpu.make_async_copy(below[0], below_ref, sems.at[0]).wait()
        pltpu.make_async_copy(above[0], above_ref, sems.at[1]).wait()
        b_g, b_a = read_packet(below_ref, width_g, width_a)
        a_g, a_a = read_packet(above_ref, width_g, width_a)
        for ref, full in ((x_g, part_g_ref[...] + b_g + a_g), (x_a, part_a_ref[...] + b_a + a_a)):
            high = full.astype(BF16)
            ref[:unit, :] = high
            ref[unit:, :] = (full - high.astype(F32)).astype(BF16)

    for side, (x, high, low) in enumerate(((x_g, gh_ref, gl_ref), (x_a, ah_ref, al_ref))):
        dims = (((1,), (1,)), ((), ()))
        both = lax.dot_general(high[0], x[...], dims, preferred_element_type=F32)
        both += lax.dot_general(low[0], x[...], dims, preferred_element_type=F32)
        out_ref[0, side] = both[:, :unit] + both[:, unit:]


def sides(where_z, chunk, klasses, part_g, part_a, below, above, tok_g, tok_a):
    queries, width_g = part_g.shape
    width_a = part_a.shape[1]
    unit = queries // CHUNKS
    slots = tok_g[0].shape[1]
    pieces = 2
    size = slots // pieces
    base = klasses[0]
    anywhere = pl.BlockSpec(memory_space=pl.ANY)
    return pl.pallas_call(
        functools.partial(side_kernel, len(below), unit),
        grid_spec=pltpu.PrefetchScalarGridSpec(
            num_scalar_prefetch=1,
            grid=(len(klasses), pieces),
            in_specs=[
                pl.BlockSpec((unit, width_g), lambda k, i, z: (chunk, 0)),
                pl.BlockSpec((unit, width_a), lambda k, i, z: (chunk, 0)),
            ]
            + [anywhere] * (2 * len(below))
            + [pl.BlockSpec((1, size, width_g), lambda k, i, z: (base + k, i, 0))] * 2
            + [pl.BlockSpec((1, size, width_a), lambda k, i, z: (base + k, i, 0))] * 2,
            out_specs=pl.BlockSpec((1, 2, size, unit), lambda k, i, z: (k, 0, i, 0)),
            scratch_shapes=[
                pltpu.VMEM((2 * unit, width_g), BF16),
                pltpu.VMEM((2 * unit, width_a), BF16),
                pltpu.VMEM(below[0].shape, jnp.int16),
                pltpu.VMEM(below[0].shape, jnp.int16),
                pltpu.SemaphoreType.DMA((2,)),
            ],
        ),
        out_shape=jax.ShapeDtypeStruct((len(klasses), 2, slots, unit), F32),
        compiler_params=params(40),
        name="side_sums",
    )(where_z, part_g, part_a, *below, *above, *tok_g, *tok_a)


def body(
    activations,
    gradients,
    tok_class,
    query_inputs,
    query_gradients,
    query_class,
    basis_a,
    basis_g,
    eigen_a,
    eigen_g,
):
    classes = basis_g.shape[0]
    deep_g, deep_a = basis_g.shape[1], basis_a.shape[1]
    tok_count, fac_count, sub_count = (lax.axis_size(a) for a in ("tok", "fac", "sub"))
    z, x, core = (lax.axis_index(a) for a in ("tok", "fac", "sub"))
    queries = query_inputs.shape[0]
    block = queries // fac_count
    rows = block // CHUNKS
    unit = fac_count * rows
    low, high = 3 * CHUNKS // 8, 5 * CHUNKS // 8
    tok_rows = activations.shape[0]
    half_rows = tok_rows // sub_count
    slot_cap = 5 * half_rows // 8
    share = half_rows // fac_count
    halves = tok_count * sub_count
    slots = halves * slot_cap
    token_ids = tok_class[:, 0]
    query_ids = query_class[:, 0]

    at = (core * fac_count + x) * share
    room = up_to(deep_g, LANES)
    blocks = []
    for step in range(tok_count):
        to = lax.rem(z + step, tok_count)
        part = jnp.concatenate(
            [
                lax.dynamic_slice(gradients, (at, to * deep_g), (share, deep_g)),
                jnp.zeros((share, room - deep_g), BF16),
                lax.dynamic_slice(activations, (at, to * deep_a), (share, deep_a)),
            ],
            axis=1,
        )
        if step:
            part = lax.ppermute(part, "tok", [(i, (i + step) % tok_count) for i in range(tok_count)])
        blocks.append(part)
    mine = jnp.concatenate(blocks, axis=0)
    raws = [mine]
    for step in range(1, fac_count):
        raws.append(lax.ppermute(mine, "fac", [(i, (i + step) % fac_count) for i in range(fac_count)]))
    for step in range(1, sub_count):
        turn = [(i, (i + step) % sub_count) for i in range(sub_count)]
        raws += [lax.ppermute(raw, "sub", turn) for raw in raws[:fac_count]]

    qids = query_ids.reshape(fac_count, block)
    key = qids * block + jnp.arange(block)
    place = jnp.sum((key[:, None, :] < key[:, :, None]).astype(jnp.int32), axis=2)
    first = jnp.sum((qids == 0).astype(jnp.int32), axis=1)
    spot = (jnp.arange(low, high)[:, None, None] * rows + jnp.arange(rows)) < first[None, :, None]
    spot = spot.reshape((high - low) * unit, 1).astype(jnp.int32)
    part_g = query_coords(place, spot, query_gradients, basis_g, fac_count, rows)
    part_a = query_coords(place, spot, query_inputs, basis_a, fac_count, rows)

    ids = token_ids.reshape(halves, half_rows)
    earlier = jnp.arange(half_rows)[None, :] < jnp.arange(half_rows)[:, None]
    rank = jnp.sum(((ids[:, None, :] == ids[:, :, None]) & earlier).astype(jnp.int32), axis=2)
    slot = ids * slots + jnp.arange(halves)[:, None] * slot_cap + rank
    slot = slot.reshape(tok_count, sub_count, fac_count, share)
    for axis, (at_axis, count) in enumerate(((z, tok_count), (core, sub_count), (x, fac_count))):
        slot = jnp.take(slot, lax.rem(at_axis - jnp.arange(count) + count, count), axis)
    slot = slot.transpose(1, 2, 0, 3).reshape(1, -1)
    tok_g = token_coords(slot, raws, 1.0 / (eigen_g + DAMPING), basis_g, 0, slots)
    tok_a = token_coords(slot, raws, 1.0 / (eigen_a + DAMPING), basis_a, room, slots)

    up = [(i, i + 1) for i in range(tok_count - 1)]
    down = [(i + 1, i) for i in range(tok_count - 1)]
    from_below, from_above = [], []
    for step in range(CHUNKS + tok_count - 2):
        for got, pairs, behind in ((from_below, up, z), (from_above, down, tok_count - 1 - z)):
            chunk = jnp.clip(step - behind, 0, CHUNKS - 1).astype(jnp.int32).reshape(1)
            got.append(lax.ppermute(stage(chunk, part_g, part_a, got[-1] if step else None), "tok", pairs))

    where_z = jnp.stack([z, tok_count - 1 - z]).astype(jnp.int32)
    columns = [[], []]
    for chunk in range(CHUNKS):
        klasses = [k for k in range(classes) if (chunk < high, chunk >= low)[k]]
        out = sides(
            where_z, chunk, klasses, part_g, part_a,
            from_below[chunk : chunk + tok_count - 1], from_above[chunk : chunk + tok_count - 1],
            tok_g, tok_a,
        )
        for i, klass in enumerate(klasses):
            columns[klass].append(
                (chunk, out[i].reshape(2, tok_count, sub_count, slot_cap, fac_count, rows))
            )

    sums = [[], []]
    for group in (range(CHUNKS - LAST_GROUP), range(CHUNKS - LAST_GROUP, CHUNKS)):
        pieces = []
        for klass in range(classes):
            pieces += [(klass, part) for chunk, part in columns[klass] if chunk in group]
        joined = jnp.stack([part for _, part in pieces])
        joined = joined.transpose(2, 5, 3, 1, 4, 0, 6)
        joined = joined.reshape(tok_count * fac_count * sub_count, 2, slot_cap, len(pieces) * rows)
        mine = lax.psum_scatter(joined, ("tok", "fac", "sub"), scatter_dimension=0, tiled=True)[0]
        for i, (klass, _) in enumerate(pieces):
            sums[klass].append(mine[:, :, i * rows : (i + 1) * rows])

    own_place = lax.dynamic_index_in_dim(place, x, 0, keepdims=False)
    own_first = lax.dynamic_index_in_dim(first, x, 0, keepdims=False)
    out = jnp.zeros((block, half_rows), F32)
    half = z * sub_count + core
    own_rank = lax.dynamic_index_in_dim(rank, half, 0, keepdims=False)
    own_ids = lax.dynamic_index_in_dim(ids, half, 0, keepdims=False)
    for klass in range(classes):
        side = jnp.concatenate(sums[klass], axis=2)
        scores = side[0] * side[1] * (1.0 / math.sqrt(FH * D))
        row = jnp.arange(high * rows) + (0, low * rows)[klass]
        of_class = (row < own_first) if klass == 0 else (row >= own_first)
        to_query = ((own_place[:, None] == row[None, :]) & of_class[None, :]).astype(F32)
        to_token = (
            (own_rank[None, :] == jnp.arange(slot_cap)[:, None]) & (own_ids[None, :] == klass)
        ).astype(F32)
        by_query = jnp.einsum("qr,sr->qs", to_query, scores, precision=lax.Precision.HIGHEST)
        out = out + jnp.dot(by_query, to_token, precision=lax.Precision.HIGHEST)
    return out


def solution(mesh):
    placed = (
        P(("grp", "tok"), None),
        P(("grp", "tok"), None),
        P("grp", None),
        P("grp", "tok"),
        P("grp", "tok"),
        P("grp", None),
        P(None, "tok", ("fac", "sub")),
        P(None, "tok", ("fac", "sub")),
        P(None, ("fac", "sub")),
        P(None, ("fac", "sub")),
    )
    return jax.shard_map(
        body, mesh=mesh, in_specs=placed, out_specs=P("fac", ("grp", "tok", "sub")), check_vma=False
    )
```

```python
import functools
import math

import jax
import jax.numpy as jnp
from jax import lax
from jax.experimental import pallas as pl
from jax.experimental.pallas import tpu as pltpu
from jax.sharding import PartitionSpec as P

D = 5120
FH = 13824
DAMPING = 0.25
CHUNKS = 8
LOW, HIGH = 3 * CHUNKS // 8, 5 * CHUNKS // 8
LARGEST = 32760.0
LANES = 128
TILE = 512
SEGMENT = 2 * TILE
MIB = 1 << 20
F32 = jnp.float32
BF16 = jnp.bfloat16
I32 = jnp.int32
FINE = 8.0 / math.log(2.0)
IN_HBM = pl.BlockSpec(memory_space=pltpu.HBM)
ANYWHERE = pl.BlockSpec(memory_space=pl.ANY)
SCALARS = pl.BlockSpec(memory_space=pltpu.SMEM)
WHOLE = pl.BlockSpec(memory_space=pltpu.VMEM)


def up_to(n, m):
    return -(-n // m) * m


def params(mib):
    return pltpu.CompilerParams(vmem_limit_bytes=mib * MIB)


def turn(count, step):
    return [(i, (i + step) % count) for i in range(count)]


def query_kernel(fac, rows, first, place_ref, feat_ref, basis_ref, *refs):
    out_ref, sorted_ref = refs[-2:]
    block = place_ref.shape[1]
    unit = fac * rows
    chunks = HIGH

    @pl.when(pl.program_id(0) == 0)
    def _():
        for f in range(fac):
            spots = lax.broadcasted_iota(I32, (chunks * rows, block), 0) + first * rows
            order = (spots == place_ref[f : f + 1, :]).astype(F32).astype(BF16)
            moved = jnp.dot(
                order, feat_ref[f * block : (f + 1) * block, :], preferred_element_type=F32
            ).astype(BF16)
            for j in range(chunks):
                sorted_ref[j * unit + f * rows : j * unit + (f + 1) * rows, :] = moved[
                    j * rows : (j + 1) * rows, :
                ]

    out_ref[...] = jnp.dot(sorted_ref[...], basis_ref[0], preferred_element_type=F32)


def query_coords(klass, place, features, basis, fac, rows, after=()):
    queries, deep = features.shape
    width = basis.shape[2]
    tile = min(TILE, width)
    count = HIGH * fac * rows
    return pl.pallas_call(
        functools.partial(query_kernel, fac, rows, (0, LOW)[klass]),
        grid=(pl.cdiv(width, tile),),
        in_specs=[
            pl.BlockSpec(place.shape, lambda i: (0, 0)),
            pl.BlockSpec((queries, deep), lambda i: (0, 0)),
            pl.BlockSpec((1, deep, tile), lambda i: (klass, 0, i)),
        ]
        + [ANYWHERE] * len(after),
        out_specs=pl.BlockSpec((count, tile), lambda i: (0, i)),
        out_shape=jax.ShapeDtypeStruct((count, width), F32),
        scratch_shapes=[pltpu.VMEM((count, deep), BF16)],
        compiler_params=params(40),
        name="query_coords",
    )(place, features, basis, *after)


def join_kernel(count, *refs):
    sources, out_ref, sems = refs[:count], refs[-2], refs[-1]
    size = sources[0].shape[0]
    copies = [
        pltpu.make_async_copy(ref, out_ref.at[pl.ds(i * size, size), :], sems.at[i])
        for i, ref in enumerate(sources)
    ]
    for copy in copies:
        copy.start()
    for copy in copies:
        copy.wait()


def join(blocks, after):
    size, width = blocks[0].shape
    return pl.pallas_call(
        functools.partial(join_kernel, len(blocks)),
        in_specs=[ANYWHERE] * (len(blocks) + len(after)),
        out_specs=IN_HBM,
        out_shape=jax.ShapeDtypeStruct((size * len(blocks), width), BF16),
        scratch_shapes=[pltpu.SemaphoreType.DMA((len(blocks),))],
        name="join_tokens",
    )(*blocks, *after)


def pack_kernel(counts, slots, at_ref, slot_ref, *refs):
    tok, sub, fac = counts
    raws = refs[: sub * fac]
    out_ref, raw_ref, sems = refs[-3:]
    size = raws[0].shape[0]
    copies = [
        pltpu.make_async_copy(ref, raw_ref.at[pl.ds(i * size, size), :], sems.at[i])
        for i, ref in enumerate(raws)
    ]
    for copy in copies:
        copy.start()
    here = []
    for s in range(sub):
        for f in range(fac):
            for k in range(tok):
                row = lax.rem(at_ref[0] + tok - k, tok) * sub + lax.rem(at_ref[1] + sub - s, sub)
                row = row * fac + lax.rem(at_ref[2] + fac - f, fac)
                here.append(slot_ref[pl.ds(row, 1), :])
    here = jnp.concatenate(here, axis=1)
    for copy in copies:
        copy.wait()
    for klass in range(2):
        table = lax.broadcasted_iota(I32, (slots, here.shape[1]), 0) + klass * slots == here
        out_ref[klass] = jnp.dot(
            table.astype(F32).astype(BF16), raw_ref[...], preferred_element_type=F32
        ).astype(BF16)


def pack(counts, at, slot, raws, slots, after):
    size, width = raws[0].shape
    return pl.pallas_call(
        functools.partial(pack_kernel, counts, slots),
        in_specs=[SCALARS, WHOLE] + [ANYWHERE] * (len(raws) + len(after)),
        out_specs=WHOLE,
        out_shape=jax.ShapeDtypeStruct((2, slots, width), BF16),
        scratch_shapes=[
            pltpu.VMEM((size * len(raws), width), BF16),
            pltpu.SemaphoreType.DMA((len(raws),)),
        ],
        compiler_params=params(48),
        name="pack_tokens",
    )(at, slot, *raws, *after)


def token_kernel(start, packed_ref, weight_ref, basis_ref, *refs):
    high_ref, low_ref = refs[-2:]
    deep = basis_ref.shape[1]
    for klass in range(2):
        coords = (
            jnp.dot(packed_ref[klass, :, start : start + deep], basis_ref[klass], preferred_element_type=F32)
            * weight_ref[klass : klass + 1, :]
        )
        high = coords.astype(BF16)
        high_ref[klass] = high
        low_ref[klass] = (coords - high.astype(F32)).astype(BF16)


def token_coords(packed, weight, basis, start, column, segment, after):
    slots, stored = packed.shape[1:]
    deep, width = basis.shape[1:]
    here = min(segment, width - column)
    tile = min(TILE, width)
    base = column // tile
    out = jax.ShapeDtypeStruct((2, slots, here), BF16)
    return pl.pallas_call(
        functools.partial(token_kernel, start),
        grid=(pl.cdiv(here, tile),),
        in_specs=[
            pl.BlockSpec((2, slots, stored), lambda i: (0, 0, 0)),
            pl.BlockSpec((2, tile), lambda i: (0, base + i)),
            pl.BlockSpec((2, deep, tile), lambda i: (0, 0, base + i)),
        ]
        + [ANYWHERE] * len(after),
        out_specs=[pl.BlockSpec((2, slots, tile), lambda i: (0, 0, i))] * 2,
        out_shape=[out, out],
        compiler_params=params(56),
        name="token_coords",
    )(packed, weight, basis, *after)


def scaled(x):
    top = jnp.max(jnp.abs(x), axis=1, keepdims=True)
    code = jnp.ceil(jnp.log(jnp.maximum(top, 1e-30)) * FINE)
    factor = LARGEST * jnp.exp(code * (-1.0 / FINE))
    return lax.round(x * factor, lax.RoundingMethod.TO_NEAREST_EVEN), code


def narrow(x):
    return x.astype(I32).astype(jnp.int16)


def wide(x):
    return x.astype(I32).astype(F32)


def read_packet(ref, width_g, width_a):
    start = up_to(width_g, LANES)
    tail = start + up_to(width_a, LANES)
    step = jnp.exp(wide(ref[:, tail : tail + LANES]) * (1.0 / FINE)) * (1.0 / LARGEST)
    return (
        wide(ref[:, :width_g]) * step[:, 0:1],
        wide(ref[:, start : start + width_a]) * step[:, LANES - 1 : LANES],
    )


def stage_kernel(first, parts, after, chunk_ref, spot_ref, *refs):
    got = None if first else refs[0]
    refs = refs[0 if first else 1 :]
    use = [k for k in range(2) if parts[k]]
    part = {k: (refs[2 * i], refs[2 * i + 1]) for i, k in enumerate(use)}
    refs = refs[2 * len(use) + after :]
    out_ref, refs = refs[0], refs[1:]
    held = {k: (refs[2 * i], refs[2 * i + 1]) for i, k in enumerate(use)}
    got_ref, sems = refs[2 * len(use) :]
    unit = out_ref.shape[0]
    size = unit // 2
    chunk = chunk_ref[0]
    width_g, width_a = part[use[0]][0].shape[1], part[use[0]][1].shape[1]
    start = up_to(width_g, LANES)
    tail = start + up_to(width_a, LANES)

    def copies(k, h):
        row = pl.multiple_of((chunk - (0, LOW)[k]) * unit + h * size, size)
        return [
            pltpu.make_async_copy(
                part[k][side].at[pl.ds(row, size), :],
                held[k][side].at[pl.ds(h * size, size), :],
                sems.at[h, 2 * k + side],
            )
            for side in range(2)
        ]

    def each(h, act):
        if got is not None:
            act(
                pltpu.make_async_copy(
                    got.at[pl.ds(h * size, size), :], got_ref.at[pl.ds(h * size, size), :], sems.at[h, 4]
                )
            )
        for k in use:
            if len(use) == 1:
                for copy in copies(k, h):
                    act(copy)
            else:

                @pl.when((chunk < HIGH) if k == 0 else (chunk >= LOW))
                def _():
                    for copy in copies(k, h):
                        act(copy)

    for h in range(2):
        each(h, lambda copy: copy.start())
    for h in range(2):
        each(h, lambda copy: copy.wait())
        at = slice(h * size, (h + 1) * size)
        if len(use) == 1:
            x_g, x_a = (ref[at, :] for ref in held[use[0]])
        else:
            of_zero = spot_ref[at, :] > 0
            x_g, x_a = (jnp.where(of_zero, held[0][i][at, :], held[1][i][at, :]) for i in range(2))
        if got is not None:
            r_g, r_a = read_packet(got_ref.at[pl.ds(h * size, size), :], width_g, width_a)
            x_g, x_a = x_g + r_g, x_a + r_a
        q_g, code_g = scaled(x_g)
        q_a, code_a = scaled(x_a)
        if start != width_g or tail != start + width_a:
            out_ref[at, :] = jnp.zeros((size, out_ref.shape[1]), jnp.int16)
        out_ref[at, :width_g] = narrow(q_g)
        out_ref[at, start : start + width_a] = narrow(q_a)
        lane = lax.broadcasted_iota(I32, (size, LANES), 1)
        out_ref[at, tail:] = narrow(jnp.where(lane < LANES // 2, code_g, code_a))


def stage(chunk, spot, received, parts, after):
    use = [part for part in parts if part is not None]
    width_g, width_a = use[0][0].shape[1], use[0][1].shape[1]
    unit = use[0][0].shape[0] // HIGH
    packet = up_to(width_g, LANES) + up_to(width_a, LANES) + LANES
    got = [] if received is None else [received]
    flat = [array for part in use for array in part]
    return pl.pallas_call(
        functools.partial(
            stage_kernel, received is None, tuple(part is not None for part in parts), len(after)
        ),
        grid_spec=pltpu.PrefetchScalarGridSpec(
            num_scalar_prefetch=1,
            grid=(1,),
            in_specs=[pl.BlockSpec((unit, 1), lambda i, c: (c[0], 0))]
            + [ANYWHERE] * len(got)
            + [IN_HBM] * len(flat)
            + [ANYWHERE] * len(after),
            out_specs=pl.BlockSpec((unit, packet), lambda i, c: (0, 0)),
            scratch_shapes=[pltpu.VMEM((unit, array.shape[1]), F32) for array in flat]
            + [pltpu.VMEM((unit, packet), jnp.int16), pltpu.SemaphoreType.DMA((2, 5))],
        ),
        out_shape=jax.ShapeDtypeStruct((unit, packet), jnp.int16),
        compiler_params=params(24),
        name="running_sum",
    )(chunk, spot, *got, *flat, *after)


def side_kernel(plan, counts, z_ref, spot_ref, *refs):
    chunks, klasses, hops, segments, after = plan
    tok, sub, fac = counts
    refs = list(refs)

    def take(n):
        out, refs[:n] = refs[:n], []
        return out

    below = [take(hops) for _ in chunks]
    above = [take(hops) for _ in chunks]
    part = {}
    for k in (0, 1):
        if any((j < HIGH, j >= LOW)[k] for j in chunks):
            part[k] = take(2)
    pieces = [take(2) for _ in segments]
    take(after)
    out_ref = take(1)[0]
    held_g, held_a, got, x_g, x_a = take(5)
    held = (held_g, held_a)
    tables = take(len(segments))
    sems, piece_sems = take(2)
    width_g, width_a = x_g.shape[1], x_a.shape[1]
    unit = held_g.shape[2]
    rows = unit // fac
    slots = pieces[0][0].shape[1]
    cap = slots // (tok * sub)
    many = len(chunks) * unit

    loads = []
    for i, j in enumerate(chunks):
        for k in part:
            if (j < HIGH, j >= LOW)[k]:
                row = (j - (0, LOW)[k]) * unit
                for side in range(2):
                    loads.append(
                        pltpu.make_async_copy(
                            part[k][side].at[pl.ds(row, unit), :], held[side].at[k, i], sems.at[i, 2 * k + side]
                        )
                    )
    for load in loads:
        load.start()
    for i in range(len(chunks)):
        for way, sources in enumerate((below[i], above[i])):
            for hop in range(hops):
                cut = (z_ref[way] <= 1) if hop == 0 else (z_ref[way] == hop + 1)

                @pl.when(cut)
                def _():
                    pltpu.make_async_copy(sources[hop], got.at[way, i], sems.at[i, 4 + way]).start()

    copies = [
        pltpu.make_async_copy(
            pieces[s][half].at[klass],
            tables[s].at[c, pl.ds(half * slots, slots), :],
            piece_sems.at[s, 2 * c + half],
        )
        for c, klass in enumerate(klasses)
        for s in range(len(segments))
        for half in range(2)
    ]
    for copy in copies:
        copy.start()
    for load in loads:
        load.wait()
    for i, j in enumerate(chunks):
        for way, sources in enumerate((below[i], above[i])):
            pltpu.make_async_copy(sources[0], got.at[way, i], sems.at[i, 4 + way]).wait()
        both = j >= LOW and j < HIGH
        for r in range(0, unit, 32):
            at = pl.ds(r, 32)
            b_g, b_a = read_packet(got.at[0, i, at, :], width_g, width_a)
            a_g, a_a = read_packet(got.at[1, i, at, :], width_g, width_a)
            for ref, own_ref, more in ((x_g, held_g, b_g + a_g), (x_a, held_a, b_a + a_a)):
                if both:
                    of_zero = spot_ref[j * unit + r : j * unit + r + 32, :] > 0
                    own = jnp.where(of_zero, own_ref[0, i, at, :], own_ref[1, i, at, :])
                else:
                    own = own_ref[0 if j < LOW else 1, i, at, :]
                full = own + more
                high = full.astype(BF16)
                ref[i * unit + r : i * unit + r + 32, :] = high
                ref[many + i * unit + r : many + i * unit + r + 32, :] = (full - high.astype(F32)).astype(BF16)

    for copy in copies:
        copy.wait()
    dims = (((1,), (1,)), ((), ()))
    for c in range(len(klasses)):
        total = [None, None]
        for s, (side, begin, width) in enumerate(segments):
            x = (x_g, x_a)[side]
            term = lax.dot_general(
                tables[s][c], x[:, begin : begin + width], dims, preferred_element_type=F32
            )
            total[side] = term if total[side] is None else total[side] + term
        for side in range(2):
            sums = total[side][:slots] + total[side][slots:]
            sums = sums[:, :many] + sums[:, many:]
            for zz in range(tok):
                for s in range(sub):
                    begin = (zz * sub + s) * cap
                    for f in range(fac):
                        for i in range(len(chunks)):
                            lane = (c * len(chunks) + i) * rows
                            out_ref[f, s, side, zz, :, lane : lane + rows] = sums[
                                begin : begin + cap, i * unit + f * rows : i * unit + (f + 1) * rows
                            ]


def sides(counts, where_z, spot, chunks, klasses, parts, from_below, from_above, pieces, after):
    tok, sub, fac = counts
    hops = tok - 1
    unit, packet = from_below[0].shape
    segments = tuple((side, begin, array[0].shape[2]) for side, begin, array in pieces)
    slots = pieces[0][2][0].shape[1]
    used = [
        array
        for k in (0, 1)
        if any((j < HIGH, j >= LOW)[k] for j in chunks)
        for array in parts[k]
    ]
    width_g, width_a = parts[0][0].shape[1], parts[0][1].shape[1]
    near = [array for j in chunks for array in from_below[j : j + hops]]
    near += [array for j in chunks for array in from_above[j : j + hops]]
    flat = [array for _, _, pair in pieces for array in pair]
    lanes = len(klasses) * len(chunks) * (unit // fac)
    many = 2 * len(chunks) * unit
    return pl.pallas_call(
        functools.partial(side_kernel, (tuple(chunks), tuple(klasses), hops, segments, len(after)), counts),
        in_specs=[SCALARS, WHOLE]
        + [ANYWHERE] * len(near)
        + [IN_HBM] * (len(used) + len(flat))
        + [ANYWHERE] * len(after),
        out_specs=WHOLE,
        out_shape=jax.ShapeDtypeStruct((fac, sub, 2, tok, slots // (tok * sub), lanes), F32),
        scratch_shapes=[
            pltpu.VMEM((2, len(chunks), unit, width_g), F32),
            pltpu.VMEM((2, len(chunks), unit, width_a), F32),
            pltpu.VMEM((2, len(chunks), unit, packet), jnp.int16),
            pltpu.VMEM((many, width_g), BF16),
            pltpu.VMEM((many, width_a), BF16),
        ]
        + [pltpu.VMEM((len(klasses), 2 * slots, width), BF16) for _, _, width in segments]
        + [
            pltpu.SemaphoreType.DMA((len(chunks), 6)),
            pltpu.SemaphoreType.DMA((len(segments), 2 * len(klasses))),
        ],
        compiler_params=params(60),
        name="side_sums",
    )(where_z, spot, *near, *used, *flat, *after)


def final_kernel(groups, counts, first_ref, place_ref, slot_ref, *refs):
    out_ref = refs[-1]
    rows = [[], []]
    for i, runs in enumerate(groups):
        ref = refs[i]
        total = ref[0]
        for hop in range(1, counts):
            total = total + ref[hop]
        scores = total[0] * total[1] * (1.0 / math.sqrt(FH * D))
        at = 0
        for klass, lanes in runs:
            rows[klass].append(scores[:, at : at + lanes])
            at += lanes
    cap = rows[0][0].shape[0]
    block, half_rows = out_ref.shape
    result = jnp.zeros((block, half_rows), F32)
    for klass in range(2):
        scores = jnp.concatenate(rows[klass], axis=1)
        count = scores.shape[1]
        begin = (0, LOW * (count // HIGH))[klass]
        row = lax.broadcasted_iota(I32, (block, count), 1) + begin
        of_class = (row < first_ref[0]) if klass == 0 else (row >= first_ref[0])
        to_query = ((place_ref[...] == row) & of_class).astype(F32)
        to_token = (lax.broadcasted_iota(I32, (cap, half_rows), 0) + klass * cap == slot_ref[...]).astype(F32)
        by_query = lax.dot_general(
            to_query, scores, (((1,), (1,)), ((), ())),
            precision=lax.Precision.HIGHEST, preferred_element_type=F32,
        )
        result = result + jnp.dot(
            by_query, to_token, precision=lax.Precision.HIGHEST, preferred_element_type=F32
        )
    out_ref[...] = result


def final(groups, first, place, slot, sums):
    counts = sums[0].shape[0]
    return pl.pallas_call(
        functools.partial(final_kernel, groups, counts),
        in_specs=[SCALARS] + [WHOLE] * (2 + len(sums)),
        out_specs=WHOLE,
        out_shape=jax.ShapeDtypeStruct((place.shape[0], slot.shape[1]), F32),
        compiler_params=params(24),
        name="place_scores",
    )(first, place, slot, *sums)


def body(
    activations,
    gradients,
    tok_class,
    query_inputs,
    query_gradients,
    query_class,
    basis_a,
    basis_g,
    eigen_a,
    eigen_g,
):
    deep_g, width_g = basis_g.shape[1:]
    deep_a, width_a = basis_a.shape[1:]
    counts = tok_count, sub_count, fac_count = tuple(lax.axis_size(a) for a in ("tok", "sub", "fac"))
    z, core, x = (lax.axis_index(a) for a in ("tok", "sub", "fac"))
    block = query_inputs.shape[0] // fac_count
    rows = block // CHUNKS
    tok_rows = activations.shape[0]
    half_rows = tok_rows // sub_count
    slot_cap = 5 * half_rows // 8
    share = half_rows // fac_count
    halves = tok_count * sub_count
    slots = halves * slot_cap
    token_ids = tok_class[:, 0]
    query_ids = query_class[:, 0]

    at = (core * fac_count + x) * share
    room = up_to(deep_g, LANES)
    blocks = []
    for step in range(tok_count):
        to = lax.rem(z + step, tok_count)
        blocks.append(
            jnp.concatenate(
                [
                    lax.dynamic_slice(gradients, (at, to * deep_g), (share, deep_g)),
                    jnp.zeros((share, room - deep_g), BF16),
                    lax.dynamic_slice(activations, (at, to * deep_a), (share, deep_a)),
                ],
                axis=1,
            )
        )
    moved = [blocks[0]] + [
        lax.ppermute(blocks[step], "tok", turn(tok_count, step)) for step in range(1, tok_count)
    ]

    qids = query_ids.reshape(fac_count, block)
    key = qids * block + jnp.arange(block)
    place = jnp.sum((key[:, None, :] < key[:, :, None]).astype(I32), axis=2)
    first = jnp.sum((qids == 0).astype(I32), axis=1)
    spot = (jnp.arange(CHUNKS)[:, None, None] * rows + jnp.arange(rows)) < first[None, :, None]
    spot = spot.reshape(query_ids.shape[0], 1).astype(I32)
    part_g = query_coords(0, place, query_gradients, basis_g, fac_count, rows, blocks[1:])
    part_a = query_coords(0, place, query_inputs, basis_a, fac_count, rows, blocks[1:])
    parts = [(part_g, part_a), None]

    ids = token_ids.reshape(halves, half_rows)
    earlier = jnp.arange(half_rows)[None, :] < jnp.arange(half_rows)[:, None]
    rank = jnp.sum(((ids[:, None, :] == ids[:, :, None]) & earlier).astype(I32), axis=2)
    slot = ids * slots + jnp.arange(halves)[:, None] * slot_cap + rank
    slot = slot.reshape(halves * fac_count, share)
    own_slot = lax.dynamic_index_in_dim(ids * slot_cap + rank, z * sub_count + core, 0)
    weight_g = 1.0 / (eigen_g + DAMPING)
    weight_a = 1.0 / (eigen_a + DAMPING)
    places = jnp.stack([z, core, x]).astype(I32)
    where_z = jnp.stack([z, tok_count - 1 - z]).astype(I32)

    state = {"pieces": []}

    def second(side):
        def run(after):
            features, basis = ((query_gradients, basis_g), (query_inputs, basis_a))[side]
            state[side] = query_coords(1, place, features, basis, fac_count, rows, after)
            if 0 in state and 1 in state:
                parts[1] = (state[0], state[1])
            return state[side]

        return run

    def joined(after):
        mine = join(moved, after)
        raws = [mine]
        for step in range(1, fac_count):
            raws.append(lax.ppermute(mine, "fac", turn(fac_count, step)))
        for step in range(1, sub_count):
            raws += [lax.ppermute(raw, "sub", turn(sub_count, step)) for raw in raws[:fac_count]]
        state["raws"] = raws
        return mine

    def packed(after):
        state["packed"] = pack(counts, places, slot, state["raws"], slots, after)
        return state["packed"]

    def token(side, column):
        def run(after):
            weight, basis = ((weight_g, basis_g), (weight_a, basis_a))[side]
            pair = token_coords(state["packed"], weight, basis, (0, room)[side], column, SEGMENT if side == 0 else width_a, after)
            state["pieces"].append((side, column, pair))
            return pair[0]

        return run

    from_below, from_above = [], []
    groups, sent = [], []

    def batch(chunks, klasses):
        def run(after):
            out = sides(
                counts, where_z, spot, chunks, klasses, parts, from_below, from_above, state["pieces"], after
            )
            groups.append(tuple((k, rows) for k in klasses for _ in chunks))
            sent.append(out)
            return out

        return run

    fillers = [[second(0)], [second(1), joined], [], [packed]]
    fillers += [[token(0, column)] for column in range(0, width_g, SEGMENT)]
    fillers[-1].append(token(1, 0))
    needs = {4 - i: j + tok_count - 2 for i, j in enumerate((LOW - 1, HIGH - 1, CHUNKS - 2, CHUNKS - 1))}
    fillers.append([batch(list(range(LOW)), [0])])
    fillers.append([batch(list(range(LOW, HIGH)), [0, 1])])
    fillers.append([batch(list(range(HIGH, CHUNKS - 1)), [1])])
    fillers.append([batch([CHUNKS - 1], [1])])

    up = [(i, i + 1) for i in range(tok_count - 1)]
    down = [(i + 1, i) for i in range(tok_count - 1)]
    after = []
    steps = CHUNKS + tok_count - 2
    for step in range(steps):
        for got, pairs, behind in ((from_below, up, z), (from_above, down, tok_count - 1 - z)):
            chunk = jnp.clip(step - behind, 0, CHUNKS - 1).astype(I32).reshape(1)
            early, late = max(step - tok_count + 1, 0), min(step, CHUNKS - 1)
            wanted = [parts[0] if early < HIGH else None, parts[1] if late >= LOW else None]
            packet = stage(chunk, spot, got[-1] if step else None, wanted, after)
            got.append(lax.ppermute(packet, "tok", pairs))
            after = [packet]
        if step < steps - 1 and fillers and needs.get(len(fillers), 0) <= step:
            for item in fillers.pop(0):
                after = [item(after)]
    for items in fillers:
        for item in items:
            item(after)
            after = []

    sums = []
    for parts_of in (sent[:2], sent[2:]):
        lanes = [out.shape[-1] for out in parts_of]
        whole = parts_of[0] if len(parts_of) == 1 else jnp.concatenate(parts_of, axis=-1)
        total = lax.dynamic_index_in_dim(whole, core, 1, keepdims=False)
        for step in range(1, sub_count):
            send = lax.dynamic_index_in_dim(whole, lax.rem(core + step, sub_count), 1, keepdims=False)
            total = total + lax.ppermute(send, "sub", turn(sub_count, step))
        whole = total
        total = lax.dynamic_index_in_dim(whole, x, 0, keepdims=False)
        for step in range(1, fac_count):
            send = lax.dynamic_index_in_dim(whole, lax.rem(x + step, fac_count), 0, keepdims=False)
            total = total + lax.ppermute(send, "fac", turn(fac_count, step))
        hops = [lax.dynamic_index_in_dim(total, z, 1, keepdims=False)]
        for step in range(1, tok_count):
            send = lax.dynamic_index_in_dim(total, lax.rem(z + step, tok_count), 1, keepdims=False)
            hops.append(lax.ppermute(send, "tok", turn(tok_count, step)))
        sums.append(jnp.stack(hops))
    runs = [groups[0] + groups[1], groups[2] + groups[3]]
    own_place = lax.dynamic_index_in_dim(place, x, 0, keepdims=False).reshape(block, 1)
    own_first = lax.dynamic_index_in_dim(first, x, 0, keepdims=False).reshape(1)
    return final(runs, own_first, own_place, own_slot, sums)


def solution(mesh):
    placed = (
        P(("grp", "tok"), None),
        P(("grp", "tok"), None),
        P("grp", None),
        P("grp", "tok"),
        P("grp", "tok"),
        P("grp", None),
        P(None, "tok", ("fac", "sub")),
        P(None, "tok", ("fac", "sub")),
        P(None, ("fac", "sub")),
        P(None, ("fac", "sub")),
    )
    return jax.shard_map(
        body, mesh=mesh, in_specs=placed, out_specs=P("fac", ("grp", "tok", "sub")), check_vma=False
    )
```

```python
import functools
import math

import jax
import jax.numpy as jnp
from jax import lax
from jax.experimental import pallas as pl
from jax.experimental.pallas import tpu as pltpu
from jax.sharding import PartitionSpec as P

D = 5120
FH = 13824
DAMPING = 0.25
CHUNKS = 8
LOW, HIGH = 3 * CHUNKS // 8, 5 * CHUNKS // 8
LARGEST = 32760.0
LANES = 128
TILE = 512
SEGMENT = 4 * TILE
GROUP = 2
MIB = 1 << 20
F32 = jnp.float32
BF16 = jnp.bfloat16
I32 = jnp.int32
FINE = 8.0 / math.log(2.0)
IN_HBM = pl.BlockSpec(memory_space=pltpu.HBM)
ANYWHERE = pl.BlockSpec(memory_space=pl.ANY)
SCALARS = pl.BlockSpec(memory_space=pltpu.SMEM)
WHOLE = pl.BlockSpec(memory_space=pltpu.VMEM)


def up_to(n, m):
    return -(-n // m) * m


def params():
    return pltpu.CompilerParams(vmem_limit_bytes=60 * MIB)


def turn(count, step):
    return [(i, (i + step) % count) for i in range(count)]


def query_kernel(fac, rows, first, place_ref, feat_ref, basis_ref, *refs):
    out_ref, sorted_ref = refs[-2:]
    block = place_ref.shape[1]
    unit = fac * rows
    chunks = HIGH

    @pl.when(pl.program_id(0) == 0)
    def _():
        for f in range(fac):
            spots = lax.broadcasted_iota(I32, (chunks * rows, block), 0) + first * rows
            order = (spots == place_ref[f : f + 1, :]).astype(F32).astype(BF16)
            moved = jnp.dot(
                order, feat_ref[f * block : (f + 1) * block, :], preferred_element_type=F32
            ).astype(BF16)
            for j in range(chunks):
                sorted_ref[j * unit + f * rows : j * unit + (f + 1) * rows, :] = moved[
                    j * rows : (j + 1) * rows, :
                ]

    out_ref[...] = jnp.dot(sorted_ref[...], basis_ref[0], preferred_element_type=F32)


def query_coords(klass, place, features, basis, fac, rows, after=()):
    queries, deep = features.shape
    width = basis.shape[2]
    tile = min(TILE, width)
    count = HIGH * fac * rows
    return pl.pallas_call(
        functools.partial(query_kernel, fac, rows, (0, LOW)[klass]),
        grid=(pl.cdiv(width, tile),),
        in_specs=[
            pl.BlockSpec(place.shape, lambda i: (0, 0)),
            pl.BlockSpec((queries, deep), lambda i: (0, 0)),
            pl.BlockSpec((1, deep, tile), lambda i: (klass, 0, i)),
        ]
        + [ANYWHERE] * len(after),
        out_specs=pl.BlockSpec((count, tile), lambda i: (0, i)),
        out_shape=jax.ShapeDtypeStruct((count, width), F32),
        scratch_shapes=[pltpu.VMEM((count, deep), BF16)],
        compiler_params=params(),
        name="query_coords",
    )(place, features, basis, *after)


def join_kernel(count, *refs):
    sources, out_ref, sems = refs[:count], refs[-2], refs[-1]
    size = sources[0].shape[0]
    copies = [
        pltpu.make_async_copy(ref, out_ref.at[pl.ds(i * size, size), :], sems.at[i])
        for i, ref in enumerate(sources)
    ]
    for copy in copies:
        copy.start()
    for copy in copies:
        copy.wait()


def join(blocks, after):
    size, width = blocks[0].shape
    return pl.pallas_call(
        functools.partial(join_kernel, len(blocks)),
        in_specs=[ANYWHERE] * (len(blocks) + len(after)),
        out_specs=WHOLE,
        out_shape=jax.ShapeDtypeStruct((size * len(blocks), width), BF16),
        scratch_shapes=[pltpu.SemaphoreType.DMA((len(blocks),))],
        compiler_params=params(),
        name="join_tokens",
    )(*blocks, *after)


def pack_kernel(counts, slots, room, at_ref, slot_ref, *refs):
    tok, sub, fac = counts
    raws = refs[: sub * fac]
    g_ref, a_ref, raw_ref, sems = refs[-4:]
    size = raws[0].shape[0]
    copies = [
        pltpu.make_async_copy(ref, raw_ref.at[pl.ds(i * size, size), :], sems.at[i])
        for i, ref in enumerate(raws)
    ]
    for copy in copies:
        copy.start()
    here = []
    for s in range(sub):
        for f in range(fac):
            for k in range(tok):
                row = lax.rem(at_ref[0] + tok - k, tok) * sub + lax.rem(at_ref[1] + sub - s, sub)
                row = row * fac + lax.rem(at_ref[2] + fac - f, fac)
                here.append(slot_ref[pl.ds(row, 1), :])
    here = jnp.concatenate(here, axis=1)
    for copy in copies:
        copy.wait()
    for klass in range(2):
        table = lax.broadcasted_iota(I32, (slots, here.shape[1]), 0) + klass * slots == here
        table = table.astype(F32).astype(BF16)
        for ref, begin in ((g_ref, 0), (a_ref, room)):
            ref[klass] = jnp.dot(
                table, raw_ref[:, begin : begin + ref.shape[2]], preferred_element_type=F32
            ).astype(BF16)


def pack(counts, at, slot, raws, slots, deep_g, deep_a, after):
    size, width = raws[0].shape
    return pl.pallas_call(
        functools.partial(pack_kernel, counts, slots, up_to(deep_g, LANES)),
        in_specs=[SCALARS, WHOLE] + [ANYWHERE] * (len(raws) + len(after)),
        out_specs=[WHOLE, WHOLE],
        out_shape=[jax.ShapeDtypeStruct((2, slots, deep), BF16) for deep in (deep_g, deep_a)],
        scratch_shapes=[
            pltpu.VMEM((size * len(raws), width), BF16),
            pltpu.SemaphoreType.DMA((len(raws),)),
        ],
        compiler_params=params(),
        name="pack_tokens",
    )(at, slot, *raws, *after)


def token_kernel(packed_ref, weight_ref, basis_ref, *refs):
    high_ref, low_ref = refs[-2:]
    for klass in range(2):
        coords = (
            jnp.dot(packed_ref[klass], basis_ref[klass], preferred_element_type=F32)
            * weight_ref[klass : klass + 1, :]
        )
        high = coords.astype(BF16)
        high_ref[klass] = high
        low_ref[klass] = (coords - high.astype(F32)).astype(BF16)


def token_coords(packed, weight, basis, column, segment, after):
    slots = packed.shape[1]
    deep, width = basis.shape[1:]
    here = min(segment, width - column)
    tile = min(TILE, width)
    base = column // tile
    out = jax.ShapeDtypeStruct((2, slots, here), BF16)
    return pl.pallas_call(
        token_kernel,
        grid=(pl.cdiv(here, tile),),
        in_specs=[
            pl.BlockSpec((2, slots, deep), lambda i: (0, 0, 0)),
            pl.BlockSpec((2, tile), lambda i: (0, base + i)),
            pl.BlockSpec((2, deep, tile), lambda i: (0, 0, base + i)),
        ]
        + [ANYWHERE] * len(after),
        out_specs=[pl.BlockSpec((2, slots, tile), lambda i: (0, 0, i))] * 2,
        out_shape=[out, out],
        compiler_params=params(),
        name="token_coords",
    )(packed, weight, basis, *after)


def scaled(x):
    top = jnp.max(jnp.abs(x), axis=1, keepdims=True)
    code = jnp.ceil(jnp.log(jnp.maximum(top, 1e-30)) * FINE)
    factor = LARGEST * jnp.exp(code * (-1.0 / FINE))
    return lax.round(x * factor, lax.RoundingMethod.TO_NEAREST_EVEN), code


def narrow(x):
    return x.astype(I32).astype(jnp.int16)


def wide(x):
    return x.astype(I32).astype(F32)


def read_packet(ref, width_g, width_a):
    start = up_to(width_g, LANES)
    tail = start + up_to(width_a, LANES)
    step = jnp.exp(wide(ref[:, tail : tail + LANES]) * (1.0 / FINE)) * (1.0 / LARGEST)
    return (
        wide(ref[:, :width_g]) * step[:, 0:1],
        wide(ref[:, start : start + width_a]) * step[:, LANES - 1 : LANES],
    )


def stage_kernel(first, parts, after, chunk_ref, spot_ref, *refs):
    got = None if first else refs[0]
    refs = refs[0 if first else 1 :]
    use = [k for k in range(2) if parts[k]]
    part = {k: (refs[2 * i], refs[2 * i + 1]) for i, k in enumerate(use)}
    refs = refs[2 * len(use) + after :]
    out_ref, refs = refs[0], refs[1:]
    held = {k: (refs[2 * i], refs[2 * i + 1]) for i, k in enumerate(use)}
    got_ref, sems = refs[2 * len(use) :]
    size = out_ref.shape[0] // GROUP
    width_g, width_a = part[use[0]][0].shape[1], part[use[0]][1].shape[1]
    start = up_to(width_g, LANES)
    tail = start + up_to(width_a, LANES)

    def copies(k, h):
        row = pl.multiple_of((chunk_ref[0] * GROUP + h - (0, LOW)[k]) * size, size)
        return [
            pltpu.make_async_copy(
                part[k][side].at[pl.ds(row, size), :],
                held[k][side].at[pl.ds(h * size, size), :],
                sems.at[h, 2 * k + side],
            )
            for side in range(2)
        ]

    def each(h, act):
        if got is not None:
            act(
                pltpu.make_async_copy(
                    got.at[pl.ds(h * size, size), :], got_ref.at[pl.ds(h * size, size), :], sems.at[h, 4]
                )
            )
        here = chunk_ref[0] * GROUP + h
        for k in use:
            if len(use) == 1:
                for copy in copies(k, h):
                    act(copy)
            else:

                @pl.when((here < HIGH) if k == 0 else (here >= LOW))
                def _():
                    for copy in copies(k, h):
                        act(copy)

    for h in range(GROUP):
        each(h, lambda copy: copy.start())
    for h in range(GROUP):
        each(h, lambda copy: copy.wait())
        at = slice(h * size, (h + 1) * size)
        if len(use) == 1:
            x_g, x_a = (ref[at, :] for ref in held[use[0]])
        else:
            of_zero = spot_ref[at, :] > 0
            x_g, x_a = (jnp.where(of_zero, held[0][i][at, :], held[1][i][at, :]) for i in range(2))
        if got is not None:
            r_g, r_a = read_packet(got_ref.at[pl.ds(h * size, size), :], width_g, width_a)
            x_g, x_a = x_g + r_g, x_a + r_a
        q_g, code_g = scaled(x_g)
        q_a, code_a = scaled(x_a)
        if start != width_g or tail != start + width_a:
            out_ref[at, :] = jnp.zeros((size, out_ref.shape[1]), jnp.int16)
        out_ref[at, :width_g] = narrow(q_g)
        out_ref[at, start : start + width_a] = narrow(q_a)
        lane = lax.broadcasted_iota(I32, (size, LANES), 1)
        out_ref[at, tail:] = narrow(jnp.where(lane < LANES // 2, code_g, code_a))


def stage(chunk, spot, received, parts, after):
    use = [part for part in parts if part is not None]
    width_g, width_a = use[0][0].shape[1], use[0][1].shape[1]
    unit = use[0][0].shape[0] // HIGH * GROUP
    packet = up_to(width_g, LANES) + up_to(width_a, LANES) + LANES
    got = [] if received is None else [received]
    flat = [array for part in use for array in part]
    return pl.pallas_call(
        functools.partial(
            stage_kernel, received is None, tuple(part is not None for part in parts), len(after)
        ),
        grid_spec=pltpu.PrefetchScalarGridSpec(
            num_scalar_prefetch=1,
            grid=(1,),
            in_specs=[pl.BlockSpec((unit, 1), lambda i, c: (c[0], 0))]
            + [ANYWHERE] * len(got)
            + [IN_HBM] * len(flat)
            + [ANYWHERE] * len(after),
            out_specs=pl.BlockSpec((unit, packet), lambda i, c: (0, 0)),
            scratch_shapes=[pltpu.VMEM((unit, array.shape[1]), F32) for array in flat]
            + [pltpu.VMEM((unit, packet), jnp.int16), pltpu.SemaphoreType.DMA((GROUP, 5))],
        ),
        out_shape=jax.ShapeDtypeStruct((unit, packet), jnp.int16),
        compiler_params=params(),
        name="running_sum",
    )(chunk, spot, *got, *flat, *after)


def side_kernel(plan, counts, z_ref, spot_ref, *refs):
    units, spans, hops, segments, after = plan
    tok, sub, fac = counts
    refs = list(refs)

    def take(n):
        out, refs[:n] = refs[:n], []
        return out

    chunks = sorted({u // GROUP for u in units})
    below = {c: take(hops) for c in chunks}
    above = {c: take(hops) for c in chunks}
    needs = {u: [k for k in (0, 1) if (u < HIGH, u >= LOW)[k]] for u in units}
    part = {k: take(2) for k in (0, 1) if any(k in needs[u] for u in units)}
    pieces = [take(2) for _ in segments]
    take(after)
    out_ref = take(1)[0]
    held_g, held_a, got, x_g, x_a = take(5)
    tables = take(len(segments))
    sems, piece_sems = take(2)
    held = (held_g, held_a)
    width_g, width_a = x_g.shape[1], x_a.shape[1]
    unit = got.shape[2]
    rows = unit // fac
    slots = pieces[0][0].shape[1]
    cap = slots // (tok * sub)
    spot_of = {}
    for u in units:
        for k in needs[u]:
            spot_of[u, k] = len(spot_of)

    def own(i, u):
        return [
            pltpu.make_async_copy(
                part[k][side].at[pl.ds((u - (0, LOW)[k]) * unit, unit), :],
                held[side].at[spot_of[u, k]],
                sems.at[i, 2 * k + side],
            )
            for k in needs[u]
            for side in range(2)
        ]

    def arrived(i, u, way, hop):
        source = (below, above)[way][u // GROUP][hop]
        return pltpu.make_async_copy(
            source.at[pl.ds(u % GROUP * unit, unit), :], got.at[way, i], sems.at[i, 4 + way]
        )

    for i, u in enumerate(units):
        for copy in own(i, u):
            copy.start()
        for way in range(2):
            for hop in range(hops):
                cut = (z_ref[way] <= 1) if hop == 0 else (z_ref[way] == hop + 1)

                @pl.when(cut)
                def _():
                    arrived(i, u, way, hop).start()

    copies = [
        pltpu.make_async_copy(
            pieces[s][half].at[klass],
            tables[s].at[c, pl.ds(half * slots, slots), :],
            piece_sems.at[s, 2 * c + half],
        )
        for c, (klass, _) in enumerate(spans)
        for s in range(len(segments))
        for half in range(2)
    ]
    for copy in copies:
        copy.start()
    for i, u in enumerate(units):
        for copy in own(i, u):
            copy.wait()
        for way in range(2):
            arrived(i, u, way, 0).wait()
        for r in range(0, unit, 32):
            at = pl.ds(r, 32)
            b_g, b_a = read_packet(got.at[0, i, at, :], width_g, width_a)
            a_g, a_a = read_packet(got.at[1, i, at, :], width_g, width_a)
            for ref, own_ref, more in ((x_g, held_g, b_g + a_g), (x_a, held_a, b_a + a_a)):
                full = own_ref[spot_of[u, needs[u][0]], at, :]
                if len(needs[u]) == 2:
                    of_zero = spot_ref[u * unit + r : u * unit + r + 32, :] > 0
                    full = jnp.where(of_zero, full, own_ref[spot_of[u, 1], at, :])
                full = full + more
                high = full.astype(BF16)
                top = 2 * i * unit + r
                ref[top : top + 32, :] = high
                ref[top + unit : top + unit + 32, :] = (full - high.astype(F32)).astype(BF16)

    for copy in copies:
        copy.wait()
    dims = (((1,), (1,)), ((), ()))
    lane = 0
    for c, (klass, members) in enumerate(spans):
        first = units.index(members[0])
        span = slice(2 * first * unit, 2 * (first + len(members)) * unit)
        total = [None, None]
        for s, (side, begin, width) in enumerate(segments):
            x = (x_g, x_a)[side]
            term = lax.dot_general(
                tables[s][c], x[span, begin : begin + width], dims, preferred_element_type=F32
            )
            total[side] = term if total[side] is None else total[side] + term
        for side in range(2):
            sums = total[side][:slots] + total[side][slots:]
            for i in range(len(members)):
                of_unit = (
                    sums[:, 2 * i * unit : (2 * i + 1) * unit] + sums[:, (2 * i + 1) * unit : (2 * i + 2) * unit]
                )
                for f in range(fac):
                    here = of_unit[:, f * rows : (f + 1) * rows]
                    for zz in range(tok):
                        for s in range(sub):
                            begin = (zz * sub + s) * cap
                            out_ref[f, s, side, zz, :, lane + i * rows : lane + (i + 1) * rows] = here[
                                begin : begin + cap
                            ]
        lane += len(members) * rows


def sides(counts, where_z, spot, units, spans, parts, from_below, from_above, pieces, after):
    tok, sub, fac = counts
    hops = tok - 1
    packet = from_below[0].shape[1]
    unit = from_below[0].shape[0] // GROUP
    segments = tuple((side, begin, array[0].shape[2]) for side, begin, array in pieces)
    slots = pieces[0][2][0].shape[1]
    needs = [[k for k in (0, 1) if (u < HIGH, u >= LOW)[k]] for u in units]
    used = [array for k in (0, 1) if any(k in some for some in needs) for array in parts[k]]
    width_g, width_a = parts[0][0].shape[1], parts[0][1].shape[1]
    chunks = sorted({u // GROUP for u in units})
    near = [array for c in chunks for array in from_below[c : c + hops]]
    near += [array for c in chunks for array in from_above[c : c + hops]]
    flat = [array for _, _, pair in pieces for array in pair]
    lanes = sum(len(members) for _, members in spans) * (unit // fac)
    owns = sum(len(some) for some in needs)
    many = 2 * len(units) * unit
    return pl.pallas_call(
        functools.partial(side_kernel, (units, spans, hops, segments, len(after)), counts),
        in_specs=[SCALARS, WHOLE]
        + [ANYWHERE] * len(near)
        + [IN_HBM] * (len(used) + len(flat))
        + [ANYWHERE] * len(after),
        out_specs=WHOLE,
        out_shape=jax.ShapeDtypeStruct((fac, sub, 2, tok, slots // (tok * sub), lanes), F32),
        scratch_shapes=[
            pltpu.VMEM((owns, unit, width_g), F32),
            pltpu.VMEM((owns, unit, width_a), F32),
            pltpu.VMEM((2, len(units), unit, packet), jnp.int16),
            pltpu.VMEM((many, width_g), BF16),
            pltpu.VMEM((many, width_a), BF16),
        ]
        + [pltpu.VMEM((len(spans), 2 * slots, width), BF16) for _, _, width in segments]
        + [
            pltpu.SemaphoreType.DMA((len(units), 6)),
            pltpu.SemaphoreType.DMA((len(segments), 2 * len(spans))),
        ],
        compiler_params=params(),
        name="side_sums",
    )(where_z, spot, *near, *used, *flat, *after)


def final_kernel(groups, counts, first_ref, place_ref, slot_ref, *refs):
    out_ref = refs[-1]
    rows = [[], []]
    for i, runs in enumerate(groups):
        ref = refs[i]
        total = ref[0]
        for hop in range(1, counts):
            total = total + ref[hop]
        scores = total[0] * total[1] * (1.0 / math.sqrt(FH * D))
        at = 0
        for klass, lanes in runs:
            rows[klass].append(scores[:, at : at + lanes])
            at += lanes
    cap = rows[0][0].shape[0]
    block, half_rows = out_ref.shape
    result = jnp.zeros((block, half_rows), F32)
    for klass in range(2):
        scores = jnp.concatenate(rows[klass], axis=1)
        count = scores.shape[1]
        begin = (0, LOW * (count // HIGH))[klass]
        row = lax.broadcasted_iota(I32, (block, count), 1) + begin
        of_class = (row < first_ref[0]) if klass == 0 else (row >= first_ref[0])
        to_query = ((place_ref[...] == row) & of_class).astype(F32)
        to_token = (lax.broadcasted_iota(I32, (cap, half_rows), 0) + klass * cap == slot_ref[...]).astype(F32)
        by_query = lax.dot_general(
            to_query, scores, (((1,), (1,)), ((), ())),
            precision=lax.Precision.HIGHEST, preferred_element_type=F32,
        )
        result = result + jnp.dot(
            by_query, to_token, precision=lax.Precision.HIGHEST, preferred_element_type=F32
        )
    out_ref[...] = result


def final(groups, first, place, slot, sums):
    counts = sums[0].shape[0]
    return pl.pallas_call(
        functools.partial(final_kernel, groups, counts),
        in_specs=[SCALARS] + [WHOLE] * (2 + len(sums)),
        out_specs=WHOLE,
        out_shape=jax.ShapeDtypeStruct((place.shape[0], slot.shape[1]), F32),
        compiler_params=params(),
        name="place_scores",
    )(first, place, slot, *sums)


def body(
    activations,
    gradients,
    tok_class,
    query_inputs,
    query_gradients,
    query_class,
    basis_a,
    basis_g,
    eigen_a,
    eigen_g,
):
    deep_g, width_g = basis_g.shape[1:]
    deep_a, width_a = basis_a.shape[1:]
    counts = tok_count, sub_count, fac_count = tuple(lax.axis_size(a) for a in ("tok", "sub", "fac"))
    z, core, x = (lax.axis_index(a) for a in ("tok", "sub", "fac"))
    block = query_inputs.shape[0] // fac_count
    rows = block // CHUNKS
    tok_rows = activations.shape[0]
    half_rows = tok_rows // sub_count
    slot_cap = 5 * half_rows // 8
    share = half_rows // fac_count
    halves = tok_count * sub_count
    slots = halves * slot_cap
    token_ids = tok_class[:, 0]
    query_ids = query_class[:, 0]

    at = (core * fac_count + x) * share
    room = up_to(deep_g, LANES)
    blocks = []
    for step in range(tok_count):
        to = lax.rem(z + step, tok_count)
        blocks.append(
            jnp.concatenate(
                [
                    lax.dynamic_slice(gradients, (at, to * deep_g), (share, deep_g)),
                    jnp.zeros((share, room - deep_g), BF16),
                    lax.dynamic_slice(activations, (at, to * deep_a), (share, deep_a)),
                ],
                axis=1,
            )
        )
    moved = [blocks[0]] + [
        lax.ppermute(blocks[step], "tok", turn(tok_count, step)) for step in range(1, tok_count)
    ]

    qids = query_ids.reshape(fac_count, block)
    key = qids * block + jnp.arange(block)
    place = jnp.sum((key[:, None, :] < key[:, :, None]).astype(I32), axis=2)
    first = jnp.sum((qids == 0).astype(I32), axis=1)
    spot = (jnp.arange(CHUNKS)[:, None, None] * rows + jnp.arange(rows)) < first[None, :, None]
    spot = spot.reshape(query_ids.shape[0], 1).astype(I32)
    part_g = query_coords(0, place, query_gradients, basis_g, fac_count, rows, blocks[1:])
    part_a = query_coords(0, place, query_inputs, basis_a, fac_count, rows, blocks[1:])
    parts = [(part_g, part_a), None]

    ids = token_ids.reshape(halves, half_rows)
    earlier = jnp.arange(half_rows)[None, :] < jnp.arange(half_rows)[:, None]
    rank = jnp.sum(((ids[:, None, :] == ids[:, :, None]) & earlier).astype(I32), axis=2)
    slot = ids * slots + jnp.arange(halves)[:, None] * slot_cap + rank
    slot = slot.reshape(halves * fac_count, share)
    own_slot = lax.dynamic_index_in_dim(ids * slot_cap + rank, z * sub_count + core, 0)
    weight_g = 1.0 / (eigen_g + DAMPING)
    weight_a = 1.0 / (eigen_a + DAMPING)
    places = jnp.stack([z, core, x]).astype(I32)
    where_z = jnp.stack([z, tok_count - 1 - z]).astype(I32)

    state = {"pieces": []}

    def second(side):
        def run(after):
            features, basis = ((query_gradients, basis_g), (query_inputs, basis_a))[side]
            state[side] = query_coords(1, place, features, basis, fac_count, rows, after)
            if 0 in state and 1 in state:
                parts[1] = (state[0], state[1])
            return state[side]

        return run

    def joined(after):
        mine = join(moved, after)
        raws = [mine]
        for step in range(1, fac_count):
            raws.append(lax.ppermute(mine, "fac", turn(fac_count, step)))
        for step in range(1, sub_count):
            raws += [lax.ppermute(raw, "sub", turn(sub_count, step)) for raw in raws[:fac_count]]
        state["raws"] = raws
        return mine

    def packed(after):
        state["packed"] = pack(counts, places, slot, state["raws"], slots, deep_g, deep_a, after)
        return state["packed"][0]

    def token(side, column):
        def run(after):
            weight, basis = ((weight_g, basis_g), (weight_a, basis_a))[side]
            segment = SEGMENT if side == 0 else width_a
            pair = token_coords(state["packed"][side], weight, basis, column, segment, after)
            state["pieces"].append((side, column, pair))
            return pair[0]

        return run

    from_below, from_above = [], []
    groups, sent = [], []

    def batch(units, spans):
        def run(after):
            out = sides(
                counts, where_z, spot, units, spans, parts, from_below, from_above, state["pieces"], after
            )
            groups.append(tuple((klass, len(members) * rows) for klass, members in spans))
            sent.append(out)
            return out

        return run

    columns = list(range(0, width_g, SEGMENT))
    fillers = [[joined, second(0), second(1)], [packed, token(1, 0)]]
    fillers += [[token(0, column)] for column in columns]
    needs = {}
    for units in (range(4), range(4, 6), range(6, 8)):
        spans = [(k, [u for u in units if (u < HIGH, u >= LOW)[k]]) for k in range(2)]
        needs[len(fillers)] = units[-1] // GROUP + tok_count - 2
        fillers.append([batch(list(units), [span for span in spans if span[1]])])

    up = [(i, i + 1) for i in range(tok_count - 1)]
    down = [(i + 1, i) for i in range(tok_count - 1)]
    after = []
    chunks = CHUNKS // GROUP
    steps = chunks + tok_count - 2
    done = 0
    for step in range(steps):
        for got, pairs, behind in ((from_below, up, z), (from_above, down, tok_count - 1 - z)):
            chunk = jnp.clip(step - behind, 0, chunks - 1).astype(I32).reshape(1)
            early, late = max(step - tok_count + 1, 0) * GROUP, min(step, chunks - 1) * GROUP + GROUP - 1
            wanted = [parts[0] if early < HIGH else None, parts[1] if late >= LOW else None]
            packet = stage(chunk, spot, got[-1] if step else None, wanted, after)
            got.append(lax.ppermute(packet, "tok", pairs))
            after = [packet]
        if step < steps - 1 and needs.get(done, -1) < step:
            for item in fillers[done]:
                after = [item(after)]
            done += 1
    for items in fillers[done:]:
        for item in items:
            after = [item(after)]

    sums = []
    for parts_of in (sent[:2], sent[2:]):
        whole = parts_of[0] if len(parts_of) == 1 else jnp.concatenate(parts_of, axis=-1)
        total = lax.dynamic_index_in_dim(whole, core, 1, keepdims=False)
        for step in range(1, sub_count):
            send = lax.dynamic_index_in_dim(whole, lax.rem(core + step, sub_count), 1, keepdims=False)
            total = total + lax.ppermute(send, "sub", turn(sub_count, step))
        whole = total
        total = lax.dynamic_index_in_dim(whole, x, 0, keepdims=False)
        for step in range(1, fac_count):
            send = lax.dynamic_index_in_dim(whole, lax.rem(x + step, fac_count), 0, keepdims=False)
            total = total + lax.ppermute(send, "fac", turn(fac_count, step))
        hops = [lax.dynamic_index_in_dim(total, z, 1, keepdims=False)]
        for step in range(1, tok_count):
            send = lax.dynamic_index_in_dim(total, lax.rem(z + step, tok_count), 1, keepdims=False)
            hops.append(lax.ppermute(send, "tok", turn(tok_count, step)))
        sums.append(jnp.stack(hops))
    runs = [groups[0] + groups[1], groups[2]]
    own_place = lax.dynamic_index_in_dim(place, x, 0, keepdims=False).reshape(block, 1)
    own_first = lax.dynamic_index_in_dim(first, x, 0, keepdims=False).reshape(1)
    return final(runs, own_first, own_place, own_slot, sums)


def solution(mesh):
    placed = (
        P(("grp", "tok"), None),
        P(("grp", "tok"), None),
        P("grp", None),
        P("grp", "tok"),
        P("grp", "tok"),
        P("grp", None),
        P(None, "tok", ("fac", "sub")),
        P(None, "tok", ("fac", "sub")),
        P(None, ("fac", "sub")),
        P(None, ("fac", "sub")),
    )
    return jax.shard_map(
        body, mesh=mesh, in_specs=placed, out_specs=P("fac", ("grp", "tok", "sub")), check_vma=False
    )
```

```python
import functools
import math

import jax
import jax.numpy as jnp
from jax import lax
from jax.experimental import pallas as pl
from jax.experimental.pallas import tpu as pltpu
from jax.sharding import PartitionSpec as P

D = 5120
FH = 13824
DAMPING = 0.25
CHUNKS = 8
LOW, HIGH = 3 * CHUNKS // 8, 5 * CHUNKS // 8
LARGEST = 32760.0
LANES = 128
TILE = 512
SEGMENT = 4 * TILE
GROUP = 2
MIB = 1 << 20
F32 = jnp.float32
BF16 = jnp.bfloat16
I32 = jnp.int32
FINE = 8.0 / math.log(2.0)
IN_HBM = pl.BlockSpec(memory_space=pltpu.HBM)
ANYWHERE = pl.BlockSpec(memory_space=pl.ANY)
SCALARS = pl.BlockSpec(memory_space=pltpu.SMEM)
WHOLE = pl.BlockSpec(memory_space=pltpu.VMEM)


def up_to(n, m):
    return -(-n // m) * m


def params():
    return pltpu.CompilerParams(vmem_limit_bytes=60 * MIB)


def turn(count, step):
    return [(i, (i + step) % count) for i in range(count)]


def query_kernel(fac, rows, first, tiles, place_ref, feat_g_ref, feat_a_ref, basis_g_ref, basis_a_ref, *refs):
    out_g_ref, out_a_ref, sorted_g_ref, sorted_a_ref = refs[-4:]
    block = place_ref.shape[1]
    unit = fac * rows

    def put(feat_ref, sorted_ref):
        for f in range(fac):
            spots = lax.broadcasted_iota(I32, (HIGH * rows, block), 0) + first * rows
            order = (spots == place_ref[f : f + 1, :]).astype(F32).astype(BF16)
            moved = jnp.dot(
                order, feat_ref[f * block : (f + 1) * block, :], preferred_element_type=F32
            ).astype(BF16)
            for j in range(HIGH):
                sorted_ref[j * unit + f * rows : j * unit + (f + 1) * rows, :] = moved[
                    j * rows : (j + 1) * rows, :
                ]

    step = pl.program_id(0)

    @pl.when(step == 0)
    def _():
        put(feat_g_ref, sorted_g_ref)

    @pl.when(step == tiles)
    def _():
        put(feat_a_ref, sorted_a_ref)

    @pl.when(step < tiles)
    def _():
        out_g_ref[...] = jnp.dot(sorted_g_ref[...], basis_g_ref[0], preferred_element_type=F32)

    @pl.when(step >= tiles)
    def _():
        out_a_ref[...] = jnp.dot(sorted_a_ref[...], basis_a_ref[0], preferred_element_type=F32)


def query_coords(klass, place, feat_g, feat_a, basis_g, basis_a, fac, rows, after=()):
    queries, deep_g = feat_g.shape
    deep_a = feat_a.shape[1]
    width_g, width_a = basis_g.shape[2], basis_a.shape[2]
    tile_g, tile_a = min(TILE, width_g), min(TILE, width_a)
    tiles_g, tiles_a = pl.cdiv(width_g, tile_g), pl.cdiv(width_a, tile_a)
    count = HIGH * fac * rows
    at_g = lambda i: jnp.minimum(i, tiles_g - 1)
    at_a = lambda i: jnp.maximum(i - tiles_g, 0)
    return pl.pallas_call(
        functools.partial(query_kernel, fac, rows, (0, LOW)[klass], tiles_g),
        grid=(tiles_g + tiles_a,),
        in_specs=[
            pl.BlockSpec(place.shape, lambda i: (0, 0)),
            pl.BlockSpec((queries, deep_g), lambda i: (0, 0)),
            pl.BlockSpec((queries, deep_a), lambda i: (0, 0)),
            pl.BlockSpec((1, deep_g, tile_g), lambda i: (klass, 0, at_g(i))),
            pl.BlockSpec((1, deep_a, tile_a), lambda i: (klass, 0, at_a(i))),
        ]
        + [ANYWHERE] * len(after),
        out_specs=[
            pl.BlockSpec((count, tile_g), lambda i: (0, at_g(i))),
            pl.BlockSpec((count, tile_a), lambda i: (0, at_a(i))),
        ],
        out_shape=[jax.ShapeDtypeStruct((count, width), F32) for width in (width_g, width_a)],
        scratch_shapes=[pltpu.VMEM((count, deep), BF16) for deep in (deep_g, deep_a)],
        compiler_params=params(),
        name="query_coords",
    )(place, feat_g, feat_a, basis_g, basis_a, *after)


def join_kernel(count, *refs):
    sources, out_ref, sems = refs[:count], refs[-2], refs[-1]
    size = sources[0].shape[0]
    copies = [
        pltpu.make_async_copy(ref, out_ref.at[pl.ds(i * size, size), :], sems.at[i])
        for i, ref in enumerate(sources)
    ]
    for copy in copies:
        copy.start()
    for copy in copies:
        copy.wait()


def join(blocks, after):
    size, width = blocks[0].shape
    return pl.pallas_call(
        functools.partial(join_kernel, len(blocks)),
        in_specs=[ANYWHERE] * (len(blocks) + len(after)),
        out_specs=WHOLE,
        out_shape=jax.ShapeDtypeStruct((size * len(blocks), width), BF16),
        scratch_shapes=[pltpu.SemaphoreType.DMA((len(blocks),))],
        compiler_params=params(),
        name="join_tokens",
    )(*blocks, *after)


def pack_kernel(counts, slots, tiles, at_ref, slot_ref, *refs):
    tok, sub, fac = counts
    raws = refs[: sub * fac]
    g_ref, a_ref, table_ref = refs[-3:]
    step = pl.program_id(0)

    @pl.when(step == 0)
    def _():
        here = []
        for s in range(sub):
            for f in range(fac):
                for k in range(tok):
                    row = lax.rem(at_ref[0] + tok - k, tok) * sub + lax.rem(at_ref[1] + sub - s, sub)
                    row = row * fac + lax.rem(at_ref[2] + fac - f, fac)
                    here.append(slot_ref[pl.ds(row, 1), :])
        here = jnp.concatenate(here, axis=1)
        some = slots // 2
        for i in range(4):
            spots = lax.broadcasted_iota(I32, (some, here.shape[1]), 0) + i * some
            table_ref[i * some : (i + 1) * some, :] = (spots == here).astype(F32).astype(BF16)

    raw = jnp.concatenate([ref[...] for ref in raws], axis=0)
    moved = jnp.dot(table_ref[...], raw, preferred_element_type=F32).astype(BF16)

    def put(ref):
        for klass in range(2):
            ref[klass] = moved[klass * slots : (klass + 1) * slots, : ref.shape[2]]

    @pl.when(step < tiles)
    def _():
        put(g_ref)

    @pl.when(step >= tiles)
    def _():
        put(a_ref)


def pack(counts, at, slot, raws, slots, deep_g, deep_a, after):
    size = raws[0].shape[0]
    tiles_g, tiles_a = pl.cdiv(deep_g, TILE), pl.cdiv(deep_a, TILE)
    return pl.pallas_call(
        functools.partial(pack_kernel, counts, slots, tiles_g),
        grid=(tiles_g + tiles_a,),
        in_specs=[SCALARS, pl.BlockSpec(slot.shape, lambda i: (0, 0))]
        + [pl.BlockSpec((size, TILE), lambda i: (0, i)) for _ in raws]
        + [ANYWHERE] * len(after),
        out_specs=[
            pl.BlockSpec((2, slots, min(TILE, deep_g)), lambda i: (0, 0, jnp.minimum(i, tiles_g - 1))),
            pl.BlockSpec((2, slots, min(TILE, deep_a)), lambda i: (0, 0, jnp.maximum(i - tiles_g, 0))),
        ],
        out_shape=[jax.ShapeDtypeStruct((2, slots, deep), BF16) for deep in (deep_g, deep_a)],
        scratch_shapes=[pltpu.VMEM((2 * slots, size * len(raws)), BF16)],
        compiler_params=params(),
        name="pack_tokens",
    )(at, slot, *raws, *after)


def token_kernel(packed_ref, weight_ref, basis_ref, *refs):
    high_ref, low_ref = refs[-2:]
    for klass in range(2):
        coords = (
            jnp.dot(packed_ref[klass], basis_ref[klass], preferred_element_type=F32)
            * weight_ref[klass : klass + 1, :]
        )
        high = coords.astype(BF16)
        high_ref[klass] = high
        low_ref[klass] = (coords - high.astype(F32)).astype(BF16)


def token_coords(packed, weight, basis, column, segment, after):
    slots = packed.shape[1]
    deep, width = basis.shape[1:]
    here = min(segment, width - column)
    tile = min(TILE, width)
    base = column // tile
    out = jax.ShapeDtypeStruct((2, slots, here), BF16)
    return pl.pallas_call(
        token_kernel,
        grid=(pl.cdiv(here, tile),),
        in_specs=[
            pl.BlockSpec((2, slots, deep), lambda i: (0, 0, 0)),
            pl.BlockSpec((2, tile), lambda i: (0, base + i)),
            pl.BlockSpec((2, deep, tile), lambda i: (0, 0, base + i)),
        ]
        + [ANYWHERE] * len(after),
        out_specs=[pl.BlockSpec((2, slots, tile), lambda i: (0, 0, i))] * 2,
        out_shape=[out, out],
        compiler_params=params(),
        name="token_coords",
    )(packed, weight, basis, *after)


def tiles_of(width):
    return [(begin, min(LANES, width - begin)) for begin in range(0, width, LANES)]


def code_of(tops):
    top = functools.reduce(jnp.maximum, [jnp.max(top, axis=1, keepdims=True) for top in tops])
    return jnp.ceil(jnp.log(jnp.maximum(top, 1e-30)) * FINE)


def narrow(x):
    return x.astype(I32).astype(jnp.int16)


def wide(x):
    return x.astype(I32).astype(F32)


def steps_of(ref, tail):
    step = jnp.exp(wide(ref[:, tail : tail + LANES]) * (1.0 / FINE)) * (1.0 / LARGEST)
    shape = step.shape
    return (
        jnp.broadcast_to(step[:, 0:1], shape),
        jnp.broadcast_to(step[:, LANES - 1 : LANES], shape),
    )


def stage_kernel(gots, parts, after, at_ref, spot_ref, *refs):
    sources, refs = refs[:gots], refs[gots:]
    use = [k for k in range(2) if parts[k]]
    part = {k: (refs[2 * i], refs[2 * i + 1]) for i, k in enumerate(use)}
    refs = refs[2 * len(use) + after :]
    out_ref, refs = refs[0], refs[1:]
    held = {k: (refs[2 * i], refs[2 * i + 1]) for i, k in enumerate(use)}
    got_ref, sems = refs[2 * len(use) :]
    size = out_ref.shape[0] // GROUP
    widths = tuple(ref.shape[1] for ref in part[use[0]])
    begins = (0, up_to(widths[0], LANES))
    tail = begins[1] + up_to(widths[1], LANES)

    def received(h, source):
        at = pl.ds(h * size, size)
        return pltpu.make_async_copy(source.at[at, :], got_ref.at[at, :], sems.at[h, 4])

    def each(h, act, first):
        if gots == 1 or (gots and not first):
            act(received(h, sources[0]))
        elif gots:
            for i in range(2):

                @pl.when(at_ref[1] == i)
                def _():
                    act(received(h, sources[i]))

        here = at_ref[0] * GROUP + h
        for k in use:
            row = pl.multiple_of((here - (0, LOW)[k]) * size, size)

            def go():
                for side in range(2):
                    act(
                        pltpu.make_async_copy(
                            part[k][side].at[pl.ds(row, size), :],
                            held[k][side].at[pl.ds(h * size, size), :],
                            sems.at[h, 2 * k + side],
                        )
                    )

            if len(use) == 1:
                go()
            else:
                pl.when((here < HIGH) if k == 0 else (here >= LOW))(go)

    for h in range(GROUP):
        each(h, lambda copy: copy.start(), True)
    for h in range(GROUP):
        each(h, lambda copy: copy.wait(), False)
        at = slice(h * size, (h + 1) * size)
        if gots:
            steps = steps_of(got_ref.at[pl.ds(h * size, size), :], tail)
        if len(use) == 2:
            of_zero = jnp.broadcast_to(spot_ref[at, :], (size, LANES)) > 0
        codes = []
        for side in range(2):
            tops = {}
            for begin, wide_by in tiles_of(widths[side]):
                cut = slice(begin, begin + wide_by)
                x = held[use[0]][side][at, cut]
                if len(use) == 2:
                    x = jnp.where(of_zero[:, :wide_by], x, held[1][side][at, cut])
                if gots:
                    there = slice(begins[side] + begin, begins[side] + begin + wide_by)
                    x = x + wide(got_ref[at, there]) * steps[side][:, :wide_by]
                if gots or len(use) == 2:
                    held[use[0]][side][at, cut] = x
                size_of = jnp.abs(x)
                tops[wide_by] = jnp.maximum(tops[wide_by], size_of) if wide_by in tops else size_of
            codes.append(code_of(list(tops.values())))
        for side in range(2):
            factor = jnp.broadcast_to(LARGEST * jnp.exp(codes[side] * (-1.0 / FINE)), (size, LANES))
            for begin, wide_by in tiles_of(widths[side]):
                x = held[use[0]][side][at, begin : begin + wide_by] * factor[:, :wide_by]
                there = begins[side] + begin
                out_ref[at, there : there + wide_by] = narrow(lax.round(x, lax.RoundingMethod.TO_NEAREST_EVEN))
                if wide_by < LANES:
                    out_ref[at, there + wide_by : there + LANES] = jnp.zeros((size, LANES - wide_by), jnp.int16)
        lane = lax.broadcasted_iota(I32, (size, LANES), 1)
        out_ref[at, tail:] = narrow(jnp.where(lane < LANES // 2, codes[0], codes[1]))


def stage(at, spot, got, parts, after):
    use = [part for part in parts if part is not None]
    width_g, width_a = use[0][0].shape[1], use[0][1].shape[1]
    unit = use[0][0].shape[0] // HIGH * GROUP
    packet = up_to(width_g, LANES) + up_to(width_a, LANES) + LANES
    flat = [array for part in use for array in part]
    return pl.pallas_call(
        functools.partial(stage_kernel, len(got), tuple(part is not None for part in parts), len(after)),
        grid_spec=pltpu.PrefetchScalarGridSpec(
            num_scalar_prefetch=1,
            grid=(1,),
            in_specs=[pl.BlockSpec((unit, 1), lambda i, c: (c[0], 0))]
            + [ANYWHERE] * len(got)
            + [IN_HBM] * len(flat)
            + [ANYWHERE] * len(after),
            out_specs=pl.BlockSpec((unit, packet), lambda i, c: (0, 0)),
            scratch_shapes=[pltpu.VMEM((unit, array.shape[1]), F32) for array in flat]
            + [pltpu.VMEM((unit, packet), jnp.int16), pltpu.SemaphoreType.DMA((GROUP, 5))],
        ),
        out_shape=jax.ShapeDtypeStruct((unit, packet), jnp.int16),
        compiler_params=params(),
        name="running_sum",
    )(at, spot, *got, *flat, *after)


def side_kernel(plan, counts, z_ref, spot_ref, *refs):
    units, spans, hops, segments, after = plan
    tok, sub, fac = counts
    refs = list(refs)

    def take(n):
        out, refs[:n] = refs[:n], []
        return out

    chunks = sorted({u // GROUP for u in units})
    below = {c: take(hops) for c in chunks}
    above = {c: take(hops) for c in chunks}
    needs = {u: [k for k in (0, 1) if (u < HIGH, u >= LOW)[k]] for u in units}
    part = {k: take(2) for k in (0, 1) if any(k in needs[u] for u in units)}
    pieces = [take(2) for _ in segments]
    take(after)
    out_ref = take(1)[0]
    held_g, held_a, got, x_g, x_a = take(5)
    tables = take(len(segments))
    sems, piece_sems = take(2)
    held = (held_g, held_a)
    width_g, width_a = x_g.shape[1], x_a.shape[1]
    unit = got.shape[2]
    rows = unit // fac
    slots = pieces[0][0].shape[1]
    cap = slots // (tok * sub)
    room = up_to(width_g, LANES)
    tail = room + up_to(width_a, LANES)
    lanes = out_ref.shape[-1] // 2
    spot_of = {}
    for u in units:
        for k in needs[u]:
            spot_of[u, k] = len(spot_of)

    def own(i, u):
        return [
            pltpu.make_async_copy(
                part[k][side].at[pl.ds((u - (0, LOW)[k]) * unit, unit), :],
                held[side].at[spot_of[u, k]],
                sems.at[i, 2 * k + side],
            )
            for k in needs[u]
            for side in range(2)
        ]

    def arrived(i, u, way, hop):
        source = (below, above)[way][u // GROUP][hop]
        return pltpu.make_async_copy(
            source.at[pl.ds(u % GROUP * unit, unit), :], got.at[way, i], sems.at[i, 4 + way]
        )

    for i, u in enumerate(units):
        for copy in own(i, u):
            copy.start()
        for way in range(2):
            for hop in range(hops):
                cut = (z_ref[way] <= 1) if hop == 0 else (z_ref[way] == hop + 1)

                @pl.when(cut)
                def _():
                    arrived(i, u, way, hop).start()

    copies = [
        pltpu.make_async_copy(
            pieces[s][half].at[klass],
            tables[s].at[c, pl.ds(half * slots, slots), :],
            piece_sems.at[s, 2 * c + half],
        )
        for c, (klass, _) in enumerate(spans)
        for s in range(len(segments))
        for half in range(2)
    ]
    for copy in copies:
        copy.start()
    for i, u in enumerate(units):
        for copy in own(i, u):
            copy.wait()
        for way in range(2):
            arrived(i, u, way, 0).wait()
        below_steps, above_steps = (steps_of(got.at[way, i], tail) for way in range(2))
        if len(needs[u]) == 2:
            of_zero = jnp.broadcast_to(spot_ref[u * unit : (u + 1) * unit, :], (unit, LANES)) > 0
        for side, (ref, own_ref) in enumerate(((x_g, held_g), (x_a, held_a))):
            for begin, wide_by in tiles_of(ref.shape[1]):
                cut = slice(begin, begin + wide_by)
                there = slice((0, room)[side] + begin, (0, room)[side] + begin + wide_by)
                full = own_ref[spot_of[u, needs[u][0]], :, cut]
                if len(needs[u]) == 2:
                    full = jnp.where(of_zero[:, :wide_by], full, own_ref[spot_of[u, 1], :, cut])
                full = full + wide(got[0, i, :, there]) * below_steps[side][:, :wide_by]
                full = full + wide(got[1, i, :, there]) * above_steps[side][:, :wide_by]
                high = full.astype(BF16)
                ref[2 * i * unit : (2 * i + 1) * unit, cut] = high
                ref[(2 * i + 1) * unit : (2 * i + 2) * unit, cut] = (full - high.astype(F32)).astype(BF16)

    for copy in copies:
        copy.wait()
    dims = (((1,), (1,)), ((), ()))
    lane = 0
    for c, (klass, members) in enumerate(spans):
        first = units.index(members[0])
        span = slice(2 * first * unit, 2 * (first + len(members)) * unit)
        total = [None, None]
        for s, (side, begin, width) in enumerate(segments):
            x = (x_g, x_a)[side]
            term = lax.dot_general(
                tables[s][c], x[span, begin : begin + width], dims, preferred_element_type=F32
            )
            total[side] = term if total[side] is None else total[side] + term
        for side in range(2):
            sums = total[side][:slots] + total[side][slots:]
            for i in range(len(members)):
                of_unit = (
                    sums[:, 2 * i * unit : (2 * i + 1) * unit] + sums[:, (2 * i + 1) * unit : (2 * i + 2) * unit]
                )
                for f in range(fac):
                    here = of_unit[:, f * rows : (f + 1) * rows]
                    for zz in range(tok):
                        for s in range(sub):
                            begin = (zz * sub + s) * cap
                            left = side * lanes + lane + i * rows
                            out_ref[f, s, zz, :, left : left + rows] = here[begin : begin + cap]
        lane += len(members) * rows


def sides(counts, where_z, spot, units, spans, parts, from_below, from_above, pieces, after):
    tok, sub, fac = counts
    hops = tok - 1
    packet = from_below[0].shape[1]
    unit = from_below[0].shape[0] // GROUP
    segments = tuple((side, begin, array[0].shape[2]) for side, begin, array in pieces)
    slots = pieces[0][2][0].shape[1]
    needs = [[k for k in (0, 1) if (u < HIGH, u >= LOW)[k]] for u in units]
    used = [array for k in (0, 1) if any(k in some for some in needs) for array in parts[k]]
    width_g, width_a = parts[0][0].shape[1], parts[0][1].shape[1]
    chunks = sorted({u // GROUP for u in units})
    near = [array for c in chunks for array in from_below[c : c + hops]]
    near += [array for c in chunks for array in from_above[c : c + hops]]
    flat = [array for _, _, pair in pieces for array in pair]
    lanes = sum(len(members) for _, members in spans) * (unit // fac)
    owns = sum(len(some) for some in needs)
    many = 2 * len(units) * unit
    return pl.pallas_call(
        functools.partial(side_kernel, (units, spans, hops, segments, len(after)), counts),
        in_specs=[SCALARS, WHOLE]
        + [ANYWHERE] * len(near)
        + [IN_HBM] * (len(used) + len(flat))
        + [ANYWHERE] * len(after),
        out_specs=WHOLE,
        out_shape=jax.ShapeDtypeStruct((fac, sub, tok, slots // (tok * sub), 2 * lanes), F32),
        scratch_shapes=[
            pltpu.VMEM((owns, unit, width_g), F32),
            pltpu.VMEM((owns, unit, width_a), F32),
            pltpu.VMEM((2, len(units), unit, packet), jnp.int16),
            pltpu.VMEM((many, width_g), BF16),
            pltpu.VMEM((many, width_a), BF16),
        ]
        + [pltpu.VMEM((len(spans), 2 * slots, width), BF16) for _, _, width in segments]
        + [
            pltpu.SemaphoreType.DMA((len(units), 6)),
            pltpu.SemaphoreType.DMA((len(segments), 2 * len(spans))),
        ],
        compiler_params=params(),
        name="side_sums",
    )(where_z, spot, *near, *used, *flat, *after)


def final_kernel(groups, hops, first_ref, place_ref, slot_ref, *refs):
    out_ref = refs[-1]
    columns = [[], []]
    for i, batches in enumerate(groups):
        total = refs[i * hops][...]
        for hop in range(1, hops):
            total = total + refs[i * hops + hop][...]
        at = 0
        for runs in batches:
            lanes = sum(run for _, run in runs)
            scores = total[:, at : at + lanes] * total[:, at + lanes : at + 2 * lanes]
            scores = scores * (1.0 / math.sqrt(FH * D))
            at += 2 * lanes
            here = 0
            for klass, run in runs:
                columns[klass].append(scores[:, here : here + run])
                here += run
    cap = columns[0][0].shape[0]
    half_rows, block = out_ref.shape
    result = jnp.zeros((half_rows, block), F32)
    for klass in range(2):
        scores = jnp.concatenate(columns[klass], axis=1)
        count = scores.shape[1]
        begin = (0, LOW * (count // HIGH))[klass]
        row = lax.broadcasted_iota(I32, (count, block), 0) + begin
        of_class = (row < first_ref[0]) if klass == 0 else (row >= first_ref[0])
        to_query = ((place_ref[...] == row) & of_class).astype(F32)
        to_token = (lax.broadcasted_iota(I32, (half_rows, cap), 1) + klass * cap == slot_ref[...]).astype(F32)
        by_query = jnp.dot(scores, to_query, precision=lax.Precision.HIGHEST, preferred_element_type=F32)
        result = result + jnp.dot(
            to_token, by_query, precision=lax.Precision.HIGHEST, preferred_element_type=F32
        )
    out_ref[...] = result


def final(groups, first, place, slot, sums):
    hops = len(sums[0])
    return pl.pallas_call(
        functools.partial(final_kernel, groups, hops),
        in_specs=[SCALARS] + [WHOLE] * (2 + hops * len(sums)),
        out_specs=WHOLE,
        out_shape=jax.ShapeDtypeStruct((slot.shape[0], place.shape[1]), F32),
        compiler_params=params(),
        name="place_scores",
    )(first, place, slot, *[array for arrays in sums for array in arrays])


def body(
    activations,
    gradients,
    tok_class,
    query_inputs,
    query_gradients,
    query_class,
    basis_a,
    basis_g,
    eigen_a,
    eigen_g,
):
    deep_g, width_g = basis_g.shape[1:]
    deep_a, width_a = basis_a.shape[1:]
    counts = tok_count, sub_count, fac_count = tuple(lax.axis_size(a) for a in ("tok", "sub", "fac"))
    z, core, x = (lax.axis_index(a) for a in ("tok", "sub", "fac"))
    block = query_inputs.shape[0] // fac_count
    rows = block // CHUNKS
    tok_rows = activations.shape[0]
    half_rows = tok_rows // sub_count
    slot_cap = 5 * half_rows // 8
    share = half_rows // fac_count
    halves = tok_count * sub_count
    slots = halves * slot_cap
    token_ids = tok_class[:, 0]
    query_ids = query_class[:, 0]

    at = (core * fac_count + x) * share
    room = up_to(deep_g, TILE)
    blocks = []
    for step in range(tok_count):
        to = lax.rem(z + step, tok_count)
        blocks.append(
            jnp.concatenate(
                [
                    lax.dynamic_slice(gradients, (at, to * deep_g), (share, deep_g)),
                    jnp.zeros((share, room - deep_g), BF16),
                    lax.dynamic_slice(activations, (at, to * deep_a), (share, deep_a)),
                ],
                axis=1,
            )
        )
    moved = [blocks[0]] + [
        lax.ppermute(blocks[step], "tok", turn(tok_count, step)) for step in range(1, tok_count)
    ]

    qids = query_ids.reshape(fac_count, block)
    key = qids * block + jnp.arange(block)
    place = jnp.sum((key[:, None, :] < key[:, :, None]).astype(I32), axis=2)
    first = jnp.sum((qids == 0).astype(I32), axis=1)
    spot = (jnp.arange(CHUNKS)[:, None, None] * rows + jnp.arange(rows)) < first[None, :, None]
    spot = spot.reshape(query_ids.shape[0], 1).astype(I32)
    features = (query_gradients, query_inputs, basis_g, basis_a, fac_count, rows)
    parts = [query_coords(0, place, *features, blocks[1:]), None]

    ids = token_ids.reshape(halves, half_rows)
    earlier = jnp.arange(half_rows)[None, :] < jnp.arange(half_rows)[:, None]
    rank = jnp.sum(((ids[:, None, :] == ids[:, :, None]) & earlier).astype(I32), axis=2)
    slot = ids * slots + jnp.arange(halves)[:, None] * slot_cap + rank
    slot = slot.reshape(halves * fac_count, share)
    own_slot = lax.dynamic_index_in_dim(ids * slot_cap + rank, z * sub_count + core, 0).reshape(half_rows, 1)
    weight_g = 1.0 / (eigen_g + DAMPING)
    weight_a = 1.0 / (eigen_a + DAMPING)
    places = jnp.stack([z, core, x]).astype(I32)
    where_z = jnp.stack([z, tok_count - 1 - z]).astype(I32)

    state = {"pieces": []}

    def second(after):
        parts[1] = query_coords(1, place, *features, after)
        return parts[1][1]

    def joined(after):
        mine = join(moved, after)
        raws = [mine]
        for step in range(1, fac_count):
            raws.append(lax.ppermute(mine, "fac", turn(fac_count, step)))
        for step in range(1, sub_count):
            raws += [lax.ppermute(raw, "sub", turn(sub_count, step)) for raw in raws[:fac_count]]
        state["raws"] = raws
        return mine

    def packed(after):
        state["packed"] = pack(counts, places, slot, state["raws"], slots, deep_g, deep_a, after)
        return state["packed"][0]

    def token(side, column):
        def run(after):
            weight, basis = ((weight_g, basis_g), (weight_a, basis_a))[side]
            segment = SEGMENT if side == 0 else width_a
            pair = token_coords(state["packed"][side], weight, basis, column, segment, after)
            state["pieces"].append((side, column, pair))
            return pair[0]

        return run

    from_below, from_above = [], []
    groups, sent = [], []

    def batch(units, spans):
        def run(after):
            out = sides(
                counts, where_z, spot, units, spans, parts, from_below, from_above, state["pieces"], after
            )
            groups.append(tuple((klass, len(members) * rows) for klass, members in spans))
            sent.append(out)
            return out

        return run

    columns = list(range(0, width_g, SEGMENT))
    fillers = [[joined, second], [packed, token(1, 0)]]
    fillers += [[token(0, column)] for column in columns]
    needs = {}
    for units in (range(4), range(4, 6), range(6, 8)):
        spans = [(k, [u for u in units if (u < HIGH, u >= LOW)[k]]) for k in range(2)]
        needs[len(fillers)] = units[-1] // GROUP + tok_count - 2
        fillers.append([batch(list(units), [span for span in spans if span[1]])])

    def reduced(pieces):
        whole = pieces[0] if len(pieces) == 1 else jnp.concatenate(pieces, axis=-1)
        total = lax.dynamic_index_in_dim(whole, core, 1, keepdims=False)
        for step in range(1, sub_count):
            send = lax.dynamic_index_in_dim(whole, lax.rem(core + step, sub_count), 1, keepdims=False)
            total = total + lax.ppermute(send, "sub", turn(sub_count, step))
        whole = total
        total = lax.dynamic_index_in_dim(whole, x, 0, keepdims=False)
        for step in range(1, fac_count):
            send = lax.dynamic_index_in_dim(whole, lax.rem(x + step, fac_count), 0, keepdims=False)
            total = total + lax.ppermute(send, "fac", turn(fac_count, step))
        hops = [lax.dynamic_index_in_dim(total, z, 0, keepdims=False)]
        for step in range(1, tok_count):
            send = lax.dynamic_index_in_dim(total, lax.rem(z + step, tok_count), 0, keepdims=False)
            hops.append(lax.ppermute(send, "tok", turn(tok_count, step)))
        return hops

    up = [(i, i + 1) for i in range(tok_count - 1)]
    down = [(i + 1, i) for i in range(tok_count - 1)]
    last = tok_count - 1
    after = []
    chunks = CHUNKS // GROUP
    steps = chunks + tok_count - 2
    done = 0
    sums = []
    for step in range(steps):
        early, late = max(step - tok_count + 1, 0) * GROUP, min(step, chunks - 1) * GROUP + GROUP - 1
        wanted = [parts[0] if early < HIGH else None, parts[1] if late >= LOW else None]
        if step == 0:
            packet = stage(jnp.zeros((2,), I32), spot, [], wanted, after)
            came = lax.ppermute(packet, "tok", [(0, 1), (last, last - 1)])
            from_below.append(came)
            from_above.append(came)
            after = [packet]
        elif step == steps - 1:
            sums.append(reduced(sent[:1]))
            at = jnp.stack([jnp.int32(chunks - 1), (z < tok_count // 2).astype(I32)])
            got = [from_below[-1], from_above[-1]]
            packet = stage(at, spot, got, [None, parts[1]], after + sums[0])
            came = lax.ppermute(packet, "tok", [(last - 1, last), (1, 0)])
            from_below.append(came)
            from_above.append(came)
            after = [packet]
        else:
            for got, pairs, behind in ((from_below, up, z), (from_above, down, last - z)):
                chunk = jnp.clip(step - behind, 0, chunks - 1).astype(I32)
                at = jnp.stack([chunk, jnp.int32(0)])
                packet = stage(at, spot, got[-1:], wanted, after)
                got.append(lax.ppermute(packet, "tok", pairs))
                after = [packet]
        if step < steps - 1 and needs.get(done, -1) < step:
            for item in fillers[done]:
                after = [item(after)]
            done += 1
    for items in fillers[done:]:
        for item in items:
            after = [item(after)]
    sums.append(reduced(sent[1:]))

    own_place = lax.dynamic_index_in_dim(place, x, 0)
    own_first = lax.dynamic_index_in_dim(first, x, 0)
    return final([groups[:1], groups[1:]], own_first, own_place, own_slot, sums).T


def solution(mesh):
    placed = (
        P(("grp", "tok"), None),
        P(("grp", "tok"), None),
        P("grp", None),
        P("grp", "tok"),
        P("grp", "tok"),
        P("grp", None),
        P(None, "tok", ("fac", "sub")),
        P(None, "tok", ("fac", "sub")),
        P(None, ("fac", "sub")),
        P(None, ("fac", "sub")),
    )
    return jax.shard_map(
        body, mesh=mesh, in_specs=placed, out_specs=P("fac", ("grp", "tok", "sub")), check_vma=False
    )
```

```python
import functools
import math

import jax
import jax.numpy as jnp
from jax import lax
from jax.experimental import pallas as pl
from jax.experimental.pallas import tpu as pltpu
from jax.sharding import PartitionSpec as P

D = 5120
FH = 13824
DAMPING = 0.25
CHUNKS = 8
LOW, HIGH = 3 * CHUNKS // 8, 5 * CHUNKS // 8
LARGEST = 32760.0
TO_WHOLE = 1.5 * 2.0**23
LANES = 128
TILE = 512
SEGMENT = 4 * TILE
GROUP = 2
ROWS = 32
STAGE_MIB = 57
MIB = 1 << 20
F32 = jnp.float32
BF16 = jnp.bfloat16
I32 = jnp.int32
FINE = 8.0 / math.log(2.0)
IN_HBM = pl.BlockSpec(memory_space=pltpu.HBM)
ANYWHERE = pl.BlockSpec(memory_space=pl.ANY)
SCALARS = pl.BlockSpec(memory_space=pltpu.SMEM)
WHOLE = pl.BlockSpec(memory_space=pltpu.VMEM)


def up_to(n, m):
    return -(-n // m) * m


def params(mib=63):
    return pltpu.CompilerParams(vmem_limit_bytes=mib * MIB)


def turn(count, step):
    return [(i, (i + step) % count) for i in range(count)]


def query_kernel(fac, rows, first, tiles, place_ref, feat_g_ref, feat_a_ref, basis_g_ref, basis_a_ref, *refs):
    out_g_ref, out_a_ref, sorted_g_ref, sorted_a_ref = refs[-4:]
    block = place_ref.shape[1]
    unit = fac * rows

    def put(feat_ref, sorted_ref):
        for f in range(fac):
            spots = lax.broadcasted_iota(I32, (HIGH * rows, block), 0) + first * rows
            order = (spots == place_ref[f : f + 1, :]).astype(F32).astype(BF16)
            moved = jnp.dot(
                order, feat_ref[f * block : (f + 1) * block, :], preferred_element_type=F32
            ).astype(BF16)
            for j in range(HIGH):
                sorted_ref[j * unit + f * rows : j * unit + (f + 1) * rows, :] = moved[
                    j * rows : (j + 1) * rows, :
                ]

    step = pl.program_id(0)

    @pl.when(step == 0)
    def _():
        put(feat_g_ref, sorted_g_ref)

    @pl.when(step == tiles)
    def _():
        put(feat_a_ref, sorted_a_ref)

    @pl.when(step < tiles)
    def _():
        out_g_ref[...] = jnp.dot(sorted_g_ref[...], basis_g_ref[0], preferred_element_type=F32)

    @pl.when(step >= tiles)
    def _():
        out_a_ref[...] = jnp.dot(sorted_a_ref[...], basis_a_ref[0], preferred_element_type=F32)


def query_coords(klass, place, feat_g, feat_a, basis_g, basis_a, fac, rows, after=()):
    queries, deep_g = feat_g.shape
    deep_a = feat_a.shape[1]
    width_g, width_a = basis_g.shape[2], basis_a.shape[2]
    tile_g, tile_a = min(TILE, width_g), min(TILE, width_a)
    tiles_g, tiles_a = pl.cdiv(width_g, tile_g), pl.cdiv(width_a, tile_a)
    count = HIGH * fac * rows
    at_g = lambda i: jnp.minimum(i, tiles_g - 1)
    at_a = lambda i: jnp.maximum(i - tiles_g, 0)
    return pl.pallas_call(
        functools.partial(query_kernel, fac, rows, (0, LOW)[klass], tiles_g),
        grid=(tiles_g + tiles_a,),
        in_specs=[
            pl.BlockSpec(place.shape, lambda i: (0, 0)),
            pl.BlockSpec((queries, deep_g), lambda i: (0, 0)),
            pl.BlockSpec((queries, deep_a), lambda i: (0, 0)),
            pl.BlockSpec((1, deep_g, tile_g), lambda i: (klass, 0, at_g(i))),
            pl.BlockSpec((1, deep_a, tile_a), lambda i: (klass, 0, at_a(i))),
        ]
        + [ANYWHERE] * len(after),
        out_specs=[
            pl.BlockSpec((count, tile_g), lambda i: (0, at_g(i))),
            pl.BlockSpec((count, tile_a), lambda i: (0, at_a(i))),
        ],
        out_shape=[jax.ShapeDtypeStruct((count, width), F32) for width in (width_g, width_a)],
        scratch_shapes=[pltpu.VMEM((count, deep), BF16) for deep in (deep_g, deep_a)],
        compiler_params=params(),
        name="query_coords",
    )(place, feat_g, feat_a, basis_g, basis_a, *after)


def join_kernel(count, *refs):
    sources, out_ref, sems = refs[:count], refs[-2], refs[-1]
    size = sources[0].shape[0]
    copies = [
        pltpu.make_async_copy(ref, out_ref.at[pl.ds(i * size, size), :], sems.at[i])
        for i, ref in enumerate(sources)
    ]
    for copy in copies:
        copy.start()
    for copy in copies:
        copy.wait()


def join(blocks, after):
    size, width = blocks[0].shape
    return pl.pallas_call(
        functools.partial(join_kernel, len(blocks)),
        in_specs=[ANYWHERE] * (len(blocks) + len(after)),
        out_specs=WHOLE,
        out_shape=jax.ShapeDtypeStruct((size * len(blocks), width), BF16),
        scratch_shapes=[pltpu.SemaphoreType.DMA((len(blocks),))],
        compiler_params=params(),
        name="join_tokens",
    )(*blocks, *after)


def pack_kernel(counts, slots, room, at_ref, slot_ref, *refs):
    tok, sub, fac = counts
    raws = refs[: sub * fac]
    g_ref, a_ref, raw_ref, sems = refs[-4:]
    size = raws[0].shape[0]
    copies = [
        pltpu.make_async_copy(ref, raw_ref.at[pl.ds(i * size, size), :], sems.at[i])
        for i, ref in enumerate(raws)
    ]
    for copy in copies:
        copy.start()
    here = []
    for s in range(sub):
        for f in range(fac):
            for k in range(tok):
                row = lax.rem(at_ref[0] + tok - k, tok) * sub + lax.rem(at_ref[1] + sub - s, sub)
                row = row * fac + lax.rem(at_ref[2] + fac - f, fac)
                here.append(slot_ref[pl.ds(row, 1), :])
    here = jnp.concatenate(here, axis=1)
    for copy in copies:
        copy.wait()
    for klass in range(2):
        table = lax.broadcasted_iota(I32, (slots, here.shape[1]), 0) + klass * slots == here
        table = table.astype(F32).astype(BF16)
        for ref, begin in ((g_ref, 0), (a_ref, room)):
            ref[klass] = jnp.dot(
                table, raw_ref[:, begin : begin + ref.shape[2]], preferred_element_type=F32
            ).astype(BF16)


def pack(counts, at, slot, raws, slots, deep_g, deep_a, after):
    size, width = raws[0].shape
    return pl.pallas_call(
        functools.partial(pack_kernel, counts, slots, up_to(deep_g, LANES)),
        in_specs=[SCALARS, WHOLE] + [ANYWHERE] * (len(raws) + len(after)),
        out_specs=[WHOLE, WHOLE],
        out_shape=[jax.ShapeDtypeStruct((2, slots, deep), BF16) for deep in (deep_g, deep_a)],
        scratch_shapes=[
            pltpu.VMEM((size * len(raws), width), BF16),
            pltpu.SemaphoreType.DMA((len(raws),)),
        ],
        compiler_params=params(),
        name="pack_tokens",
    )(at, slot, *raws, *after)


def token_kernel(packed_ref, weight_ref, basis_ref, *refs):
    high_ref, low_ref = refs[-2:]
    for klass in range(2):
        coords = (
            jnp.dot(packed_ref[klass], basis_ref[klass], preferred_element_type=F32)
            * weight_ref[klass : klass + 1, :]
        )
        high = coords.astype(BF16)
        high_ref[klass] = high
        low_ref[klass] = (coords - high.astype(F32)).astype(BF16)


def token_coords(packed, weight, basis, column, segment, after):
    slots = packed.shape[1]
    deep, width = basis.shape[1:]
    here = min(segment, width - column)
    tile = min(TILE, width)
    base = column // tile
    out = jax.ShapeDtypeStruct((2, slots, here), BF16)
    return pl.pallas_call(
        token_kernel,
        grid=(pl.cdiv(here, tile),),
        in_specs=[
            pl.BlockSpec((2, slots, deep), lambda i: (0, 0, 0)),
            pl.BlockSpec((2, tile), lambda i: (0, base + i)),
            pl.BlockSpec((2, deep, tile), lambda i: (0, 0, base + i)),
        ]
        + [ANYWHERE] * len(after),
        out_specs=[pl.BlockSpec((2, slots, tile), lambda i: (0, 0, i))] * 2,
        out_shape=[out, out],
        compiler_params=params(),
        name="token_coords",
    )(packed, weight, basis, *after)


def tiles_of(width):
    return [(begin, min(LANES, width - begin)) for begin in range(0, width, LANES)]


def scaled(x):
    top = jnp.max(jnp.abs(x), axis=1, keepdims=True)
    code = jnp.ceil(jnp.log(jnp.maximum(top, 1e-30)) * FINE)
    factor = LARGEST * jnp.exp(code * (-1.0 / FINE))
    return (x * factor + TO_WHOLE) - TO_WHOLE, code


def narrow(x):
    return x.astype(I32).astype(jnp.int16)


def wide(x):
    return x.astype(I32).astype(F32)


def steps_of(ref, tail):
    step = jnp.exp(wide(ref[:, tail : tail + LANES]) * (1.0 / FINE)) * (1.0 / LARGEST)
    shape = step.shape
    return (
        jnp.broadcast_to(step[:, 0:1], shape),
        jnp.broadcast_to(step[:, LANES - 1 : LANES], shape),
    )


def stage_kernel(row_at, gots, parts, after, at_ref, spot_ref, *refs):
    sources, refs = refs[:gots], refs[gots:]
    use = [k for k in range(2) if parts[k]]
    part = {k: (refs[2 * i], refs[2 * i + 1]) for i, k in enumerate(use)}
    refs = refs[2 * len(use) + after :]
    out_ref, refs = refs[0], refs[1:]
    held = {k: (refs[2 * i], refs[2 * i + 1]) for i, k in enumerate(use)}
    got_ref, made_ref, sems = refs[2 * len(use) :]
    chunk, which = at_ref[row_at], at_ref[row_at + 1]
    size = ROWS
    blocks = out_ref.shape[0] // size
    per_unit = blocks // GROUP
    width_g, width_a = (ref.shape[1] for ref in part[use[0]])
    room = up_to(width_g, LANES)
    tail = room + up_to(width_a, LANES)

    def received(b, source):
        at = pl.ds(b * size, size)
        return pltpu.make_async_copy(source.at[at, :], got_ref.at[at, :], sems.at[b, 4])

    def each(b, act, first):
        if gots == 1 or (gots and not first):
            act(received(b, sources[0]))
        elif gots:
            for i in range(2):

                @pl.when(which == i)
                def _():
                    act(received(b, sources[i]))

        unit = chunk * GROUP + b // per_unit
        for k in use:
            row = pl.multiple_of(((unit - (0, LOW)[k]) * per_unit + b % per_unit) * size, size)

            def go():
                for side in range(2):
                    act(
                        pltpu.make_async_copy(
                            part[k][side].at[pl.ds(row, size), :],
                            held[k][side].at[pl.ds(b * size, size), :],
                            sems.at[b, 2 * k + side],
                        )
                    )

            if len(use) == 1:
                go()
            else:
                pl.when((unit < HIGH) if k == 0 else (unit >= LOW))(go)

    def sent(b):
        at = pl.ds(b * size, size)
        return pltpu.make_async_copy(made_ref.at[at, :], out_ref.at[at, :], sems.at[b, 5])

    for b in range(blocks):
        each(b, lambda copy: copy.start(), True)
    for b in range(blocks):
        each(b, lambda copy: copy.wait(), False)
        at = slice(b * size, (b + 1) * size)
        if len(use) == 1:
            x_g, x_a = (ref[at, :] for ref in held[use[0]])
        else:
            of_zero = spot_ref[at, :] > 0
            x_g, x_a = (jnp.where(of_zero, held[0][i][at, :], held[1][i][at, :]) for i in range(2))
        if gots:
            step = jnp.exp(wide(got_ref[at, tail : tail + LANES]) * (1.0 / FINE)) * (1.0 / LARGEST)
            x_g = x_g + wide(got_ref[at, :width_g]) * step[:, 0:1]
            x_a = x_a + wide(got_ref[at, room : room + width_a]) * step[:, LANES - 1 : LANES]
        q_g, code_g = scaled(x_g)
        q_a, code_a = scaled(x_a)
        if room != width_g or tail != room + width_a:
            made_ref[at, :] = jnp.zeros((size, made_ref.shape[1]), jnp.int16)
        made_ref[at, :width_g] = narrow(q_g)
        made_ref[at, room : room + width_a] = narrow(q_a)
        lane = lax.broadcasted_iota(I32, (size, LANES), 1)
        made_ref[at, tail:] = narrow(jnp.where(lane < LANES // 2, code_g, code_a))
        sent(b).start()
    for b in range(blocks):
        sent(b).wait()


def stage(table, number, spot, got, parts, after):
    use = [part for part in parts if part is not None]
    width_g, width_a = use[0][0].shape[1], use[0][1].shape[1]
    unit = use[0][0].shape[0] // HIGH * GROUP
    packet = up_to(width_g, LANES) + up_to(width_a, LANES) + LANES
    flat = [array for part in use for array in part]
    row_at = 2 * number
    return pl.pallas_call(
        functools.partial(
            stage_kernel, row_at, len(got), tuple(part is not None for part in parts), len(after)
        ),
        grid_spec=pltpu.PrefetchScalarGridSpec(
            num_scalar_prefetch=1,
            grid=(1,),
            in_specs=[pl.BlockSpec((unit, 1), lambda i, c: (c[row_at], 0))]
            + [ANYWHERE] * len(got)
            + [IN_HBM] * len(flat)
            + [ANYWHERE] * len(after),
            out_specs=ANYWHERE,
            scratch_shapes=[pltpu.VMEM((unit, array.shape[1]), F32) for array in flat]
            + [pltpu.VMEM((unit, packet), jnp.int16)] * 2
            + [pltpu.SemaphoreType.DMA((unit // ROWS, 6))],
        ),
        out_shape=jax.ShapeDtypeStruct((unit, packet), jnp.int16),
        compiler_params=params(STAGE_MIB),
        name="running_sum",
    )(table, spot, *got, *flat, *after)


def side_kernel(plan, counts, z_ref, spot_ref, *refs):
    units, spans, hops, segments, after = plan
    tok, sub, fac = counts
    refs = list(refs)

    def take(n):
        out, refs[:n] = refs[:n], []
        return out

    chunks = sorted({u // GROUP for u in units})
    below = {c: take(hops) for c in chunks}
    above = {c: take(hops) for c in chunks}
    needs = {u: [k for k in (0, 1) if (u < HIGH, u >= LOW)[k]] for u in units}
    part = {k: take(2) for k in (0, 1) if any(k in needs[u] for u in units)}
    pieces = [take(2) for _ in segments]
    take(after)
    out_ref = take(1)[0]
    held_g, held_a, got, x_g, x_a = take(5)
    tables = take(len(segments))
    sems, piece_sems = take(2)
    held = (held_g, held_a)
    width_g, width_a = x_g.shape[1], x_a.shape[1]
    unit = got.shape[2]
    rows = unit // fac
    slots = pieces[0][0].shape[1]
    cap = slots // (tok * sub)
    room = up_to(width_g, LANES)
    tail = room + up_to(width_a, LANES)
    lanes = out_ref.shape[-1] // 2
    spot_of = {}
    for u in units:
        for k in needs[u]:
            spot_of[u, k] = len(spot_of)

    def own(i, u):
        return [
            pltpu.make_async_copy(
                part[k][side].at[pl.ds((u - (0, LOW)[k]) * unit, unit), :],
                held[side].at[spot_of[u, k]],
                sems.at[i, 2 * k + side],
            )
            for k in needs[u]
            for side in range(2)
        ]

    def arrived(i, u, way, hop):
        source = (below, above)[way][u // GROUP][hop]
        return pltpu.make_async_copy(
            source.at[pl.ds(u % GROUP * unit, unit), :], got.at[way, i], sems.at[i, 4 + way]
        )

    for i, u in enumerate(units):
        for copy in own(i, u):
            copy.start()
        for way in range(2):
            for hop in range(hops):
                cut = (z_ref[way] <= 1) if hop == 0 else (z_ref[way] == hop + 1)

                @pl.when(cut)
                def _():
                    arrived(i, u, way, hop).start()

    copies = [
        pltpu.make_async_copy(
            pieces[s][half].at[klass],
            tables[s].at[c, pl.ds(half * slots, slots), :],
            piece_sems.at[s, 2 * c + half],
        )
        for c, (klass, _) in enumerate(spans)
        for s in range(len(segments))
        for half in range(2)
    ]
    for copy in copies:
        copy.start()
    for i, u in enumerate(units):
        for copy in own(i, u):
            copy.wait()
        for way in range(2):
            arrived(i, u, way, 0).wait()
        below_steps, above_steps = (steps_of(got.at[way, i], tail) for way in range(2))
        if len(needs[u]) == 2:
            of_zero = jnp.broadcast_to(spot_ref[u * unit : (u + 1) * unit, :], (unit, LANES)) > 0
        for side, (ref, own_ref) in enumerate(((x_g, held_g), (x_a, held_a))):
            for begin, wide_by in tiles_of(ref.shape[1]):
                cut = slice(begin, begin + wide_by)
                there = slice((0, room)[side] + begin, (0, room)[side] + begin + wide_by)
                full = own_ref[spot_of[u, needs[u][0]], :, cut]
                if len(needs[u]) == 2:
                    full = jnp.where(of_zero[:, :wide_by], full, own_ref[spot_of[u, 1], :, cut])
                full = full + wide(got[0, i, :, there]) * below_steps[side][:, :wide_by]
                full = full + wide(got[1, i, :, there]) * above_steps[side][:, :wide_by]
                high = full.astype(BF16)
                ref[2 * i * unit : (2 * i + 1) * unit, cut] = high
                ref[(2 * i + 1) * unit : (2 * i + 2) * unit, cut] = (full - high.astype(F32)).astype(BF16)

    for copy in copies:
        copy.wait()
    dims = (((1,), (1,)), ((), ()))
    lane = 0
    for c, (klass, members) in enumerate(spans):
        first = units.index(members[0])
        span = slice(2 * first * unit, 2 * (first + len(members)) * unit)
        total = [None, None]
        for s, (side, begin, width) in enumerate(segments):
            x = (x_g, x_a)[side]
            term = lax.dot_general(
                tables[s][c], x[span, begin : begin + width], dims, preferred_element_type=F32
            )
            total[side] = term if total[side] is None else total[side] + term
        for side in range(2):
            sums = total[side][:slots] + total[side][slots:]
            for i in range(len(members)):
                of_unit = (
                    sums[:, 2 * i * unit : (2 * i + 1) * unit] + sums[:, (2 * i + 1) * unit : (2 * i + 2) * unit]
                )
                for f in range(fac):
                    here = of_unit[:, f * rows : (f + 1) * rows]
                    for zz in range(tok):
                        for s in range(sub):
                            begin = (zz * sub + s) * cap
                            left = side * lanes + lane + i * rows
                            out_ref[f, s, zz, :, left : left + rows] = here[begin : begin + cap]
        lane += len(members) * rows


def sides(counts, where_z, spot, units, spans, parts, from_below, from_above, pieces, after):
    tok, sub, fac = counts
    hops = tok - 1
    packet = from_below[0].shape[1]
    unit = from_below[0].shape[0] // GROUP
    segments = tuple((side, begin, array[0].shape[2]) for side, begin, array in pieces)
    slots = pieces[0][2][0].shape[1]
    needs = [[k for k in (0, 1) if (u < HIGH, u >= LOW)[k]] for u in units]
    used = [array for k in (0, 1) if any(k in some for some in needs) for array in parts[k]]
    width_g, width_a = parts[0][0].shape[1], parts[0][1].shape[1]
    chunks = sorted({u // GROUP for u in units})
    near = [array for c in chunks for array in from_below[c : c + hops]]
    near += [array for c in chunks for array in from_above[c : c + hops]]
    flat = [array for _, _, pair in pieces for array in pair]
    lanes = sum(len(members) for _, members in spans) * (unit // fac)
    owns = sum(len(some) for some in needs)
    many = 2 * len(units) * unit
    return pl.pallas_call(
        functools.partial(side_kernel, (units, spans, hops, segments, len(after)), counts),
        in_specs=[SCALARS, WHOLE]
        + [ANYWHERE] * len(near)
        + [IN_HBM] * (len(used) + len(flat))
        + [ANYWHERE] * len(after),
        out_specs=WHOLE,
        out_shape=jax.ShapeDtypeStruct((fac, sub, tok, slots // (tok * sub), 2 * lanes), F32),
        scratch_shapes=[
            pltpu.VMEM((owns, unit, width_g), F32),
            pltpu.VMEM((owns, unit, width_a), F32),
            pltpu.VMEM((2, len(units), unit, packet), jnp.int16),
            pltpu.VMEM((many, width_g), BF16),
            pltpu.VMEM((many, width_a), BF16),
        ]
        + [pltpu.VMEM((len(spans), 2 * slots, width), BF16) for _, _, width in segments]
        + [
            pltpu.SemaphoreType.DMA((len(units), 6)),
            pltpu.SemaphoreType.DMA((len(segments), 2 * len(spans))),
        ],
        compiler_params=params(),
        name="side_sums",
    )(where_z, spot, *near, *used, *flat, *after)


def final_kernel(groups, hops, first_ref, place_ref, slot_ref, *refs):
    out_ref = refs[-1]
    columns = [[], []]
    for i, batches in enumerate(groups):
        total = refs[i * hops][...]
        for hop in range(1, hops):
            total = total + refs[i * hops + hop][...]
        at = 0
        for runs in batches:
            lanes = sum(run for _, run in runs)
            scores = total[:, at : at + lanes] * total[:, at + lanes : at + 2 * lanes]
            scores = scores * (1.0 / math.sqrt(FH * D))
            at += 2 * lanes
            here = 0
            for klass, run in runs:
                columns[klass].append(scores[:, here : here + run])
                here += run
    cap = columns[0][0].shape[0]
    half_rows, block = out_ref.shape
    result = jnp.zeros((half_rows, block), F32)
    for klass in range(2):
        scores = jnp.concatenate(columns[klass], axis=1)
        count = scores.shape[1]
        begin = (0, LOW * (count // HIGH))[klass]
        row = lax.broadcasted_iota(I32, (count, block), 0) + begin
        of_class = (row < first_ref[0]) if klass == 0 else (row >= first_ref[0])
        to_query = ((place_ref[...] == row) & of_class).astype(F32)
        to_token = (lax.broadcasted_iota(I32, (half_rows, cap), 1) + klass * cap == slot_ref[...]).astype(F32)
        by_query = jnp.dot(scores, to_query, precision=lax.Precision.HIGHEST, preferred_element_type=F32)
        result = result + jnp.dot(
            to_token, by_query, precision=lax.Precision.HIGHEST, preferred_element_type=F32
        )
    out_ref[...] = result


def final(groups, first, place, slot, sums):
    hops = len(sums[0])
    return pl.pallas_call(
        functools.partial(final_kernel, groups, hops),
        in_specs=[SCALARS] + [WHOLE] * (2 + hops * len(sums)),
        out_specs=WHOLE,
        out_shape=jax.ShapeDtypeStruct((slot.shape[0], place.shape[1]), F32),
        compiler_params=params(),
        name="place_scores",
    )(first, place, slot, *[array for arrays in sums for array in arrays])


def body(
    activations,
    gradients,
    tok_class,
    query_inputs,
    query_gradients,
    query_class,
    basis_a,
    basis_g,
    eigen_a,
    eigen_g,
):
    deep_g, width_g = basis_g.shape[1:]
    deep_a, width_a = basis_a.shape[1:]
    counts = tok_count, sub_count, fac_count = tuple(lax.axis_size(a) for a in ("tok", "sub", "fac"))
    z, core, x = (lax.axis_index(a) for a in ("tok", "sub", "fac"))
    block = query_inputs.shape[0] // fac_count
    rows = block // CHUNKS
    tok_rows = activations.shape[0]
    half_rows = tok_rows // sub_count
    slot_cap = 5 * half_rows // 8
    share = half_rows // fac_count
    halves = tok_count * sub_count
    slots = halves * slot_cap
    token_ids = tok_class[:, 0]
    query_ids = query_class[:, 0]

    at = (core * fac_count + x) * share
    room = up_to(deep_g, LANES)
    blocks = []
    for step in range(tok_count):
        to = lax.rem(z + step, tok_count)
        blocks.append(
            jnp.concatenate(
                [
                    lax.dynamic_slice(gradients, (at, to * deep_g), (share, deep_g)),
                    jnp.zeros((share, room - deep_g), BF16),
                    lax.dynamic_slice(activations, (at, to * deep_a), (share, deep_a)),
                ],
                axis=1,
            )
        )
    moved = [blocks[0]] + [
        lax.ppermute(blocks[step], "tok", turn(tok_count, step)) for step in range(1, tok_count)
    ]

    qids = query_ids.reshape(fac_count, block)
    key = qids * block + jnp.arange(block)
    place = jnp.sum((key[:, None, :] < key[:, :, None]).astype(I32), axis=2)
    first = jnp.sum((qids == 0).astype(I32), axis=1)
    spot = (jnp.arange(CHUNKS)[:, None, None] * rows + jnp.arange(rows)) < first[None, :, None]
    spot = spot.reshape(query_ids.shape[0], 1).astype(I32)
    features = (query_gradients, query_inputs, basis_g, basis_a, fac_count, rows)
    parts = [query_coords(0, place, *features, blocks[1:]), None]

    ids = token_ids.reshape(halves, half_rows)
    earlier = jnp.arange(half_rows)[None, :] < jnp.arange(half_rows)[:, None]
    rank = jnp.sum(((ids[:, None, :] == ids[:, :, None]) & earlier).astype(I32), axis=2)
    slot = ids * slots + jnp.arange(halves)[:, None] * slot_cap + rank
    slot = slot.reshape(halves * fac_count, share)
    own_slot = lax.dynamic_index_in_dim(ids * slot_cap + rank, z * sub_count + core, 0).reshape(half_rows, 1)
    weight_g = 1.0 / (eigen_g + DAMPING)
    weight_a = 1.0 / (eigen_a + DAMPING)
    places = jnp.stack([z, core, x]).astype(I32)
    where_z = jnp.stack([z, tok_count - 1 - z]).astype(I32)

    state = {"pieces": []}

    def second(after):
        parts[1] = query_coords(1, place, *features, after)
        return parts[1][1]

    def joined(after):
        mine = join(moved, after)
        raws = [mine]
        for step in range(1, fac_count):
            raws.append(lax.ppermute(mine, "fac", turn(fac_count, step)))
        for step in range(1, sub_count):
            raws += [lax.ppermute(raw, "sub", turn(sub_count, step)) for raw in raws[:fac_count]]
        state["raws"] = raws
        return mine

    def packed(after):
        state["packed"] = pack(counts, places, slot, state["raws"], slots, deep_g, deep_a, after)
        return state["packed"][0]

    def token(side, column):
        def run(after):
            weight, basis = ((weight_g, basis_g), (weight_a, basis_a))[side]
            segment = SEGMENT if side == 0 else width_a
            pair = token_coords(state["packed"][side], weight, basis, column, segment, after)
            state["pieces"].append((side, column, pair))
            return pair[0]

        return run

    from_below, from_above = [], []
    groups, sent = [], []

    def batch(units, spans):
        def run(after):
            out = sides(
                counts, where_z, spot, units, spans, parts, from_below, from_above, state["pieces"], after
            )
            groups.append(tuple((klass, len(members) * rows) for klass, members in spans))
            sent.append(out)
            return out

        return run

    columns = list(range(0, width_g, SEGMENT))
    fillers = [[joined, second], [packed, token(1, 0)]]
    fillers += [[token(0, column)] for column in columns]
    needs = {}
    for units in (range(4), range(4, 6), range(6, 8)):
        spans = [(k, [u for u in units if (u < HIGH, u >= LOW)[k]]) for k in range(2)]
        needs[len(fillers)] = units[-1] // GROUP + tok_count - 2
        fillers.append([batch(list(units), [span for span in spans if span[1]])])

    def reduced(pieces):
        whole = pieces[0] if len(pieces) == 1 else jnp.concatenate(pieces, axis=-1)
        total = lax.dynamic_index_in_dim(whole, core, 1, keepdims=False)
        for step in range(1, sub_count):
            send = lax.dynamic_index_in_dim(whole, lax.rem(core + step, sub_count), 1, keepdims=False)
            total = total + lax.ppermute(send, "sub", turn(sub_count, step))
        whole = total
        total = lax.dynamic_index_in_dim(whole, x, 0, keepdims=False)
        for step in range(1, fac_count):
            send = lax.dynamic_index_in_dim(whole, lax.rem(x + step, fac_count), 0, keepdims=False)
            total = total + lax.ppermute(send, "fac", turn(fac_count, step))
        hops = [lax.dynamic_index_in_dim(total, z, 0, keepdims=False)]
        for step in range(1, tok_count):
            send = lax.dynamic_index_in_dim(total, lax.rem(z + step, tok_count), 0, keepdims=False)
            hops.append(lax.ppermute(send, "tok", turn(tok_count, step)))
        return hops

    up = [(i, i + 1) for i in range(tok_count - 1)]
    down = [(i + 1, i) for i in range(tok_count - 1)]
    last = tok_count - 1
    after = []
    chunks = CHUNKS // GROUP
    steps = chunks + tok_count - 2
    done = 0
    low_half = z < tok_count // 2
    low_flag = low_half.astype(I32)
    behinds = (z, last - z)
    near_end = jnp.minimum(z, last - z)
    table = []
    for step in range(steps):
        if step < 2:
            table += [jnp.clip(step - near_end, 0, chunks - 1), jnp.int32(0)] * 2
        elif step == steps - 1:
            table += [jnp.int32(chunks - 1), low_flag] * 2
        else:
            for behind in behinds:
                table += [jnp.clip(step - behind, 0, chunks - 1), jnp.int32(0)]
    table = jnp.stack([jnp.asarray(entry).astype(I32) for entry in table])
    for step in range(steps):
        early, late = max(step - tok_count + 1, 0) * GROUP, min(step, chunks - 1) * GROUP + GROUP - 1
        wanted = [parts[0] if early < HIGH else None, parts[1] if late >= LOW else None]
        if step == 0:
            packet = stage(table, 0, spot, [], wanted, after)
            came = lax.ppermute(packet, "tok", [(0, 1), (last, last - 1)])
            from_below.append(came)
            from_above.append(came)
            after = [packet]
        elif step == 1:
            packet = stage(table, 2, spot, [from_below[-1]], wanted, after)
            from_below.append(lax.ppermute(packet, "tok", up[:2]))
            from_above.append(lax.ppermute(packet, "tok", down[-2:]))
            after = [packet]
        elif step == steps - 1:
            got = [from_below[-1], from_above[-1]]
            packet = stage(table, 2 * step, spot, got, [None, parts[1]], after)
            came = lax.ppermute(packet, "tok", [(last - 1, last), (1, 0)])
            from_below.append(came)
            from_above.append(came)
            after = [packet]
        else:
            for way, (got, pairs) in enumerate(((from_below, up), (from_above, down))):
                packet = stage(table, 2 * step + way, spot, got[-1:], wanted, after)
                got.append(lax.ppermute(packet, "tok", pairs))
                after = [packet]
        if step < steps - 1 and needs.get(done, -1) < step:
            for item in fillers[done]:
                after = [item(after)]
            done += 1
    for items in fillers[done:]:
        for item in items:
            after = [item(after)]
    sums = [reduced(sent)]

    own_place = lax.dynamic_index_in_dim(place, x, 0)
    own_first = lax.dynamic_index_in_dim(first, x, 0)
    return final([groups], own_first, own_place, own_slot, sums).T


def solution(mesh):
    placed = (
        P(("grp", "tok"), None),
        P(("grp", "tok"), None),
        P("grp", None),
        P("grp", "tok"),
        P("grp", "tok"),
        P("grp", None),
        P(None, "tok", ("fac", "sub")),
        P(None, "tok", ("fac", "sub")),
        P(None, ("fac", "sub")),
        P(None, ("fac", "sub")),
    )
    return jax.shard_map(
        body, mesh=mesh, in_specs=placed, out_specs=P("fac", ("grp", "tok", "sub")), check_vma=False
    )
```

```python
import functools
import math

import jax
import jax.numpy as jnp
from jax import lax
from jax.experimental import pallas as pl
from jax.experimental.pallas import tpu as pltpu
from jax.sharding import PartitionSpec as P

D = 5120
FH = 13824
DAMPING = 0.25
CHUNKS = 8
LOW, HIGH = 3 * CHUNKS // 8, 5 * CHUNKS // 8
LARGEST = 32760.0
TO_WHOLE = 1.5 * 2.0**23
LANES = 128
TILE = 512
SEGMENT = 4 * TILE
GROUP = 2
ROWS = 64
STAGE_MIB = 57
MIB = 1 << 20
F32 = jnp.float32
BF16 = jnp.bfloat16
I32 = jnp.int32
FINE = 8.0 / math.log(2.0)
IN_HBM = pl.BlockSpec(memory_space=pltpu.HBM)
ANYWHERE = pl.BlockSpec(memory_space=pl.ANY)
SCALARS = pl.BlockSpec(memory_space=pltpu.SMEM)
WHOLE = pl.BlockSpec(memory_space=pltpu.VMEM)


def up_to(n, m):
    return -(-n // m) * m


def params(mib=63):
    return pltpu.CompilerParams(vmem_limit_bytes=mib * MIB)


def turn(count, step):
    return [(i, (i + step) % count) for i in range(count)]


def query_kernel(fac, rows, first, tiles, place_ref, feat_g_ref, feat_a_ref, basis_g_ref, basis_a_ref, *refs):
    out_g_ref, out_a_ref, sorted_g_ref, sorted_a_ref = refs[-4:]
    block = place_ref.shape[1]
    unit = fac * rows

    def put(feat_ref, sorted_ref):
        for f in range(fac):
            spots = lax.broadcasted_iota(I32, (HIGH * rows, block), 0) + first * rows
            order = (spots == place_ref[f : f + 1, :]).astype(F32).astype(BF16)
            moved = jnp.dot(
                order, feat_ref[f * block : (f + 1) * block, :], preferred_element_type=F32
            ).astype(BF16)
            for j in range(HIGH):
                sorted_ref[j * unit + f * rows : j * unit + (f + 1) * rows, :] = moved[
                    j * rows : (j + 1) * rows, :
                ]

    step = pl.program_id(0)

    @pl.when(step == 0)
    def _():
        put(feat_g_ref, sorted_g_ref)

    @pl.when(step == tiles)
    def _():
        put(feat_a_ref, sorted_a_ref)

    @pl.when(step < tiles)
    def _():
        out_g_ref[...] = jnp.dot(sorted_g_ref[...], basis_g_ref[0], preferred_element_type=F32)

    @pl.when(step >= tiles)
    def _():
        out_a_ref[...] = jnp.dot(sorted_a_ref[...], basis_a_ref[0], preferred_element_type=F32)


def query_coords(klass, place, feat_g, feat_a, basis_g, basis_a, fac, rows, after=()):
    queries, deep_g = feat_g.shape
    deep_a = feat_a.shape[1]
    width_g, width_a = basis_g.shape[2], basis_a.shape[2]
    tile_g, tile_a = min(TILE, width_g), min(TILE, width_a)
    tiles_g, tiles_a = pl.cdiv(width_g, tile_g), pl.cdiv(width_a, tile_a)
    count = HIGH * fac * rows
    at_g = lambda i: jnp.minimum(i, tiles_g - 1)
    at_a = lambda i: jnp.maximum(i - tiles_g, 0)
    return pl.pallas_call(
        functools.partial(query_kernel, fac, rows, (0, LOW)[klass], tiles_g),
        grid=(tiles_g + tiles_a,),
        in_specs=[
            pl.BlockSpec(place.shape, lambda i: (0, 0)),
            pl.BlockSpec((queries, deep_g), lambda i: (0, 0)),
            pl.BlockSpec((queries, deep_a), lambda i: (0, 0)),
            pl.BlockSpec((1, deep_g, tile_g), lambda i: (klass, 0, at_g(i))),
            pl.BlockSpec((1, deep_a, tile_a), lambda i: (klass, 0, at_a(i))),
        ]
        + [ANYWHERE] * len(after),
        out_specs=[
            pl.BlockSpec((count, tile_g), lambda i: (0, at_g(i))),
            pl.BlockSpec((count, tile_a), lambda i: (0, at_a(i))),
        ],
        out_shape=[jax.ShapeDtypeStruct((count, width), F32) for width in (width_g, width_a)],
        scratch_shapes=[pltpu.VMEM((count, deep), BF16) for deep in (deep_g, deep_a)],
        compiler_params=params(),
        name="query_coords",
    )(place, feat_g, feat_a, basis_g, basis_a, *after)


def join_kernel(count, *refs):
    sources, out_ref, sems = refs[:count], refs[-2], refs[-1]
    size = sources[0].shape[0]
    copies = [
        pltpu.make_async_copy(ref, out_ref.at[pl.ds(i * size, size), :], sems.at[i])
        for i, ref in enumerate(sources)
    ]
    for copy in copies:
        copy.start()
    for copy in copies:
        copy.wait()


def join(blocks, after):
    size, width = blocks[0].shape
    return pl.pallas_call(
        functools.partial(join_kernel, len(blocks)),
        in_specs=[ANYWHERE] * (len(blocks) + len(after)),
        out_specs=WHOLE,
        out_shape=jax.ShapeDtypeStruct((size * len(blocks), width), BF16),
        scratch_shapes=[pltpu.SemaphoreType.DMA((len(blocks),))],
        compiler_params=params(),
        name="join_tokens",
    )(*blocks, *after)


def pack_kernel(counts, slots, room, at_ref, slot_ref, *refs):
    tok, sub, fac = counts
    raws = refs[: sub * fac]
    g_ref, a_ref, made_g, made_a, raw_ref, sems, out_sems = refs[-7:]
    size = raws[0].shape[0]
    copies = [
        pltpu.make_async_copy(ref, raw_ref.at[pl.ds(i * size, size), :], sems.at[i])
        for i, ref in enumerate(raws)
    ]
    for copy in copies:
        copy.start()
    here = []
    for s in range(sub):
        for f in range(fac):
            for k in range(tok):
                row = lax.rem(at_ref[0] + tok - k, tok) * sub + lax.rem(at_ref[1] + sub - s, sub)
                row = row * fac + lax.rem(at_ref[2] + fac - f, fac)
                here.append(slot_ref[pl.ds(row, 1), :])
    here = jnp.concatenate(here, axis=1)
    for copy in copies:
        copy.wait()
    outs = []
    for klass in range(2):
        table = lax.broadcasted_iota(I32, (slots, here.shape[1]), 0) + klass * slots == here
        table = table.astype(F32).astype(BF16)
        for side, (ref, made, begin) in enumerate(((g_ref, made_g, 0), (a_ref, made_a, room))):
            made[klass] = jnp.dot(
                table, raw_ref[:, begin : begin + ref.shape[2]], preferred_element_type=F32
            ).astype(BF16)
            out = pltpu.make_async_copy(made.at[klass], ref.at[klass], out_sems.at[klass, side])
            out.start()
            outs.append(out)
    for out in outs:
        out.wait()


def pack(counts, at, slot, raws, slots, deep_g, deep_a, after):
    size, width = raws[0].shape
    return pl.pallas_call(
        functools.partial(pack_kernel, counts, slots, up_to(deep_g, LANES)),
        in_specs=[SCALARS, WHOLE] + [ANYWHERE] * (len(raws) + len(after)),
        out_specs=[ANYWHERE, ANYWHERE],
        out_shape=[jax.ShapeDtypeStruct((2, slots, deep), BF16) for deep in (deep_g, deep_a)],
        scratch_shapes=[
            pltpu.VMEM((2, slots, deep_g), BF16),
            pltpu.VMEM((2, slots, deep_a), BF16),
            pltpu.VMEM((size * len(raws), width), BF16),
            pltpu.SemaphoreType.DMA((len(raws),)),
            pltpu.SemaphoreType.DMA((2, 2)),
        ],
        compiler_params=params(),
        name="pack_tokens",
    )(at, slot, *raws, *after)


def token_kernel(packed_ref, eigen_ref, basis_ref, *refs):
    high_ref, low_ref = refs[-2:]
    for klass in range(2):
        coords = (
            jnp.dot(packed_ref[klass], basis_ref[klass], preferred_element_type=F32)
            / (eigen_ref[klass : klass + 1, :] + DAMPING)
        )
        high = coords.astype(BF16)
        high_ref[klass] = high
        low_ref[klass] = (coords - high.astype(F32)).astype(BF16)


def token_coords(packed, eigen, basis, column, segment, after):
    slots = packed.shape[1]
    deep, width = basis.shape[1:]
    here = min(segment, width - column)
    tile = min(TILE, width)
    base = column // tile
    out = jax.ShapeDtypeStruct((2, slots, here), BF16)
    return pl.pallas_call(
        token_kernel,
        grid=(pl.cdiv(here, tile),),
        in_specs=[
            pl.BlockSpec((2, slots, deep), lambda i: (0, 0, 0)),
            pl.BlockSpec((2, tile), lambda i: (0, base + i)),
            pl.BlockSpec((2, deep, tile), lambda i: (0, 0, base + i)),
        ]
        + [ANYWHERE] * len(after),
        out_specs=[pl.BlockSpec((2, slots, tile), lambda i: (0, 0, i))] * 2,
        out_shape=[out, out],
        compiler_params=params(),
        name="token_coords",
    )(packed, eigen, basis, *after)


def tiles_of(width):
    return [(begin, min(LANES, width - begin)) for begin in range(0, width, LANES)]


def scaled(x):
    top = jnp.max(jnp.abs(x), axis=1, keepdims=True)
    code = jnp.ceil(jnp.log(jnp.maximum(top, 1e-30)) * FINE)
    factor = LARGEST * jnp.exp(code * (-1.0 / FINE))
    return (x * factor + TO_WHOLE) - TO_WHOLE, code


def narrow(x):
    return x.astype(I32).astype(jnp.int16)


def wide(x):
    return x.astype(I32).astype(F32)


def steps_of(ref, tail):
    step = jnp.exp(wide(ref[:, tail : tail + LANES]) * (1.0 / FINE)) * (1.0 / LARGEST)
    shape = step.shape
    return (
        jnp.broadcast_to(step[:, 0:1], shape),
        jnp.broadcast_to(step[:, LANES - 1 : LANES], shape),
    )


def stage_kernel(row_at, gots, parts, after, at_ref, spot_ref, *refs):
    sources, refs = refs[:gots], refs[gots:]
    use = [k for k in range(2) if parts[k]]
    part = {k: (refs[2 * i], refs[2 * i + 1]) for i, k in enumerate(use)}
    refs = refs[2 * len(use) + after :]
    out_ref, refs = refs[0], refs[1:]
    held = {k: (refs[2 * i], refs[2 * i + 1]) for i, k in enumerate(use)}
    got_ref, made_ref, sems = refs[2 * len(use) :]
    chunk, which = at_ref[row_at], at_ref[row_at + 1]
    size = ROWS
    blocks = out_ref.shape[0] // size
    per_unit = blocks // GROUP
    width_g, width_a = (ref.shape[1] for ref in part[use[0]])
    room = up_to(width_g, LANES)
    tail = room + up_to(width_a, LANES)

    def received(b, source):
        at = pl.ds(b * size, size)
        return pltpu.make_async_copy(source.at[at, :], got_ref.at[at, :], sems.at[b, 4])

    def each(b, act, first):
        if gots == 1 or (gots and not first):
            act(received(b, sources[0]))
        elif gots:
            for i in range(2):

                @pl.when(which == i)
                def _():
                    act(received(b, sources[i]))

        unit = chunk * GROUP + b // per_unit
        for k in use:
            row = pl.multiple_of(((unit - (0, LOW)[k]) * per_unit + b % per_unit) * size, size)

            def go():
                for side in range(2):
                    act(
                        pltpu.make_async_copy(
                            part[k][side].at[pl.ds(row, size), :],
                            held[k][side].at[pl.ds(b * size, size), :],
                            sems.at[b, 2 * k + side],
                        )
                    )

            if len(use) == 1:
                go()
            else:
                pl.when((unit < HIGH) if k == 0 else (unit >= LOW))(go)

    def sent(b):
        at = pl.ds(b * size, size)
        return pltpu.make_async_copy(made_ref.at[at, :], out_ref.at[at, :], sems.at[b, 5])

    for b in range(blocks):
        each(b, lambda copy: copy.start(), True)
    for b in range(blocks):
        each(b, lambda copy: copy.wait(), False)
        at = slice(b * size, (b + 1) * size)
        if len(use) == 1:
            x_g, x_a = (ref[at, :] for ref in held[use[0]])
        else:
            of_zero = spot_ref[at, :] > 0
            x_g, x_a = (jnp.where(of_zero, held[0][i][at, :], held[1][i][at, :]) for i in range(2))
        if gots:
            step = jnp.exp(wide(got_ref[at, tail : tail + LANES]) * (1.0 / FINE)) * (1.0 / LARGEST)
            x_g = x_g + wide(got_ref[at, :width_g]) * step[:, 0:1]
            x_a = x_a + wide(got_ref[at, room : room + width_a]) * step[:, LANES - 1 : LANES]
        q_g, code_g = scaled(x_g)
        q_a, code_a = scaled(x_a)
        if room != width_g or tail != room + width_a:
            made_ref[at, :] = jnp.zeros((size, made_ref.shape[1]), jnp.int16)
        made_ref[at, :width_g] = narrow(q_g)
        made_ref[at, room : room + width_a] = narrow(q_a)
        lane = lax.broadcasted_iota(I32, (size, LANES), 1)
        made_ref[at, tail:] = narrow(jnp.where(lane < LANES // 2, code_g, code_a))
        sent(b).start()
    for b in range(blocks):
        sent(b).wait()


def stage(table, number, spot, got, parts, after):
    use = [part for part in parts if part is not None]
    width_g, width_a = use[0][0].shape[1], use[0][1].shape[1]
    unit = use[0][0].shape[0] // HIGH * GROUP
    packet = up_to(width_g, LANES) + up_to(width_a, LANES) + LANES
    flat = [array for part in use for array in part]
    row_at = 2 * number
    return pl.pallas_call(
        functools.partial(
            stage_kernel, row_at, len(got), tuple(part is not None for part in parts), len(after)
        ),
        grid_spec=pltpu.PrefetchScalarGridSpec(
            num_scalar_prefetch=1,
            grid=(1,),
            in_specs=[pl.BlockSpec((unit, 1), lambda i, c: (c[row_at], 0))]
            + [ANYWHERE] * len(got)
            + [IN_HBM] * len(flat)
            + [ANYWHERE] * len(after),
            out_specs=ANYWHERE,
            scratch_shapes=[pltpu.VMEM((unit, array.shape[1]), F32) for array in flat]
            + [pltpu.VMEM((unit, packet), jnp.int16)] * 2
            + [pltpu.SemaphoreType.DMA((unit // ROWS, 6))],
        ),
        out_shape=jax.ShapeDtypeStruct((unit, packet), jnp.int16),
        compiler_params=params(STAGE_MIB),
        name="running_sum",
    )(table, spot, *got, *flat, *after)


def side_kernel(plan, counts, z_ref, spot_ref, *refs):
    units, spans, hops, segments, after = plan
    tok, sub, fac = counts
    refs = list(refs)

    def take(n):
        out, refs[:n] = refs[:n], []
        return out

    chunks = sorted({u // GROUP for u in units})
    below = {c: take(hops) for c in chunks}
    above = {c: take(hops) for c in chunks}
    needs = {u: [k for k in (0, 1) if (u < HIGH, u >= LOW)[k]] for u in units}
    part = {k: take(2) for k in (0, 1) if any(k in needs[u] for u in units)}
    pieces = [take(2) for _ in segments]
    take(after)
    out_refs = take(sub)
    held_g, held_a, got, x_g, x_a, sums_ref = take(6)
    tables = take(len(segments))
    sems, piece_sems = take(2)
    held = (held_g, held_a)
    width_g, width_a = x_g.shape[1], x_a.shape[1]
    unit = got.shape[2]
    rows = unit // fac
    slots = pieces[0][0].shape[1]
    cap = slots // (tok * sub)
    room = up_to(width_g, LANES)
    tail = room + up_to(width_a, LANES)
    lanes = out_refs[0].shape[-1] // 2
    z, core, at_x = z_ref[0], z_ref[2], z_ref[3]
    spot_of = {}
    for u in units:
        for k in needs[u]:
            spot_of[u, k] = len(spot_of)

    def own(i, u):
        return [
            pltpu.make_async_copy(
                part[k][side].at[pl.ds((u - (0, LOW)[k]) * unit, unit), :],
                held[side].at[spot_of[u, k]],
                sems.at[i, 2 * k + side],
            )
            for k in needs[u]
            for side in range(2)
        ]

    def arrived(i, u, way, hop):
        source = (below, above)[way][u // GROUP][hop]
        return pltpu.make_async_copy(
            source.at[pl.ds(u % GROUP * unit, unit), :], got.at[way, i], sems.at[i, 4 + way]
        )

    for i, u in enumerate(units):
        for copy in own(i, u):
            copy.start()
        for way in range(2):
            for hop in range(hops):
                cut = (z_ref[way] <= 1) if hop == 0 else (z_ref[way] == hop + 1)

                @pl.when(cut)
                def _():
                    arrived(i, u, way, hop).start()

    copies = [
        pltpu.make_async_copy(
            pieces[s][half].at[klass],
            tables[s].at[c, pl.ds(half * slots, slots), :],
            piece_sems.at[s, 2 * c + half],
        )
        for c, (klass, _) in enumerate(spans)
        for s in range(len(segments))
        for half in range(2)
    ]
    for copy in copies:
        copy.start()
    for i, u in enumerate(units):
        for copy in own(i, u):
            copy.wait()
        for way in range(2):
            arrived(i, u, way, 0).wait()
        below_steps, above_steps = (steps_of(got.at[way, i], tail) for way in range(2))
        if len(needs[u]) == 2:
            of_zero = jnp.broadcast_to(spot_ref[u * unit : (u + 1) * unit, :], (unit, LANES)) > 0
        for side, (ref, own_ref) in enumerate(((x_g, held_g), (x_a, held_a))):
            for begin, wide_by in tiles_of(ref.shape[1]):
                cut = slice(begin, begin + wide_by)
                there = slice((0, room)[side] + begin, (0, room)[side] + begin + wide_by)
                full = own_ref[spot_of[u, needs[u][0]], :, cut]
                if len(needs[u]) == 2:
                    full = jnp.where(of_zero[:, :wide_by], full, own_ref[spot_of[u, 1], :, cut])
                full = full + wide(got[0, i, :, there]) * below_steps[side][:, :wide_by]
                full = full + wide(got[1, i, :, there]) * above_steps[side][:, :wide_by]
                high = full.astype(BF16)
                ref[2 * i * unit : (2 * i + 1) * unit, cut] = high
                ref[(2 * i + 1) * unit : (2 * i + 2) * unit, cut] = (full - high.astype(F32)).astype(BF16)

    for copy in copies:
        copy.wait()
    dims = (((1,), (1,)), ((), ()))
    lane = 0
    for c, (klass, members) in enumerate(spans):
        first = units.index(members[0])
        span = slice(2 * first * unit, 2 * (first + len(members)) * unit)
        total = [None, None]
        for s, (side, begin, width) in enumerate(segments):
            x = (x_g, x_a)[side]
            term = lax.dot_general(
                tables[s][c], x[span, begin : begin + width], dims, preferred_element_type=F32
            )
            total[side] = term if total[side] is None else total[side] + term
        for side in range(2):
            sums = total[side][:slots] + total[side][slots:]
            for i in range(len(members)):
                of_unit = (
                    sums[:, 2 * i * unit : (2 * i + 1) * unit] + sums[:, (2 * i + 1) * unit : (2 * i + 2) * unit]
                )
                sums_ref[...] = of_unit
                left = side * lanes + lane + i * rows
                for zz in range(tok):
                    to = lax.rem(zz + tok - z, tok)
                    for s in range(sub):
                        begin = (zz * sub + lax.rem(core + s, sub)) * cap
                        block = sums_ref[pl.ds(pl.multiple_of(begin, 8), cap), :]
                        for f in range(fac):
                            out_refs[s][lax.rem(f + fac - at_x, fac), to, :, left : left + rows] = block[
                                :, f * rows : (f + 1) * rows
                            ]
        lane += len(members) * rows


def sides(counts, where_z, spot, units, spans, parts, from_below, from_above, pieces, after):
    tok, sub, fac = counts
    hops = tok - 1
    packet = from_below[0].shape[1]
    unit = from_below[0].shape[0] // GROUP
    segments = tuple((side, begin, array[0].shape[2]) for side, begin, array in pieces)
    slots = pieces[0][2][0].shape[1]
    needs = [[k for k in (0, 1) if (u < HIGH, u >= LOW)[k]] for u in units]
    used = [array for k in (0, 1) if any(k in some for some in needs) for array in parts[k]]
    width_g, width_a = parts[0][0].shape[1], parts[0][1].shape[1]
    chunks = sorted({u // GROUP for u in units})
    near = [array for c in chunks for array in from_below[c : c + hops]]
    near += [array for c in chunks for array in from_above[c : c + hops]]
    flat = [array for _, _, pair in pieces for array in pair]
    lanes = sum(len(members) for _, members in spans) * (unit // fac)
    owns = sum(len(some) for some in needs)
    many = 2 * len(units) * unit
    return pl.pallas_call(
        functools.partial(side_kernel, (units, spans, hops, segments, len(after)), counts),
        in_specs=[SCALARS, WHOLE]
        + [ANYWHERE] * len(near)
        + [IN_HBM] * (len(used) + len(flat))
        + [ANYWHERE] * len(after),
        out_specs=[WHOLE] * sub,
        out_shape=[jax.ShapeDtypeStruct((fac, tok, slots // (tok * sub), 2 * lanes), F32)] * sub,
        scratch_shapes=[
            pltpu.VMEM((owns, unit, width_g), F32),
            pltpu.VMEM((owns, unit, width_a), F32),
            pltpu.VMEM((2, len(units), unit, packet), jnp.int16),
            pltpu.VMEM((many, width_g), BF16),
            pltpu.VMEM((many, width_a), BF16),
            pltpu.VMEM((slots, unit), F32),
        ]
        + [pltpu.VMEM((len(spans), 2 * slots, width), BF16) for _, _, width in segments]
        + [
            pltpu.SemaphoreType.DMA((len(units), 6)),
            pltpu.SemaphoreType.DMA((len(segments), 2 * len(spans))),
        ],
        compiler_params=params(),
        name="side_sums",
    )(where_z, spot, *near, *used, *flat, *after)


def final_kernel(groups, hops, first_ref, place_ref, slot_ref, *refs):
    out_ref = refs[-1]
    columns = [[], []]
    for i, batches in enumerate(groups):
        total = refs[i * hops][...]
        for hop in range(1, hops):
            total = total + refs[i * hops + hop][...]
        at = 0
        for runs in batches:
            lanes = sum(run for _, run in runs)
            scores = total[:, at : at + lanes] * total[:, at + lanes : at + 2 * lanes]
            scores = scores * (1.0 / math.sqrt(FH * D))
            at += 2 * lanes
            here = 0
            for klass, run in runs:
                columns[klass].append(scores[:, here : here + run])
                here += run
    cap = columns[0][0].shape[0]
    half_rows, block = out_ref.shape
    result = jnp.zeros((half_rows, block), F32)
    for klass in range(2):
        scores = jnp.concatenate(columns[klass], axis=1)
        count = scores.shape[1]
        begin = (0, LOW * (count // HIGH))[klass]
        row = lax.broadcasted_iota(I32, (count, block), 0) + begin
        of_class = (row < first_ref[0]) if klass == 0 else (row >= first_ref[0])
        to_query = ((place_ref[...] == row) & of_class).astype(F32)
        to_token = (lax.broadcasted_iota(I32, (half_rows, cap), 1) + klass * cap == slot_ref[...]).astype(F32)
        by_query = jnp.dot(scores, to_query, precision=lax.Precision.HIGHEST, preferred_element_type=F32)
        result = result + jnp.dot(
            to_token, by_query, precision=lax.Precision.HIGHEST, preferred_element_type=F32
        )
    out_ref[...] = result


def final(groups, first, place, slot, sums):
    hops = len(sums[0])
    return pl.pallas_call(
        functools.partial(final_kernel, groups, hops),
        in_specs=[SCALARS] + [WHOLE] * (2 + hops * len(sums)),
        out_specs=WHOLE,
        out_shape=jax.ShapeDtypeStruct((slot.shape[0], place.shape[1]), F32),
        compiler_params=params(),
        name="place_scores",
    )(first, place, slot, *[array for arrays in sums for array in arrays])


def body(
    activations,
    gradients,
    tok_class,
    query_inputs,
    query_gradients,
    query_class,
    basis_a,
    basis_g,
    eigen_a,
    eigen_g,
):
    deep_g, width_g = basis_g.shape[1:]
    deep_a, width_a = basis_a.shape[1:]
    counts = tok_count, sub_count, fac_count = tuple(lax.axis_size(a) for a in ("tok", "sub", "fac"))
    z, core, x = (lax.axis_index(a) for a in ("tok", "sub", "fac"))
    block = query_inputs.shape[0] // fac_count
    rows = block // CHUNKS
    tok_rows = activations.shape[0]
    half_rows = tok_rows // sub_count
    slot_cap = 5 * half_rows // 8
    share = half_rows // fac_count
    halves = tok_count * sub_count
    slots = halves * slot_cap
    token_ids = tok_class[:, 0]
    query_ids = query_class[:, 0]

    at = (core * fac_count + x) * share
    room = up_to(deep_g, LANES)
    blocks = []
    for step in range(tok_count):
        to = lax.rem(z + step, tok_count)
        blocks.append(
            jnp.concatenate(
                [
                    lax.dynamic_slice(gradients, (at, to * deep_g), (share, deep_g)),
                    jnp.zeros((share, room - deep_g), BF16),
                    lax.dynamic_slice(activations, (at, to * deep_a), (share, deep_a)),
                ],
                axis=1,
            )
        )
    moved = [blocks[0]] + [
        lax.ppermute(blocks[step], "tok", turn(tok_count, step)) for step in range(1, tok_count)
    ]

    qids = query_ids.reshape(fac_count, block)
    key = qids * block + jnp.arange(block)
    place = jnp.sum((key[:, None, :] < key[:, :, None]).astype(I32), axis=2)
    first = jnp.sum((qids == 0).astype(I32), axis=1)
    spot = (jnp.arange(CHUNKS)[:, None, None] * rows + jnp.arange(rows)) < first[None, :, None]
    spot = spot.reshape(query_ids.shape[0], 1).astype(I32)
    features = (query_gradients, query_inputs, basis_g, basis_a, fac_count, rows)
    parts = [query_coords(0, place, *features, blocks[1:]), None]

    ids = token_ids.reshape(halves, half_rows)
    earlier = jnp.arange(half_rows)[None, :] < jnp.arange(half_rows)[:, None]
    rank = jnp.sum(((ids[:, None, :] == ids[:, :, None]) & earlier).astype(I32), axis=2)
    slot = ids * slots + jnp.arange(halves)[:, None] * slot_cap + rank
    slot = slot.reshape(halves * fac_count, share)
    own_slot = lax.dynamic_index_in_dim(ids * slot_cap + rank, z * sub_count + core, 0).reshape(half_rows, 1)
    places = jnp.stack([z, core, x]).astype(I32)
    where_z = jnp.stack([z, tok_count - 1 - z, core, x]).astype(I32)

    state = {"pieces": []}

    def second(after):
        parts[1] = query_coords(1, place, *features, after)
        return parts[1][1]

    def joined(after):
        mine = join(moved, after)
        raws = [mine]
        for step in range(1, fac_count):
            raws.append(lax.ppermute(mine, "fac", turn(fac_count, step)))
        for step in range(1, sub_count):
            raws += [lax.ppermute(raw, "sub", turn(sub_count, step)) for raw in raws[:fac_count]]
        state["raws"] = raws
        return mine

    def packed(after):
        state["packed"] = pack(counts, places, slot, state["raws"], slots, deep_g, deep_a, after)
        return state["packed"][0]

    def token(side, column):
        def run(after):
            eigen, basis = ((eigen_g, basis_g), (eigen_a, basis_a))[side]
            segment = SEGMENT if side == 0 else width_a
            pair = token_coords(state["packed"][side], eigen, basis, column, segment, after)
            state["pieces"].append((side, column, pair))
            return pair[0]

        return run

    from_below, from_above = [], []
    groups, sent = [], []

    def batch(units, spans):
        def run(after):
            out = sides(
                counts, where_z, spot, units, spans, parts, from_below, from_above, state["pieces"], after
            )
            groups.append(tuple((klass, len(members) * rows) for klass, members in spans))
            sent.append(out)
            return out[0]

        return run

    columns = list(range(0, width_g, SEGMENT))
    fillers = [[joined, second], [packed, token(1, 0)]]
    fillers += [[token(0, column)] for column in columns]
    needs = {}
    for units in (range(4), range(4, 6), range(6, 8)):
        spans = [(k, [u for u in units if (u < HIGH, u >= LOW)[k]]) for k in range(2)]
        needs[len(fillers)] = units[-1] // GROUP + tok_count - 2
        fillers.append([batch(list(units), [span for span in spans if span[1]])])

    def over_plane(batches):
        totals = []
        for own, *others in batches:
            for step, other in enumerate(others, 1):
                own = own + lax.ppermute(other, "sub", turn(sub_count, step))
            totals.append(own)
        whole = totals[0] if len(totals) == 1 else jnp.concatenate(totals, axis=-1)
        total = whole[0]
        for step in range(1, fac_count):
            total = total + lax.ppermute(whole[step], "fac", turn(fac_count, step))
        return total

    def over_line(totals):
        whole = jnp.concatenate(totals, axis=-1)
        return [whole[0]] + [
            lax.ppermute(whole[step], "tok", turn(tok_count, step)) for step in range(1, tok_count)
        ]

    up = [(i, i + 1) for i in range(tok_count - 1)]
    down = [(i + 1, i) for i in range(tok_count - 1)]
    last = tok_count - 1
    after = []
    chunks = CHUNKS // GROUP
    steps = chunks + tok_count - 2
    done = 0
    low_half = z < tok_count // 2
    low_flag = low_half.astype(I32)
    behinds = (z, last - z)
    near_end = jnp.minimum(z, last - z)
    table = []
    for step in range(steps):
        if step < 2:
            table += [jnp.clip(step - near_end, 0, chunks - 1), jnp.int32(0)] * 2
        elif step == steps - 1:
            table += [jnp.int32(chunks - 1), low_flag] * 2
        else:
            for behind in behinds:
                table += [jnp.clip(step - behind, 0, chunks - 1), jnp.int32(0)]
    table = jnp.stack([jnp.asarray(entry).astype(I32) for entry in table])
    for step in range(steps):
        early, late = max(step - tok_count + 1, 0) * GROUP, min(step, chunks - 1) * GROUP + GROUP - 1
        wanted = [parts[0] if early < HIGH else None, parts[1] if late >= LOW else None]
        if step == 0:
            packet = stage(table, 0, spot, [], wanted, after)
            came = lax.ppermute(packet, "tok", [(0, 1), (last, last - 1)])
            from_below.append(came)
            from_above.append(came)
            after = [packet]
        elif step == 1:
            packet = stage(table, 2, spot, [from_below[-1]], wanted, after)
            from_below.append(lax.ppermute(packet, "tok", up[:2]))
            from_above.append(lax.ppermute(packet, "tok", down[-2:]))
            after = [packet]
        elif step == steps - 1:
            got = [from_below[-1], from_above[-1]]
            packet = stage(table, 2 * step, spot, got, [None, parts[1]], after)
            came = lax.ppermute(packet, "tok", [(last - 1, last), (1, 0)])
            from_below.append(came)
            from_above.append(came)
            after = [packet]
        else:
            for way, (got, pairs) in enumerate(((from_below, up), (from_above, down))):
                packet = stage(table, 2 * step + way, spot, got[-1:], wanted, after)
                got.append(lax.ppermute(packet, "tok", pairs))
                after = [packet]
        if step < steps - 1 and needs.get(done, -1) < step:
            for item in fillers[done]:
                after = [item(after)]
            done += 1
    for items in fillers[done:]:
        for item in items:
            after = [item(after)]
    sums = [over_line([over_plane(sent[:2]), over_plane(sent[2:])])]

    own_place = lax.dynamic_index_in_dim(place, x, 0)
    own_first = lax.dynamic_index_in_dim(first, x, 0)
    return final([groups], own_first, own_place, own_slot, sums).T


def solution(mesh):
    placed = (
        P(("grp", "tok"), None),
        P(("grp", "tok"), None),
        P("grp", None),
        P("grp", "tok"),
        P("grp", "tok"),
        P("grp", None),
        P(None, "tok", ("fac", "sub")),
        P(None, "tok", ("fac", "sub")),
        P(None, ("fac", "sub")),
        P(None, ("fac", "sub")),
    )
    return jax.shard_map(
        body, mesh=mesh, in_specs=placed, out_specs=P("fac", ("grp", "tok", "sub")), check_vma=False
    )
```

```python
import functools
import math

import jax
import jax.numpy as jnp
from jax import lax
from jax.experimental import pallas as pl
from jax.experimental.pallas import tpu as pltpu
from jax.sharding import PartitionSpec as P

D = 5120
FH = 13824
DAMPING = 0.25
CHUNKS = 8
LOW, HIGH = 3 * CHUNKS // 8, 5 * CHUNKS // 8
LARGEST = 32760.0
TO_WHOLE = 1.5 * 2.0**23
LANES = 128
TILE = 512
SEGMENT = 4 * TILE
GROUP = 2
ROWS = 64
STAGE_MIB = 20
MIB = 1 << 20
F32 = jnp.float32
BF16 = jnp.bfloat16
I32 = jnp.int32
FINE = 8.0 / math.log(2.0)
IN_HBM = pl.BlockSpec(memory_space=pltpu.HBM)
ANYWHERE = pl.BlockSpec(memory_space=pl.ANY)
SCALARS = pl.BlockSpec(memory_space=pltpu.SMEM)
WHOLE = pl.BlockSpec(memory_space=pltpu.VMEM)


def up_to(n, m):
    return -(-n // m) * m


def params(mib=34, slots=0):
    return pltpu.CompilerParams(vmem_limit_bytes=(mib if slots <= 512 else 63) * MIB)


def turn(count, step):
    return [(i, (i + step) % count) for i in range(count)]


def query_kernel(fac, rows, first, tiles, place_ref, feat_g_ref, feat_a_ref, basis_g_ref, basis_a_ref, *refs):
    out_g_ref, out_a_ref, sorted_g_ref, sorted_a_ref = refs[-4:]
    block = place_ref.shape[1]
    unit = fac * rows

    def put(feat_ref, sorted_ref):
        for f in range(fac):
            spots = lax.broadcasted_iota(I32, (HIGH * rows, block), 0) + first * rows
            order = (spots == place_ref[f : f + 1, :]).astype(F32).astype(BF16)
            moved = jnp.dot(
                order, feat_ref[f * block : (f + 1) * block, :], preferred_element_type=F32
            ).astype(BF16)
            for j in range(HIGH):
                sorted_ref[j * unit + f * rows : j * unit + (f + 1) * rows, :] = moved[
                    j * rows : (j + 1) * rows, :
                ]

    step = pl.program_id(0)

    @pl.when(step == 0)
    def _():
        put(feat_g_ref, sorted_g_ref)

    @pl.when(step == tiles)
    def _():
        put(feat_a_ref, sorted_a_ref)

    @pl.when(step < tiles)
    def _():
        out_g_ref[...] = jnp.dot(sorted_g_ref[...], basis_g_ref[0], preferred_element_type=F32)

    @pl.when(step >= tiles)
    def _():
        out_a_ref[...] = jnp.dot(sorted_a_ref[...], basis_a_ref[0], preferred_element_type=F32)


def query_coords(klass, place, feat_g, feat_a, basis_g, basis_a, fac, rows, after=()):
    queries, deep_g = feat_g.shape
    deep_a = feat_a.shape[1]
    width_g, width_a = basis_g.shape[2], basis_a.shape[2]
    tile_g, tile_a = min(TILE, width_g), min(TILE, width_a)
    tiles_g, tiles_a = pl.cdiv(width_g, tile_g), pl.cdiv(width_a, tile_a)
    count = HIGH * fac * rows
    at_g = lambda i: jnp.minimum(i, tiles_g - 1)
    at_a = lambda i: jnp.maximum(i - tiles_g, 0)
    return pl.pallas_call(
        functools.partial(query_kernel, fac, rows, (0, LOW)[klass], tiles_g),
        grid=(tiles_g + tiles_a,),
        in_specs=[
            pl.BlockSpec(place.shape, lambda i: (0, 0)),
            pl.BlockSpec((queries, deep_g), lambda i: (0, 0)),
            pl.BlockSpec((queries, deep_a), lambda i: (0, 0)),
            pl.BlockSpec((1, deep_g, tile_g), lambda i: (klass, 0, at_g(i))),
            pl.BlockSpec((1, deep_a, tile_a), lambda i: (klass, 0, at_a(i))),
        ]
        + [ANYWHERE] * len(after),
        out_specs=[
            pl.BlockSpec((count, tile_g), lambda i: (0, at_g(i))),
            pl.BlockSpec((count, tile_a), lambda i: (0, at_a(i))),
        ],
        out_shape=[jax.ShapeDtypeStruct((count, width), F32) for width in (width_g, width_a)],
        scratch_shapes=[pltpu.VMEM((count, deep), BF16) for deep in (deep_g, deep_a)],
        compiler_params=params(),
        name="query_coords",
    )(place, feat_g, feat_a, basis_g, basis_a, *after)


def join_kernel(count, *refs):
    sources, out_ref, sems = refs[:count], refs[-2], refs[-1]
    size = sources[0].shape[0]
    copies = [
        pltpu.make_async_copy(ref, out_ref.at[pl.ds(i * size, size), :], sems.at[i])
        for i, ref in enumerate(sources)
    ]
    for copy in copies:
        copy.start()
    for copy in copies:
        copy.wait()


def join(blocks, after):
    size, width = blocks[0].shape
    return pl.pallas_call(
        functools.partial(join_kernel, len(blocks)),
        in_specs=[ANYWHERE] * (len(blocks) + len(after)),
        out_specs=WHOLE,
        out_shape=jax.ShapeDtypeStruct((size * len(blocks), width), BF16),
        scratch_shapes=[pltpu.SemaphoreType.DMA((len(blocks),))],
        compiler_params=params(),
        name="join_tokens",
    )(*blocks, *after)


def pack_kernel(counts, slots, room, at_ref, slot_ref, *refs):
    tok, sub, fac = counts
    raws = refs[: sub * fac]
    g_ref, a_ref, made_g, made_a, raw_ref, sems, out_sems = refs[-7:]
    size = raws[0].shape[0]
    copies = [
        pltpu.make_async_copy(ref, raw_ref.at[pl.ds(i * size, size), :], sems.at[i])
        for i, ref in enumerate(raws)
    ]
    for copy in copies:
        copy.start()
    here = []
    for s in range(sub):
        for f in range(fac):
            for k in range(tok):
                row = lax.rem(at_ref[0] + tok - k, tok) * sub + lax.rem(at_ref[1] + sub - s, sub)
                row = row * fac + lax.rem(at_ref[2] + fac - f, fac)
                here.append(slot_ref[pl.ds(row, 1), :])
    here = jnp.concatenate(here, axis=1)
    for copy in copies:
        copy.wait()
    outs = []
    for klass in range(2):
        table = lax.broadcasted_iota(I32, (slots, here.shape[1]), 0) + klass * slots == here
        table = table.astype(F32).astype(BF16)
        for side, (ref, made, begin) in enumerate(((g_ref, made_g, 0), (a_ref, made_a, room))):
            made[klass] = jnp.dot(
                table, raw_ref[:, begin : begin + ref.shape[2]], preferred_element_type=F32
            ).astype(BF16)
            out = pltpu.make_async_copy(made.at[klass], ref.at[klass], out_sems.at[klass, side])
            out.start()
            outs.append(out)
    for out in outs:
        out.wait()


def pack(counts, at, slot, raws, slots, deep_g, deep_a, after):
    size, width = raws[0].shape
    return pl.pallas_call(
        functools.partial(pack_kernel, counts, slots, up_to(deep_g, LANES)),
        in_specs=[SCALARS, WHOLE] + [ANYWHERE] * (len(raws) + len(after)),
        out_specs=[ANYWHERE, ANYWHERE],
        out_shape=[jax.ShapeDtypeStruct((2, slots, deep), BF16) for deep in (deep_g, deep_a)],
        scratch_shapes=[
            pltpu.VMEM((2, slots, deep_g), BF16),
            pltpu.VMEM((2, slots, deep_a), BF16),
            pltpu.VMEM((size * len(raws), width), BF16),
            pltpu.SemaphoreType.DMA((len(raws),)),
            pltpu.SemaphoreType.DMA((2, 2)),
        ],
        compiler_params=params(slots=slots),
        name="pack_tokens",
    )(at, slot, *raws, *after)


def token_kernel(packed_ref, eigen_ref, basis_ref, *refs):
    high_ref, low_ref = refs[-2:]
    for klass in range(2):
        coords = (
            jnp.dot(packed_ref[klass], basis_ref[klass], preferred_element_type=F32)
            / (eigen_ref[klass : klass + 1, :] + DAMPING)
        )
        high = coords.astype(BF16)
        high_ref[klass] = high
        low_ref[klass] = (coords - high.astype(F32)).astype(BF16)


def token_coords(packed, eigen, basis, column, segment, after):
    slots = packed.shape[1]
    deep, width = basis.shape[1:]
    here = min(segment, width - column)
    tile = min(TILE, width)
    base = column // tile
    out = jax.ShapeDtypeStruct((2, slots, here), BF16)
    return pl.pallas_call(
        token_kernel,
        grid=(pl.cdiv(here, tile),),
        in_specs=[
            pl.BlockSpec((2, slots, deep), lambda i: (0, 0, 0)),
            pl.BlockSpec((2, tile), lambda i: (0, base + i)),
            pl.BlockSpec((2, deep, tile), lambda i: (0, 0, base + i)),
        ]
        + [ANYWHERE] * len(after),
        out_specs=[pl.BlockSpec((2, slots, tile), lambda i: (0, 0, i))] * 2,
        out_shape=[out, out],
        compiler_params=params(slots=slots),
        name="token_coords",
    )(packed, eigen, basis, *after)


def tiles_of(width):
    return [(begin, min(LANES, width - begin)) for begin in range(0, width, LANES)]


def scaled(x):
    top = jnp.max(jnp.abs(x), axis=1, keepdims=True)
    code = jnp.ceil(jnp.log(jnp.maximum(top, 1e-30)) * FINE)
    factor = LARGEST * jnp.exp(code * (-1.0 / FINE))
    return (x * factor + TO_WHOLE) - TO_WHOLE, code


def narrow(x):
    return x.astype(I32).astype(jnp.int16)


def wide(x):
    return x.astype(I32).astype(F32)


def steps_of(ref, tail):
    step = jnp.exp(wide(ref[:, tail : tail + LANES]) * (1.0 / FINE)) * (1.0 / LARGEST)
    shape = step.shape
    return (
        jnp.broadcast_to(step[:, 0:1], shape),
        jnp.broadcast_to(step[:, LANES - 1 : LANES], shape),
    )


def stage_kernel(row_at, gots, parts, after, at_ref, spot_ref, *refs):
    sources, refs = refs[:gots], refs[gots:]
    use = [k for k in range(2) if parts[k]]
    part = {k: (refs[2 * i], refs[2 * i + 1]) for i, k in enumerate(use)}
    refs = refs[2 * len(use) + after :]
    out_ref, refs = refs[0], refs[1:]
    held = {k: (refs[2 * i], refs[2 * i + 1]) for i, k in enumerate(use)}
    got_ref, made_ref, sems = refs[2 * len(use) :]
    chunk, which = at_ref[row_at], at_ref[row_at + 1]
    size = ROWS
    blocks = out_ref.shape[0] // size
    per_unit = blocks // GROUP
    width_g, width_a = (ref.shape[1] for ref in part[use[0]])
    room = up_to(width_g, LANES)
    tail = room + up_to(width_a, LANES)

    def received(b, source):
        at = pl.ds(b * size, size)
        return pltpu.make_async_copy(source.at[at, :], got_ref.at[at, :], sems.at[b, 4])

    def each(b, act, first):
        if gots == 1 or (gots and not first):
            act(received(b, sources[0]))
        elif gots:
            for i in range(2):

                @pl.when(which == i)
                def _():
                    act(received(b, sources[i]))

        unit = chunk * GROUP + b // per_unit
        for k in use:
            row = pl.multiple_of(((unit - (0, LOW)[k]) * per_unit + b % per_unit) * size, size)

            def go():
                for side in range(2):
                    act(
                        pltpu.make_async_copy(
                            part[k][side].at[pl.ds(row, size), :],
                            held[k][side].at[pl.ds(b * size, size), :],
                            sems.at[b, 2 * k + side],
                        )
                    )

            if len(use) == 1:
                go()
            else:
                pl.when((unit < HIGH) if k == 0 else (unit >= LOW))(go)

    def sent(b):
        at = pl.ds(b * size, size)
        return pltpu.make_async_copy(made_ref.at[at, :], out_ref.at[at, :], sems.at[b, 5])

    for b in range(blocks):
        each(b, lambda copy: copy.start(), True)
    for b in range(blocks):
        each(b, lambda copy: copy.wait(), False)
        at = slice(b * size, (b + 1) * size)
        if len(use) == 1:
            x_g, x_a = (ref[at, :] for ref in held[use[0]])
        else:
            of_zero = spot_ref[at, :] > 0
            x_g, x_a = (jnp.where(of_zero, held[0][i][at, :], held[1][i][at, :]) for i in range(2))
        if gots:
            step = jnp.exp(wide(got_ref[at, tail : tail + LANES]) * (1.0 / FINE)) * (1.0 / LARGEST)
            x_g = x_g + wide(got_ref[at, :width_g]) * step[:, 0:1]
            x_a = x_a + wide(got_ref[at, room : room + width_a]) * step[:, LANES - 1 : LANES]
        q_g, code_g = scaled(x_g)
        q_a, code_a = scaled(x_a)
        if room != width_g or tail != room + width_a:
            made_ref[at, :] = jnp.zeros((size, made_ref.shape[1]), jnp.int16)
        made_ref[at, :width_g] = narrow(q_g)
        made_ref[at, room : room + width_a] = narrow(q_a)
        lane = lax.broadcasted_iota(I32, (size, LANES), 1)
        made_ref[at, tail:] = narrow(jnp.where(lane < LANES // 2, code_g, code_a))
        sent(b).start()
    for b in range(blocks):
        sent(b).wait()


def stage(table, number, spot, got, parts, after):
    use = [part for part in parts if part is not None]
    width_g, width_a = use[0][0].shape[1], use[0][1].shape[1]
    unit = use[0][0].shape[0] // HIGH * GROUP
    packet = up_to(width_g, LANES) + up_to(width_a, LANES) + LANES
    flat = [array for part in use for array in part]
    row_at = 2 * number
    return pl.pallas_call(
        functools.partial(
            stage_kernel, row_at, len(got), tuple(part is not None for part in parts), len(after)
        ),
        grid_spec=pltpu.PrefetchScalarGridSpec(
            num_scalar_prefetch=1,
            grid=(1,),
            in_specs=[pl.BlockSpec((unit, 1), lambda i, c: (c[row_at], 0))]
            + [ANYWHERE] * len(got)
            + [IN_HBM] * len(flat)
            + [ANYWHERE] * len(after),
            out_specs=ANYWHERE,
            scratch_shapes=[pltpu.VMEM((unit, array.shape[1]), F32) for array in flat]
            + [pltpu.VMEM((unit, packet), jnp.int16)] * 2
            + [pltpu.SemaphoreType.DMA((unit // ROWS, 6))],
        ),
        out_shape=jax.ShapeDtypeStruct((unit, packet), jnp.int16),
        compiler_params=params(STAGE_MIB),
        name="running_sum",
    )(table, spot, *got, *flat, *after)


def side_kernel(plan, counts, z_ref, spot_ref, *refs):
    units, spans, hops, segments, after = plan
    tok, sub, fac = counts
    refs = list(refs)

    def take(n):
        out, refs[:n] = refs[:n], []
        return out

    chunks = sorted({u // GROUP for u in units})
    below = {c: take(hops) for c in chunks}
    above = {c: take(hops) for c in chunks}
    needs = {u: [k for k in (0, 1) if (u < HIGH, u >= LOW)[k]] for u in units}
    part = {k: take(2) for k in (0, 1) if any(k in needs[u] for u in units)}
    pieces = [take(2) for _ in segments]
    take(after)
    out_refs = take(sub)
    held_g, held_a, got, x_g, x_a, sums_ref = take(6)
    tables = take(len(segments))
    sems, piece_sems = take(2)
    held = (held_g, held_a)
    width_g, width_a = x_g.shape[1], x_a.shape[1]
    unit = got.shape[2]
    rows = unit // fac
    slots = pieces[0][0].shape[1]
    cap = slots // (tok * sub)
    room = up_to(width_g, LANES)
    tail = room + up_to(width_a, LANES)
    lanes = out_refs[0].shape[-1] // 2
    z, core, at_x = z_ref[0], z_ref[2], z_ref[3]
    spot_of = {}
    for u in units:
        for k in needs[u]:
            spot_of[u, k] = len(spot_of)

    def own(i, u):
        return [
            pltpu.make_async_copy(
                part[k][side].at[pl.ds((u - (0, LOW)[k]) * unit, unit), :],
                held[side].at[spot_of[u, k]],
                sems.at[i, 2 * k + side],
            )
            for k in needs[u]
            for side in range(2)
        ]

    def arrived(i, u, way, hop):
        source = (below, above)[way][u // GROUP][hop]
        return pltpu.make_async_copy(
            source.at[pl.ds(u % GROUP * unit, unit), :], got.at[way, i], sems.at[i, 4 + way]
        )

    for i, u in enumerate(units):
        for copy in own(i, u):
            copy.start()
        for way in range(2):
            for hop in range(hops):
                cut = (z_ref[way] <= 1) if hop == 0 else (z_ref[way] == hop + 1)

                @pl.when(cut)
                def _():
                    arrived(i, u, way, hop).start()

    copies = [
        pltpu.make_async_copy(
            pieces[s][half].at[klass],
            tables[s].at[c, pl.ds(half * slots, slots), :],
            piece_sems.at[s, 2 * c + half],
        )
        for c, (klass, _) in enumerate(spans)
        for s in range(len(segments))
        for half in range(2)
    ]
    for copy in copies:
        copy.start()
    for i, u in enumerate(units):
        for copy in own(i, u):
            copy.wait()
        for way in range(2):
            arrived(i, u, way, 0).wait()
        below_steps, above_steps = (steps_of(got.at[way, i], tail) for way in range(2))
        if len(needs[u]) == 2:
            of_zero = jnp.broadcast_to(spot_ref[u * unit : (u + 1) * unit, :], (unit, LANES)) > 0
        for side, (ref, own_ref) in enumerate(((x_g, held_g), (x_a, held_a))):
            for begin, wide_by in tiles_of(ref.shape[1]):
                cut = slice(begin, begin + wide_by)
                there = slice((0, room)[side] + begin, (0, room)[side] + begin + wide_by)
                full = own_ref[spot_of[u, needs[u][0]], :, cut]
                if len(needs[u]) == 2:
                    full = jnp.where(of_zero[:, :wide_by], full, own_ref[spot_of[u, 1], :, cut])
                full = full + wide(got[0, i, :, there]) * below_steps[side][:, :wide_by]
                full = full + wide(got[1, i, :, there]) * above_steps[side][:, :wide_by]
                high = full.astype(BF16)
                ref[2 * i * unit : (2 * i + 1) * unit, cut] = high
                ref[(2 * i + 1) * unit : (2 * i + 2) * unit, cut] = (full - high.astype(F32)).astype(BF16)

    for copy in copies:
        copy.wait()
    dims = (((1,), (1,)), ((), ()))
    lane = 0
    for c, (klass, members) in enumerate(spans):
        first = units.index(members[0])
        span = slice(2 * first * unit, 2 * (first + len(members)) * unit)
        total = [None, None]
        for s, (side, begin, width) in enumerate(segments):
            x = (x_g, x_a)[side]
            term = lax.dot_general(
                tables[s][c], x[span, begin : begin + width], dims, preferred_element_type=F32
            )
            total[side] = term if total[side] is None else total[side] + term
        for side in range(2):
            sums = total[side][:slots] + total[side][slots:]
            for i in range(len(members)):
                of_unit = (
                    sums[:, 2 * i * unit : (2 * i + 1) * unit] + sums[:, (2 * i + 1) * unit : (2 * i + 2) * unit]
                )
                sums_ref[...] = of_unit
                left = side * lanes + lane + i * rows
                for zz in range(tok):
                    to = lax.rem(zz + tok - z, tok)
                    for s in range(sub):
                        begin = (zz * sub + lax.rem(core + s, sub)) * cap
                        block = sums_ref[pl.ds(pl.multiple_of(begin, 8), cap), :]
                        for f in range(fac):
                            out_refs[s][lax.rem(f + fac - at_x, fac), to, :, left : left + rows] = block[
                                :, f * rows : (f + 1) * rows
                            ]
        lane += len(members) * rows


def sides(counts, where_z, spot, units, spans, parts, from_below, from_above, pieces, after):
    tok, sub, fac = counts
    hops = tok - 1
    packet = from_below[0].shape[1]
    unit = from_below[0].shape[0] // GROUP
    segments = tuple((side, begin, array[0].shape[2]) for side, begin, array in pieces)
    slots = pieces[0][2][0].shape[1]
    needs = [[k for k in (0, 1) if (u < HIGH, u >= LOW)[k]] for u in units]
    used = [array for k in (0, 1) if any(k in some for some in needs) for array in parts[k]]
    width_g, width_a = parts[0][0].shape[1], parts[0][1].shape[1]
    chunks = sorted({u // GROUP for u in units})
    near = [array for c in chunks for array in from_below[c : c + hops]]
    near += [array for c in chunks for array in from_above[c : c + hops]]
    flat = [array for _, _, pair in pieces for array in pair]
    lanes = sum(len(members) for _, members in spans) * (unit // fac)
    owns = sum(len(some) for some in needs)
    many = 2 * len(units) * unit
    return pl.pallas_call(
        functools.partial(side_kernel, (units, spans, hops, segments, len(after)), counts),
        in_specs=[SCALARS, WHOLE]
        + [ANYWHERE] * len(near)
        + [IN_HBM] * (len(used) + len(flat))
        + [ANYWHERE] * len(after),
        out_specs=[WHOLE] * sub,
        out_shape=[jax.ShapeDtypeStruct((fac, tok, slots // (tok * sub), 2 * lanes), F32)] * sub,
        scratch_shapes=[
            pltpu.VMEM((owns, unit, width_g), F32),
            pltpu.VMEM((owns, unit, width_a), F32),
            pltpu.VMEM((2, len(units), unit, packet), jnp.int16),
            pltpu.VMEM((many, width_g), BF16),
            pltpu.VMEM((many, width_a), BF16),
            pltpu.VMEM((slots, unit), F32),
        ]
        + [pltpu.VMEM((len(spans), 2 * slots, width), BF16) for _, _, width in segments]
        + [
            pltpu.SemaphoreType.DMA((len(units), 6)),
            pltpu.SemaphoreType.DMA((len(segments), 2 * len(spans))),
        ],
        compiler_params=params(slots=slots),
        name="side_sums",
    )(where_z, spot, *near, *used, *flat, *after)


def final_kernel(groups, hops, first_ref, place_ref, slot_ref, *refs):
    out_ref = refs[-1]
    columns = [[], []]
    for i, batches in enumerate(groups):
        total = refs[i * hops][...]
        for hop in range(1, hops):
            total = total + refs[i * hops + hop][...]
        at = 0
        for runs in batches:
            lanes = sum(run for _, run in runs)
            scores = total[:, at : at + lanes] * total[:, at + lanes : at + 2 * lanes]
            scores = scores * (1.0 / math.sqrt(FH * D))
            at += 2 * lanes
            here = 0
            for klass, run in runs:
                columns[klass].append(scores[:, here : here + run])
                here += run
    cap = columns[0][0].shape[0]
    half_rows, block = out_ref.shape
    result = jnp.zeros((half_rows, block), F32)
    for klass in range(2):
        scores = jnp.concatenate(columns[klass], axis=1)
        count = scores.shape[1]
        begin = (0, LOW * (count // HIGH))[klass]
        row = lax.broadcasted_iota(I32, (count, block), 0) + begin
        of_class = (row < first_ref[0]) if klass == 0 else (row >= first_ref[0])
        to_query = ((place_ref[...] == row) & of_class).astype(F32)
        to_token = (lax.broadcasted_iota(I32, (half_rows, cap), 1) + klass * cap == slot_ref[...]).astype(F32)
        by_query = jnp.dot(scores, to_query, precision=lax.Precision.HIGHEST, preferred_element_type=F32)
        result = result + jnp.dot(
            to_token, by_query, precision=lax.Precision.HIGHEST, preferred_element_type=F32
        )
    out_ref[...] = result


def final(groups, first, place, slot, sums):
    hops = len(sums[0])
    return pl.pallas_call(
        functools.partial(final_kernel, groups, hops),
        in_specs=[SCALARS] + [WHOLE] * (2 + hops * len(sums)),
        out_specs=WHOLE,
        out_shape=jax.ShapeDtypeStruct((slot.shape[0], place.shape[1]), F32),
        compiler_params=params(),
        name="place_scores",
    )(first, place, slot, *[array for arrays in sums for array in arrays])


def body(
    activations,
    gradients,
    tok_class,
    query_inputs,
    query_gradients,
    query_class,
    basis_a,
    basis_g,
    eigen_a,
    eigen_g,
):
    deep_g, width_g = basis_g.shape[1:]
    deep_a, width_a = basis_a.shape[1:]
    counts = tok_count, sub_count, fac_count = tuple(lax.axis_size(a) for a in ("tok", "sub", "fac"))
    z, core, x = (lax.axis_index(a) for a in ("tok", "sub", "fac"))
    block = query_inputs.shape[0] // fac_count
    rows = block // CHUNKS
    tok_rows = activations.shape[0]
    half_rows = tok_rows // sub_count
    slot_cap = 5 * half_rows // 8
    share = half_rows // fac_count
    halves = tok_count * sub_count
    slots = halves * slot_cap
    token_ids = tok_class[:, 0]
    query_ids = query_class[:, 0]

    at = (core * fac_count + x) * share
    room = up_to(deep_g, LANES)
    blocks = []
    for step in range(tok_count):
        to = lax.rem(z + step, tok_count)
        blocks.append(
            jnp.concatenate(
                [
                    lax.dynamic_slice(gradients, (at, to * deep_g), (share, deep_g)),
                    jnp.zeros((share, room - deep_g), BF16),
                    lax.dynamic_slice(activations, (at, to * deep_a), (share, deep_a)),
                ],
                axis=1,
            )
        )
    moved = [blocks[0]] + [
        lax.ppermute(blocks[step], "tok", turn(tok_count, step)) for step in range(1, tok_count)
    ]

    qids = query_ids.reshape(fac_count, block)
    key = qids * block + jnp.arange(block)
    place = jnp.sum((key[:, None, :] < key[:, :, None]).astype(I32), axis=2)
    first = jnp.sum((qids == 0).astype(I32), axis=1)
    spot = (jnp.arange(CHUNKS)[:, None, None] * rows + jnp.arange(rows)) < first[None, :, None]
    spot = spot.reshape(query_ids.shape[0], 1).astype(I32)
    features = (query_gradients, query_inputs, basis_g, basis_a, fac_count, rows)
    parts = [query_coords(0, place, *features, blocks[1:]), None]

    ids = token_ids.reshape(halves, half_rows)
    earlier = jnp.arange(half_rows)[None, :] < jnp.arange(half_rows)[:, None]
    rank = jnp.sum(((ids[:, None, :] == ids[:, :, None]) & earlier).astype(I32), axis=2)
    slot = ids * slots + jnp.arange(halves)[:, None] * slot_cap + rank
    slot = slot.reshape(halves * fac_count, share)
    own_slot = lax.dynamic_index_in_dim(ids * slot_cap + rank, z * sub_count + core, 0).reshape(half_rows, 1)
    places = jnp.stack([z, core, x]).astype(I32)
    where_z = jnp.stack([z, tok_count - 1 - z, core, x]).astype(I32)

    state = {"pieces": []}

    def second(after):
        parts[1] = query_coords(1, place, *features, after)
        return parts[1][1]

    def joined(after):
        mine = join(moved, after)
        raws = [mine]
        for step in range(1, fac_count):
            raws.append(lax.ppermute(mine, "fac", turn(fac_count, step)))
        for step in range(1, sub_count):
            raws += [lax.ppermute(raw, "sub", turn(sub_count, step)) for raw in raws[:fac_count]]
        state["raws"] = raws
        return mine

    def packed(after):
        state["packed"] = pack(counts, places, slot, state["raws"], slots, deep_g, deep_a, after)
        return state["packed"][0]

    def token(side, column):
        def run(after):
            eigen, basis = ((eigen_g, basis_g), (eigen_a, basis_a))[side]
            segment = SEGMENT if side == 0 else width_a
            pair = token_coords(state["packed"][side], eigen, basis, column, segment, after)
            state["pieces"].append((side, column, pair))
            return pair[0]

        return run

    from_below, from_above = [], []
    groups, sent = [], []

    def batch(units, spans):
        def run(after):
            out = sides(
                counts, where_z, spot, units, spans, parts, from_below, from_above, state["pieces"], after
            )
            groups.append(tuple((klass, len(members) * rows) for klass, members in spans))
            sent.append(out)
            return out[0]

        return run

    columns = list(range(0, width_g, SEGMENT))
    fillers = [[joined, second], [packed, token(1, 0)]]
    fillers += [[token(0, column)] for column in columns]
    needs = {}
    for units in (range(4), range(4, 6), range(6, 8)):
        spans = [(k, [u for u in units if (u < HIGH, u >= LOW)[k]]) for k in range(2)]
        needs[len(fillers)] = units[-1] // GROUP + tok_count - 2
        fillers.append([batch(list(units), [span for span in spans if span[1]])])

    def over_plane(batches):
        totals = []
        for own, *others in batches:
            for step, other in enumerate(others, 1):
                own = own + lax.ppermute(other, "sub", turn(sub_count, step))
            totals.append(own)
        whole = totals[0] if len(totals) == 1 else jnp.concatenate(totals, axis=-1)
        total = whole[0]
        for step in range(1, fac_count):
            total = total + lax.ppermute(whole[step], "fac", turn(fac_count, step))
        return total

    def over_line(totals):
        whole = jnp.concatenate(totals, axis=-1)
        return [whole[0]] + [
            lax.ppermute(whole[step], "tok", turn(tok_count, step)) for step in range(1, tok_count)
        ]

    up = [(i, i + 1) for i in range(tok_count - 1)]
    down = [(i + 1, i) for i in range(tok_count - 1)]
    last = tok_count - 1
    after = []
    chunks = CHUNKS // GROUP
    steps = chunks + tok_count - 2
    done = 0
    low_half = z < tok_count // 2
    low_flag = low_half.astype(I32)
    behinds = (z, last - z)
    near_end = jnp.minimum(z, last - z)
    table = []
    for step in range(steps):
        if step < 2:
            table += [jnp.clip(step - near_end, 0, chunks - 1), jnp.int32(0)] * 2
        elif step == steps - 1:
            table += [jnp.int32(chunks - 1), low_flag] * 2
        else:
            for behind in behinds:
                table += [jnp.clip(step - behind, 0, chunks - 1), jnp.int32(0)]
    table = jnp.stack([jnp.asarray(entry).astype(I32) for entry in table])
    for step in range(steps):
        early, late = max(step - tok_count + 1, 0) * GROUP, min(step, chunks - 1) * GROUP + GROUP - 1
        wanted = [parts[0] if early < HIGH else None, parts[1] if late >= LOW else None]
        if step == 0:
            packet = stage(table, 0, spot, [], wanted, after)
            came = lax.ppermute(packet, "tok", [(0, 1), (last, last - 1)])
            from_below.append(came)
            from_above.append(came)
            after = [packet]
        elif step == 1:
            packet = stage(table, 2, spot, [from_below[-1]], wanted, after)
            from_below.append(lax.ppermute(packet, "tok", up[:2]))
            from_above.append(lax.ppermute(packet, "tok", down[-2:]))
            after = [packet]
        elif step == steps - 1:
            got = [from_below[-1], from_above[-1]]
            packet = stage(table, 2 * step, spot, got, [None, parts[1]], after)
            came = lax.ppermute(packet, "tok", [(last - 1, last), (1, 0)])
            from_below.append(came)
            from_above.append(came)
            after = [packet]
        else:
            for way, (got, pairs) in enumerate(((from_below, up), (from_above, down))):
                packet = stage(table, 2 * step + way, spot, got[-1:], wanted, after)
                got.append(lax.ppermute(packet, "tok", pairs))
                after = [packet]
        if step < steps - 1 and needs.get(done, -1) < step:
            for item in fillers[done]:
                after = [item(after)]
            done += 1
    for items in fillers[done:]:
        for item in items:
            after = [item(after)]
    sums = [over_line([over_plane(sent[:2]), over_plane(sent[2:])])]

    own_place = lax.dynamic_index_in_dim(place, x, 0)
    own_first = lax.dynamic_index_in_dim(first, x, 0)
    return final([groups], own_first, own_place, own_slot, sums).T


def solution(mesh):
    placed = (
        P(("grp", "tok"), None),
        P(("grp", "tok"), None),
        P("grp", None),
        P("grp", "tok"),
        P("grp", "tok"),
        P("grp", None),
        P(None, "tok", ("fac", "sub")),
        P(None, "tok", ("fac", "sub")),
        P(None, ("fac", "sub")),
        P(None, ("fac", "sub")),
    )
    return jax.shard_map(
        body, mesh=mesh, in_specs=placed, out_specs=P("fac", ("grp", "tok", "sub")), check_vma=False
    )
```

```python
import functools
import math

import jax
import jax.numpy as jnp
from jax import lax
from jax.experimental import pallas as pl
from jax.experimental.pallas import tpu as pltpu
from jax.sharding import PartitionSpec as P

D = 5120
FH = 13824
DAMPING = 0.25
CHUNKS = 8
LOW, HIGH = 3 * CHUNKS // 8, 5 * CHUNKS // 8
LARGEST = 32760.0
TO_WHOLE = 1.5 * 2.0**23
LANES = 128
TILE = 512
SEGMENT = 4 * TILE
GROUP = 2
ROWS = 64
STAGE_MIB = (57, 20)
QUERY_MIB = (63, 34)
PACK_MIB = 34
SIDE_MIB = (63, 63)
MIB = 1 << 20
F32 = jnp.float32
BF16 = jnp.bfloat16
I32 = jnp.int32
FINE = 8.0 / math.log(2.0)
IN_HBM = pl.BlockSpec(memory_space=pltpu.HBM)
ANYWHERE = pl.BlockSpec(memory_space=pl.ANY)
SCALARS = pl.BlockSpec(memory_space=pltpu.SMEM)
WHOLE = pl.BlockSpec(memory_space=pltpu.VMEM)


def up_to(n, m):
    return -(-n // m) * m


def params(mib=34, slots=0):
    return pltpu.CompilerParams(vmem_limit_bytes=(mib if slots <= 512 else 63) * MIB)


def turn(count, step):
    return [(i, (i + step) % count) for i in range(count)]


def query_kernel(fac, rows, first, tiles, place_ref, feat_g_ref, feat_a_ref, basis_g_ref, basis_a_ref, *refs):
    out_g_ref, out_a_ref, sorted_g_ref, sorted_a_ref = refs[-4:]
    block = place_ref.shape[1]
    unit = fac * rows

    def put(feat_ref, sorted_ref):
        for f in range(fac):
            spots = lax.broadcasted_iota(I32, (HIGH * rows, block), 0) + first * rows
            order = (spots == place_ref[f : f + 1, :]).astype(F32).astype(BF16)
            moved = jnp.dot(
                order, feat_ref[f * block : (f + 1) * block, :], preferred_element_type=F32
            ).astype(BF16)
            for j in range(HIGH):
                sorted_ref[j * unit + f * rows : j * unit + (f + 1) * rows, :] = moved[
                    j * rows : (j + 1) * rows, :
                ]

    step = pl.program_id(0)

    @pl.when(step == 0)
    def _():
        put(feat_g_ref, sorted_g_ref)

    @pl.when(step == tiles)
    def _():
        put(feat_a_ref, sorted_a_ref)

    @pl.when(step < tiles)
    def _():
        out_g_ref[...] = jnp.dot(sorted_g_ref[...], basis_g_ref[0], preferred_element_type=F32)

    @pl.when(step >= tiles)
    def _():
        out_a_ref[...] = jnp.dot(sorted_a_ref[...], basis_a_ref[0], preferred_element_type=F32)


def query_coords(klass, place, feat_g, feat_a, basis_g, basis_a, fac, rows, after=()):
    queries, deep_g = feat_g.shape
    deep_a = feat_a.shape[1]
    width_g, width_a = basis_g.shape[2], basis_a.shape[2]
    tile_g, tile_a = min(TILE, width_g), min(TILE, width_a)
    tiles_g, tiles_a = pl.cdiv(width_g, tile_g), pl.cdiv(width_a, tile_a)
    count = HIGH * fac * rows
    at_g = lambda i: jnp.minimum(i, tiles_g - 1)
    at_a = lambda i: jnp.maximum(i - tiles_g, 0)
    return pl.pallas_call(
        functools.partial(query_kernel, fac, rows, (0, LOW)[klass], tiles_g),
        grid=(tiles_g + tiles_a,),
        in_specs=[
            pl.BlockSpec(place.shape, lambda i: (0, 0)),
            pl.BlockSpec((queries, deep_g), lambda i: (0, 0)),
            pl.BlockSpec((queries, deep_a), lambda i: (0, 0)),
            pl.BlockSpec((1, deep_g, tile_g), lambda i: (klass, 0, at_g(i))),
            pl.BlockSpec((1, deep_a, tile_a), lambda i: (klass, 0, at_a(i))),
        ]
        + [ANYWHERE] * len(after),
        out_specs=[
            pl.BlockSpec((count, tile_g), lambda i: (0, at_g(i))),
            pl.BlockSpec((count, tile_a), lambda i: (0, at_a(i))),
        ],
        out_shape=[jax.ShapeDtypeStruct((count, width), F32) for width in (width_g, width_a)],
        scratch_shapes=[pltpu.VMEM((count, deep), BF16) for deep in (deep_g, deep_a)],
        compiler_params=params(QUERY_MIB[klass]),
        name="query_coords",
    )(place, feat_g, feat_a, basis_g, basis_a, *after)


def join_kernel(count, *refs):
    sources, out_ref, sems = refs[:count], refs[-2], refs[-1]
    size = sources[0].shape[0]
    copies = [
        pltpu.make_async_copy(ref, out_ref.at[pl.ds(i * size, size), :], sems.at[i])
        for i, ref in enumerate(sources)
    ]
    for copy in copies:
        copy.start()
    for copy in copies:
        copy.wait()


def join(blocks, after):
    size, width = blocks[0].shape
    return pl.pallas_call(
        functools.partial(join_kernel, len(blocks)),
        in_specs=[ANYWHERE] * (len(blocks) + len(after)),
        out_specs=WHOLE,
        out_shape=jax.ShapeDtypeStruct((size * len(blocks), width), BF16),
        scratch_shapes=[pltpu.SemaphoreType.DMA((len(blocks),))],
        compiler_params=params(),
        name="join_tokens",
    )(*blocks, *after)


def pack_kernel(counts, slots, room, at_ref, slot_ref, *refs):
    tok, sub, fac = counts
    raws = refs[: sub * fac]
    g_ref, a_ref, made_g, made_a, raw_ref, sems, out_sems = refs[-7:]
    size = raws[0].shape[0]
    copies = [
        pltpu.make_async_copy(ref, raw_ref.at[pl.ds(i * size, size), :], sems.at[i])
        for i, ref in enumerate(raws)
    ]
    for copy in copies:
        copy.start()
    here = []
    for s in range(sub):
        for f in range(fac):
            for k in range(tok):
                row = lax.rem(at_ref[0] + tok - k, tok) * sub + lax.rem(at_ref[1] + sub - s, sub)
                row = row * fac + lax.rem(at_ref[2] + fac - f, fac)
                here.append(slot_ref[pl.ds(row, 1), :])
    here = jnp.concatenate(here, axis=1)
    for copy in copies:
        copy.wait()
    outs = []
    for klass in range(2):
        table = lax.broadcasted_iota(I32, (slots, here.shape[1]), 0) + klass * slots == here
        table = table.astype(F32).astype(BF16)
        for side, (ref, made, begin) in enumerate(((g_ref, made_g, 0), (a_ref, made_a, room))):
            made[klass] = jnp.dot(
                table, raw_ref[:, begin : begin + ref.shape[2]], preferred_element_type=F32
            ).astype(BF16)
            out = pltpu.make_async_copy(made.at[klass], ref.at[klass], out_sems.at[klass, side])
            out.start()
            outs.append(out)
    for out in outs:
        out.wait()


def pack(counts, at, slot, raws, slots, deep_g, deep_a, after):
    size, width = raws[0].shape
    return pl.pallas_call(
        functools.partial(pack_kernel, counts, slots, up_to(deep_g, LANES)),
        in_specs=[SCALARS, WHOLE] + [ANYWHERE] * (len(raws) + len(after)),
        out_specs=[ANYWHERE, ANYWHERE],
        out_shape=[jax.ShapeDtypeStruct((2, slots, deep), BF16) for deep in (deep_g, deep_a)],
        scratch_shapes=[
            pltpu.VMEM((2, slots, deep_g), BF16),
            pltpu.VMEM((2, slots, deep_a), BF16),
            pltpu.VMEM((size * len(raws), width), BF16),
            pltpu.SemaphoreType.DMA((len(raws),)),
            pltpu.SemaphoreType.DMA((2, 2)),
        ],
        compiler_params=params(PACK_MIB, slots),
        name="pack_tokens",
    )(at, slot, *raws, *after)


def token_kernel(packed_ref, eigen_ref, basis_ref, *refs):
    high_ref, low_ref = refs[-2:]
    for klass in range(2):
        coords = (
            jnp.dot(packed_ref[klass], basis_ref[klass], preferred_element_type=F32)
            / (eigen_ref[klass : klass + 1, :] + DAMPING)
        )
        high = coords.astype(BF16)
        high_ref[klass] = high
        low_ref[klass] = (coords - high.astype(F32)).astype(BF16)


def token_coords(packed, eigen, basis, column, segment, after):
    slots = packed.shape[1]
    deep, width = basis.shape[1:]
    here = min(segment, width - column)
    tile = min(TILE, width)
    base = column // tile
    out = jax.ShapeDtypeStruct((2, slots, here), BF16)
    return pl.pallas_call(
        token_kernel,
        grid=(pl.cdiv(here, tile),),
        in_specs=[
            pl.BlockSpec((2, slots, deep), lambda i: (0, 0, 0)),
            pl.BlockSpec((2, tile), lambda i: (0, base + i)),
            pl.BlockSpec((2, deep, tile), lambda i: (0, 0, base + i)),
        ]
        + [ANYWHERE] * len(after),
        out_specs=[pl.BlockSpec((2, slots, tile), lambda i: (0, 0, i))] * 2,
        out_shape=[out, out],
        compiler_params=params(slots=slots),
        name="token_coords",
    )(packed, eigen, basis, *after)


def tiles_of(width):
    return [(begin, min(LANES, width - begin)) for begin in range(0, width, LANES)]


def scaled(x):
    top = jnp.max(jnp.abs(x), axis=1, keepdims=True)
    code = jnp.ceil(jnp.log(jnp.maximum(top, 1e-30)) * FINE)
    factor = LARGEST * jnp.exp(code * (-1.0 / FINE))
    return (x * factor + TO_WHOLE) - TO_WHOLE, code


def narrow(x):
    return x.astype(I32).astype(jnp.int16)


def wide(x):
    return x.astype(I32).astype(F32)


def steps_of(ref, tail):
    step = jnp.exp(wide(ref[:, tail : tail + LANES]) * (1.0 / FINE)) * (1.0 / LARGEST)
    shape = step.shape
    return (
        jnp.broadcast_to(step[:, 0:1], shape),
        jnp.broadcast_to(step[:, LANES - 1 : LANES], shape),
    )


def stage_kernel(row_at, gots, parts, after, at_ref, spot_ref, *refs):
    sources, refs = refs[:gots], refs[gots:]
    use = [k for k in range(2) if parts[k]]
    part = {k: (refs[2 * i], refs[2 * i + 1]) for i, k in enumerate(use)}
    refs = refs[2 * len(use) + after :]
    out_ref, refs = refs[0], refs[1:]
    held = {k: (refs[2 * i], refs[2 * i + 1]) for i, k in enumerate(use)}
    got_ref, made_ref, sems = refs[2 * len(use) :]
    chunk, which, heed = (at_ref[row_at + i] for i in range(3))
    size = ROWS
    blocks = out_ref.shape[0] // size
    per_unit = blocks // GROUP
    width_g, width_a = (ref.shape[1] for ref in part[use[0]])
    room = up_to(width_g, LANES)
    tail = room + up_to(width_a, LANES)

    def received(b, source):
        at = pl.ds(b * size, size)
        return pltpu.make_async_copy(source.at[at, :], got_ref.at[at, :], sems.at[b, 4])

    def each(b, act, first):
        if gots == 1 or (gots and not first):
            act(received(b, sources[0]))
        elif gots:
            for i in range(2):

                @pl.when(which == i)
                def _():
                    act(received(b, sources[i]))

        unit = chunk * GROUP + b // per_unit
        for k in use:
            row = pl.multiple_of(((unit - (0, LOW)[k]) * per_unit + b % per_unit) * size, size)

            def go():
                for side in range(2):
                    act(
                        pltpu.make_async_copy(
                            part[k][side].at[pl.ds(row, size), :],
                            held[k][side].at[pl.ds(b * size, size), :],
                            sems.at[b, 2 * k + side],
                        )
                    )

            if len(use) == 1:
                go()
            else:
                pl.when((unit < HIGH) if k == 0 else (unit >= LOW))(go)

    def sent(b):
        at = pl.ds(b * size, size)
        return pltpu.make_async_copy(made_ref.at[at, :], out_ref.at[at, :], sems.at[b, 5])

    for b in range(blocks):
        each(b, lambda copy: copy.start(), True)
    for b in range(blocks):
        each(b, lambda copy: copy.wait(), False)
        at = slice(b * size, (b + 1) * size)
        if len(use) == 1:
            x_g, x_a = (ref[at, :] for ref in held[use[0]])
        else:
            of_zero = spot_ref[at, :] > 0
            x_g, x_a = (jnp.where(of_zero, held[0][i][at, :], held[1][i][at, :]) for i in range(2))
        if gots:
            step = jnp.exp(wide(got_ref[at, tail : tail + LANES]) * (1.0 / FINE)) * (1.0 / LARGEST)
            step = jnp.where(heed > 0, step, 0.0)
            x_g = x_g + wide(got_ref[at, :width_g]) * step[:, 0:1]
            x_a = x_a + wide(got_ref[at, room : room + width_a]) * step[:, LANES - 1 : LANES]
        q_g, code_g = scaled(x_g)
        q_a, code_a = scaled(x_a)
        if room != width_g or tail != room + width_a:
            made_ref[at, :] = jnp.zeros((size, made_ref.shape[1]), jnp.int16)
        made_ref[at, :width_g] = narrow(q_g)
        made_ref[at, room : room + width_a] = narrow(q_a)
        lane = lax.broadcasted_iota(I32, (size, LANES), 1)
        made_ref[at, tail:] = narrow(jnp.where(lane < LANES // 2, code_g, code_a))
        sent(b).start()
    for b in range(blocks):
        sent(b).wait()


def stage(table, number, spot, got, parts, after):
    use = [part for part in parts if part is not None]
    width_g, width_a = use[0][0].shape[1], use[0][1].shape[1]
    unit = use[0][0].shape[0] // HIGH * GROUP
    packet = up_to(width_g, LANES) + up_to(width_a, LANES) + LANES
    flat = [array for part in use for array in part]
    row_at = 3 * number
    return pl.pallas_call(
        functools.partial(
            stage_kernel, row_at, len(got), tuple(part is not None for part in parts), len(after)
        ),
        grid_spec=pltpu.PrefetchScalarGridSpec(
            num_scalar_prefetch=1,
            grid=(1,),
            in_specs=[pl.BlockSpec((unit, 1), lambda i, c: (c[row_at], 0))]
            + [ANYWHERE] * len(got)
            + [IN_HBM] * len(flat)
            + [ANYWHERE] * len(after),
            out_specs=ANYWHERE,
            scratch_shapes=[pltpu.VMEM((unit, array.shape[1]), F32) for array in flat]
            + [pltpu.VMEM((unit, packet), jnp.int16)] * 2
            + [pltpu.SemaphoreType.DMA((unit // ROWS, 6))],
        ),
        out_shape=jax.ShapeDtypeStruct((unit, packet), jnp.int16),
        compiler_params=params(STAGE_MIB[min(number, 1)]),
        name="running_sum",
    )(table, spot, *got, *flat, *after)


def side_kernel(plan, counts, z_ref, spot_ref, *refs):
    units, spans, hops, segments, after = plan
    tok, sub, fac = counts
    refs = list(refs)

    def take(n):
        out, refs[:n] = refs[:n], []
        return out

    chunks = sorted({u // GROUP for u in units})
    below = {c: take(hops) for c in chunks}
    above = {c: take(hops) for c in chunks}
    needs = {u: [k for k in (0, 1) if (u < HIGH, u >= LOW)[k]] for u in units}
    part = {k: take(2) for k in (0, 1) if any(k in needs[u] for u in units)}
    pieces = [take(2) for _ in segments]
    take(after)
    out_refs = take(sub)
    held_g, held_a, got, x_g, x_a, sums_ref = take(6)
    tables = take(len(segments))
    sems, piece_sems = take(2)
    held = (held_g, held_a)
    width_g, width_a = x_g.shape[1], x_a.shape[1]
    unit = got.shape[2]
    rows = unit // fac
    slots = pieces[0][0].shape[1]
    cap = slots // (tok * sub)
    room = up_to(width_g, LANES)
    tail = room + up_to(width_a, LANES)
    lanes = out_refs[0].shape[-1] // 2
    z, core, at_x = z_ref[2], z_ref[3], z_ref[4]
    spot_of = {}
    for u in units:
        for k in needs[u]:
            spot_of[u, k] = len(spot_of)

    def own(i, u):
        return [
            pltpu.make_async_copy(
                part[k][side].at[pl.ds((u - (0, LOW)[k]) * unit, unit), :],
                held[side].at[spot_of[u, k]],
                sems.at[i, 2 * k + side],
            )
            for k in needs[u]
            for side in range(2)
        ]

    def arrived(i, u, way, hop):
        source = (below, above)[way][u // GROUP][hop]
        return pltpu.make_async_copy(
            source.at[pl.ds(u % GROUP * unit, unit), :], got.at[way, i], sems.at[i, 4 + way]
        )

    for i, u in enumerate(units):
        for copy in own(i, u):
            copy.start()
        for way in range(2):
            for hop in range(hops):
                cut = (z_ref[way] <= 1) if hop == 0 else (z_ref[way] == hop + 1)

                @pl.when(cut)
                def _():
                    arrived(i, u, way, hop).start()

    copies = [
        pltpu.make_async_copy(
            pieces[s][half].at[klass],
            tables[s].at[c, pl.ds(half * slots, slots), :],
            piece_sems.at[s, 2 * c + half],
        )
        for c, (klass, _) in enumerate(spans)
        for s in range(len(segments))
        for half in range(2)
    ]
    for copy in copies:
        copy.start()
    for i, u in enumerate(units):
        for copy in own(i, u):
            copy.wait()
        for way in range(2):
            arrived(i, u, way, 0).wait()
        below_steps, above_steps = (
            tuple(jnp.where(z_ref[way] > 0, step, 0.0) for step in steps_of(got.at[way, i], tail))
            for way in range(2)
        )
        if len(needs[u]) == 2:
            of_zero = jnp.broadcast_to(spot_ref[u * unit : (u + 1) * unit, :], (unit, LANES)) > 0
        for side, (ref, own_ref) in enumerate(((x_g, held_g), (x_a, held_a))):
            for begin, wide_by in tiles_of(ref.shape[1]):
                cut = slice(begin, begin + wide_by)
                there = slice((0, room)[side] + begin, (0, room)[side] + begin + wide_by)
                full = own_ref[spot_of[u, needs[u][0]], :, cut]
                if len(needs[u]) == 2:
                    full = jnp.where(of_zero[:, :wide_by], full, own_ref[spot_of[u, 1], :, cut])
                full = full + wide(got[0, i, :, there]) * below_steps[side][:, :wide_by]
                full = full + wide(got[1, i, :, there]) * above_steps[side][:, :wide_by]
                high = full.astype(BF16)
                ref[2 * i * unit : (2 * i + 1) * unit, cut] = high
                ref[(2 * i + 1) * unit : (2 * i + 2) * unit, cut] = (full - high.astype(F32)).astype(BF16)

    for copy in copies:
        copy.wait()
    dims = (((1,), (1,)), ((), ()))
    lane = 0
    for c, (klass, members) in enumerate(spans):
        first = units.index(members[0])
        span = slice(2 * first * unit, 2 * (first + len(members)) * unit)
        total = [None, None]
        for s, (side, begin, width) in enumerate(segments):
            x = (x_g, x_a)[side]
            term = lax.dot_general(
                tables[s][c], x[span, begin : begin + width], dims, preferred_element_type=F32
            )
            total[side] = term if total[side] is None else total[side] + term
        for side in range(2):
            sums = total[side][:slots] + total[side][slots:]
            for i in range(len(members)):
                of_unit = (
                    sums[:, 2 * i * unit : (2 * i + 1) * unit] + sums[:, (2 * i + 1) * unit : (2 * i + 2) * unit]
                )
                sums_ref[...] = of_unit
                left = side * lanes + lane + i * rows
                for zz in range(tok):
                    to = lax.rem(zz + tok - z, tok)
                    for s in range(sub):
                        begin = (zz * sub + lax.rem(core + s, sub)) * cap
                        block = sums_ref[pl.ds(pl.multiple_of(begin, 8), cap), :]
                        for f in range(fac):
                            out_refs[s][lax.rem(f + fac - at_x, fac), to, :, left : left + rows] = block[
                                :, f * rows : (f + 1) * rows
                            ]
        lane += len(members) * rows


def sides(counts, where_z, spot, units, spans, parts, first_got, second_got, pieces, after):
    tok, sub, fac = counts
    hops = tok - 1
    packet = first_got[0].shape[1]
    unit = first_got[0].shape[0] // GROUP
    segments = tuple((side, begin, array[0].shape[2]) for side, begin, array in pieces)
    slots = pieces[0][2][0].shape[1]
    needs = [[k for k in (0, 1) if (u < HIGH, u >= LOW)[k]] for u in units]
    used = [array for k in (0, 1) if any(k in some for some in needs) for array in parts[k]]
    width_g, width_a = parts[0][0].shape[1], parts[0][1].shape[1]
    chunks = sorted({u // GROUP for u in units})
    near = [array for c in chunks for array in first_got[c : c + hops]]
    near += [array for c in chunks for array in second_got[c : c + hops]]
    flat = [array for _, _, pair in pieces for array in pair]
    lanes = sum(len(members) for _, members in spans) * (unit // fac)
    owns = sum(len(some) for some in needs)
    many = 2 * len(units) * unit
    return pl.pallas_call(
        functools.partial(side_kernel, (units, spans, hops, segments, len(after)), counts),
        in_specs=[SCALARS, WHOLE]
        + [ANYWHERE] * len(near)
        + [IN_HBM] * (len(used) + len(flat))
        + [ANYWHERE] * len(after),
        out_specs=[WHOLE] * sub,
        out_shape=[jax.ShapeDtypeStruct((fac, tok, slots // (tok * sub), 2 * lanes), F32)] * sub,
        scratch_shapes=[
            pltpu.VMEM((owns, unit, width_g), F32),
            pltpu.VMEM((owns, unit, width_a), F32),
            pltpu.VMEM((2, len(units), unit, packet), jnp.int16),
            pltpu.VMEM((many, width_g), BF16),
            pltpu.VMEM((many, width_a), BF16),
            pltpu.VMEM((slots, unit), F32),
        ]
        + [pltpu.VMEM((len(spans), 2 * slots, width), BF16) for _, _, width in segments]
        + [
            pltpu.SemaphoreType.DMA((len(units), 6)),
            pltpu.SemaphoreType.DMA((len(segments), 2 * len(spans))),
        ],
        compiler_params=params(SIDE_MIB[min(units[0] // 4, 1)], slots),
        name="side_sums",
    )(where_z, spot, *near, *used, *flat, *after)


def final_kernel(groups, hops, first_ref, place_ref, slot_ref, *refs):
    out_ref = refs[-1]
    columns = [[], []]
    for i, batches in enumerate(groups):
        total = refs[i * hops][...]
        for hop in range(1, hops):
            total = total + refs[i * hops + hop][...]
        at = 0
        for runs in batches:
            lanes = sum(run for _, run in runs)
            scores = total[:, at : at + lanes] * total[:, at + lanes : at + 2 * lanes]
            scores = scores * (1.0 / math.sqrt(FH * D))
            at += 2 * lanes
            here = 0
            for klass, run in runs:
                columns[klass].append(scores[:, here : here + run])
                here += run
    cap = columns[0][0].shape[0]
    half_rows, block = out_ref.shape
    result = jnp.zeros((half_rows, block), F32)
    for klass in range(2):
        scores = jnp.concatenate(columns[klass], axis=1)
        count = scores.shape[1]
        begin = (0, LOW * (count // HIGH))[klass]
        row = lax.broadcasted_iota(I32, (count, block), 0) + begin
        of_class = (row < first_ref[0]) if klass == 0 else (row >= first_ref[0])
        to_query = ((place_ref[...] == row) & of_class).astype(F32)
        to_token = (lax.broadcasted_iota(I32, (half_rows, cap), 1) + klass * cap == slot_ref[...]).astype(F32)
        by_query = jnp.dot(scores, to_query, precision=lax.Precision.HIGHEST, preferred_element_type=F32)
        result = result + jnp.dot(
            to_token, by_query, precision=lax.Precision.HIGHEST, preferred_element_type=F32
        )
    out_ref[...] = result


def final(groups, first, place, slot, sums):
    hops = len(sums[0])
    return pl.pallas_call(
        functools.partial(final_kernel, groups, hops),
        in_specs=[SCALARS] + [WHOLE] * (2 + hops * len(sums)),
        out_specs=WHOLE,
        out_shape=jax.ShapeDtypeStruct((slot.shape[0], place.shape[1]), F32),
        compiler_params=params(),
        name="place_scores",
    )(first, place, slot, *[array for arrays in sums for array in arrays])


def body(
    activations,
    gradients,
    tok_class,
    query_inputs,
    query_gradients,
    query_class,
    basis_a,
    basis_g,
    eigen_a,
    eigen_g,
):
    deep_g, width_g = basis_g.shape[1:]
    deep_a, width_a = basis_a.shape[1:]
    counts = tok_count, sub_count, fac_count = tuple(lax.axis_size(a) for a in ("tok", "sub", "fac"))
    z, core, x = (lax.axis_index(a) for a in ("tok", "sub", "fac"))
    block = query_inputs.shape[0] // fac_count
    rows = block // CHUNKS
    tok_rows = activations.shape[0]
    half_rows = tok_rows // sub_count
    slot_cap = 5 * half_rows // 8
    share = half_rows // fac_count
    halves = tok_count * sub_count
    slots = halves * slot_cap
    token_ids = tok_class[:, 0]
    query_ids = query_class[:, 0]

    at = (core * fac_count + x) * share
    room = up_to(deep_g, LANES)
    blocks = []
    for step in range(tok_count):
        to = lax.rem(z + step, tok_count)
        blocks.append(
            jnp.concatenate(
                [
                    lax.dynamic_slice(gradients, (at, to * deep_g), (share, deep_g)),
                    jnp.zeros((share, room - deep_g), BF16),
                    lax.dynamic_slice(activations, (at, to * deep_a), (share, deep_a)),
                ],
                axis=1,
            )
        )
    moved = [blocks[0]] + [
        lax.ppermute(blocks[step], "tok", turn(tok_count, step)) for step in range(1, tok_count)
    ]

    qids = query_ids.reshape(fac_count, block)
    key = qids * block + jnp.arange(block)
    place = jnp.sum((key[:, None, :] < key[:, :, None]).astype(I32), axis=2)
    first = jnp.sum((qids == 0).astype(I32), axis=1)
    spot = (jnp.arange(CHUNKS)[:, None, None] * rows + jnp.arange(rows)) < first[None, :, None]
    spot = spot.reshape(query_ids.shape[0], 1).astype(I32)
    features = (query_gradients, query_inputs, basis_g, basis_a, fac_count, rows)
    parts = [query_coords(0, place, *features, blocks[1:]), None]

    ids = token_ids.reshape(halves, half_rows)
    earlier = jnp.arange(half_rows)[None, :] < jnp.arange(half_rows)[:, None]
    rank = jnp.sum(((ids[:, None, :] == ids[:, :, None]) & earlier).astype(I32), axis=2)
    slot = ids * slots + jnp.arange(halves)[:, None] * slot_cap + rank
    slot = slot.reshape(halves * fac_count, share)
    own_slot = lax.dynamic_index_in_dim(ids * slot_cap + rank, z * sub_count + core, 0).reshape(half_rows, 1)
    places = jnp.stack([z, core, x]).astype(I32)
    last = tok_count - 1
    behinds = (jnp.where(core == 0, z, last - z), jnp.where(core == 0, last - z, z))
    where_z = jnp.stack([*behinds, z, core, x]).astype(I32)

    state = {"pieces": []}

    def second(after):
        parts[1] = query_coords(1, place, *features, after)
        return parts[1][1]

    def joined(after):
        mine = join(moved, after)
        raws = [mine]
        for step in range(1, fac_count):
            raws.append(lax.ppermute(mine, "fac", turn(fac_count, step)))
        for step in range(1, sub_count):
            raws += [lax.ppermute(raw, "sub", turn(sub_count, step)) for raw in raws[:fac_count]]
        state["raws"] = raws
        return mine

    def packed(after):
        state["packed"] = pack(counts, places, slot, state["raws"], slots, deep_g, deep_a, after)
        return state["packed"][0]

    def token(side, column):
        def run(after):
            eigen, basis = ((eigen_g, basis_g), (eigen_a, basis_a))[side]
            segment = SEGMENT if side == 0 else width_a
            pair = token_coords(state["packed"][side], eigen, basis, column, segment, after)
            state["pieces"].append((side, column, pair))
            return pair[0]

        return run

    first_got, second_got = [], []
    groups, sent = [], []

    def batch(units, spans):
        def run(after):
            out = sides(
                counts, where_z, spot, units, spans, parts, first_got, second_got, state["pieces"], after
            )
            groups.append(tuple((klass, len(members) * rows) for klass, members in spans))
            sent.append(out)
            return out[0]

        return run

    columns = list(range(0, width_g, SEGMENT))
    fillers = [[joined, second], [packed, token(1, 0)]]
    fillers += [[token(0, column)] for column in columns]
    needs = {}
    for units in (range(4), range(4, 6), range(6, 8)):
        spans = [(k, [u for u in units if (u < HIGH, u >= LOW)[k]]) for k in range(2)]
        needs[len(fillers)] = units[-1] // GROUP + tok_count - 2
        fillers.append([batch(list(units), [span for span in spans if span[1]])])

    def over_plane(batches):
        totals = []
        for own, *others in batches:
            for step, other in enumerate(others, 1):
                own = own + lax.ppermute(other, "sub", turn(sub_count, step))
            totals.append(own)
        whole = totals[0] if len(totals) == 1 else jnp.concatenate(totals, axis=-1)
        total = whole[0]
        for step in range(1, fac_count):
            total = total + lax.ppermute(whole[step], "fac", turn(fac_count, step))
        return total

    def over_line(totals):
        whole = jnp.concatenate(totals, axis=-1)
        return [whole[0]] + [
            lax.ppermute(whole[step], "tok", turn(tok_count, step)) for step in range(1, tok_count)
        ]

    at_of = lambda chip, half: chip * sub_count + half
    rounds = []
    for upward in range(2):
        other = 1 - upward
        pairs = [(at_of(i, upward), at_of(i + 1, upward)) for i in range(last)]
        pairs += [(at_of(i + 1, other), at_of(i, other)) for i in range(last)]
        rounds.append(pairs + [(at_of(last, upward), at_of(last, other)), (at_of(0, other), at_of(0, upward))])
    swap = [(0, 1), (1, 0), (last, last - 1), (last - 1, last)]
    after = []
    chunks = CHUNKS // GROUP
    steps = chunks + tok_count - 2
    done = 0
    near_end = jnp.minimum(z, last - z)
    from_upper = (z >= tok_count // 2) == (core == 0)
    table = []
    for step in range(steps):
        if step < 2:
            table += [jnp.clip(step - near_end, 0, chunks - 1), jnp.int32(0), near_end] * 2
        elif step == steps - 1:
            table += [jnp.int32(chunks - 1), jnp.where(from_upper, 0, 1), jnp.int32(1)] * 2
        else:
            for behind in behinds:
                table += [jnp.clip(step - behind, 0, chunks - 1), jnp.int32(0), behind]
    table = jnp.stack([jnp.asarray(entry).astype(I32) for entry in table])
    for step in range(steps):
        early, late = max(step - tok_count + 1, 0) * GROUP, min(step, chunks - 1) * GROUP + GROUP - 1
        wanted = [parts[0] if early < HIGH else None, parts[1] if late >= LOW else None]
        if step == 0:
            packet = stage(table, 0, spot, [], wanted, after)
            came = lax.ppermute(packet, "tok", swap)
            first_got.append(came)
            second_got.append(came)
            after = [packet]
        elif step == 1:
            packet = stage(table, 2, spot, [first_got[-1]], wanted, after)
            first_got.append(lax.ppermute(packet, ("tok", "sub"), rounds[0]))
            second_got.append(lax.ppermute(packet, ("tok", "sub"), rounds[1]))
            after = [packet]
        elif step == steps - 1:
            got = [first_got[-1], second_got[-1]]
            packet = stage(table, 2 * step, spot, got, [None, parts[1]], after)
            came = lax.ppermute(packet, "tok", swap)
            first_got.append(came)
            second_got.append(came)
            after = [packet]
        else:
            for way, (got, pairs) in enumerate(((first_got, rounds[0]), (second_got, rounds[1]))):
                packet = stage(table, 2 * step + way, spot, got[-1:], wanted, after)
                got.append(lax.ppermute(packet, ("tok", "sub"), pairs))
                after = [packet]
        if step < steps - 1 and needs.get(done, -1) < step:
            for item in fillers[done]:
                after = [item(after)]
            done += 1
    for items in fillers[done:]:
        for item in items:
            after = [item(after)]
    sums = [over_line([over_plane(sent[:2]), over_plane(sent[2:])])]

    own_place = lax.dynamic_index_in_dim(place, x, 0)
    own_first = lax.dynamic_index_in_dim(first, x, 0)
    return final([groups], own_first, own_place, own_slot, sums).T


def solution(mesh):
    placed = (
        P(("grp", "tok"), None),
        P(("grp", "tok"), None),
        P("grp", None),
        P("grp", "tok"),
        P("grp", "tok"),
        P("grp", None),
        P(None, "tok", ("fac", "sub")),
        P(None, "tok", ("fac", "sub")),
        P(None, ("fac", "sub")),
        P(None, ("fac", "sub")),
    )
    return jax.shard_map(
        body, mesh=mesh, in_specs=placed, out_specs=P("fac", ("grp", "tok", "sub")), check_vma=False
    )
```

```python
import functools
import math

import jax
import jax.numpy as jnp
from jax import lax
from jax.experimental import pallas as pl
from jax.experimental.pallas import tpu as pltpu
from jax.sharding import PartitionSpec as P

D = 5120
FH = 13824
DAMPING = 0.25
CHUNKS = 8
LOW, HIGH = 3 * CHUNKS // 8, 5 * CHUNKS // 8
LARGEST = 32760.0
TO_WHOLE = 1.5 * 2.0**23
LANES = 128
TILE = 512
SEGMENT = 4 * TILE
GROUP = 2
ROWS = 64
STAGE_MIB = (57, 20)
QUERY_MIB = (63, 34)
PACK_MIB = 34
SIDE_MIB = (63, 63)
MIB = 1 << 20
F32 = jnp.float32
BF16 = jnp.bfloat16
I32 = jnp.int32
FINE = 8.0 / math.log(2.0)
IN_HBM = pl.BlockSpec(memory_space=pltpu.HBM)
ANYWHERE = pl.BlockSpec(memory_space=pl.ANY)
SCALARS = pl.BlockSpec(memory_space=pltpu.SMEM)
WHOLE = pl.BlockSpec(memory_space=pltpu.VMEM)


def up_to(n, m):
    return -(-n // m) * m


def params(mib=34, slots=0):
    return pltpu.CompilerParams(vmem_limit_bytes=(mib if slots <= 512 else 63) * MIB)


def turn(count, step):
    return [(i, (i + step) % count) for i in range(count)]


def query_kernel(fac, rows, first, tiles, place_ref, feat_g_ref, feat_a_ref, basis_g_ref, basis_a_ref, *refs):
    out_g_ref, out_a_ref, sorted_g_ref, sorted_a_ref = refs[-4:]
    block = place_ref.shape[1]
    unit = fac * rows

    def put(feat_ref, sorted_ref):
        for f in range(fac):
            spots = lax.broadcasted_iota(I32, (HIGH * rows, block), 0) + first * rows
            order = (spots == place_ref[f : f + 1, :]).astype(F32).astype(BF16)
            moved = jnp.dot(
                order, feat_ref[f * block : (f + 1) * block, :], preferred_element_type=F32
            ).astype(BF16)
            for j in range(HIGH):
                sorted_ref[j * unit + f * rows : j * unit + (f + 1) * rows, :] = moved[
                    j * rows : (j + 1) * rows, :
                ]

    step = pl.program_id(0)

    @pl.when(step == 0)
    def _():
        put(feat_g_ref, sorted_g_ref)

    @pl.when(step == tiles)
    def _():
        put(feat_a_ref, sorted_a_ref)

    @pl.when(step < tiles)
    def _():
        out_g_ref[...] = jnp.dot(sorted_g_ref[...], basis_g_ref[0], preferred_element_type=F32)

    @pl.when(step >= tiles)
    def _():
        out_a_ref[...] = jnp.dot(sorted_a_ref[...], basis_a_ref[0], preferred_element_type=F32)


def query_coords(klass, place, feat_g, feat_a, basis_g, basis_a, fac, rows, after=()):
    queries, deep_g = feat_g.shape
    deep_a = feat_a.shape[1]
    width_g, width_a = basis_g.shape[2], basis_a.shape[2]
    tile_g, tile_a = min(TILE, width_g), min(TILE, width_a)
    tiles_g, tiles_a = pl.cdiv(width_g, tile_g), pl.cdiv(width_a, tile_a)
    count = HIGH * fac * rows
    at_g = lambda i: jnp.minimum(i, tiles_g - 1)
    at_a = lambda i: jnp.maximum(i - tiles_g, 0)
    return pl.pallas_call(
        functools.partial(query_kernel, fac, rows, (0, LOW)[klass], tiles_g),
        grid=(tiles_g + tiles_a,),
        in_specs=[
            pl.BlockSpec(place.shape, lambda i: (0, 0)),
            pl.BlockSpec((queries, deep_g), lambda i: (0, 0)),
            pl.BlockSpec((queries, deep_a), lambda i: (0, 0)),
            pl.BlockSpec((1, deep_g, tile_g), lambda i: (klass, 0, at_g(i))),
            pl.BlockSpec((1, deep_a, tile_a), lambda i: (klass, 0, at_a(i))),
        ]
        + [ANYWHERE] * len(after),
        out_specs=[
            pl.BlockSpec((count, tile_g), lambda i: (0, at_g(i))),
            pl.BlockSpec((count, tile_a), lambda i: (0, at_a(i))),
        ],
        out_shape=[jax.ShapeDtypeStruct((count, width), F32) for width in (width_g, width_a)],
        scratch_shapes=[pltpu.VMEM((count, deep), BF16) for deep in (deep_g, deep_a)],
        compiler_params=params(QUERY_MIB[klass]),
        name="query_coords",
    )(place, feat_g, feat_a, basis_g, basis_a, *after)


def join_kernel(count, *refs):
    sources, out_ref, sems = refs[:count], refs[-2], refs[-1]
    size = sources[0].shape[0]
    copies = [
        pltpu.make_async_copy(ref, out_ref.at[pl.ds(i * size, size), :], sems.at[i])
        for i, ref in enumerate(sources)
    ]
    for copy in copies:
        copy.start()
    for copy in copies:
        copy.wait()


def join(blocks, after):
    size, width = blocks[0].shape
    return pl.pallas_call(
        functools.partial(join_kernel, len(blocks)),
        in_specs=[ANYWHERE] * (len(blocks) + len(after)),
        out_specs=WHOLE,
        out_shape=jax.ShapeDtypeStruct((size * len(blocks), width), BF16),
        scratch_shapes=[pltpu.SemaphoreType.DMA((len(blocks),))],
        compiler_params=params(),
        name="join_tokens",
    )(*blocks, *after)


def pack_kernel(counts, slots, room, at_ref, slot_ref, *refs):
    tok, sub, fac = counts
    raws = refs[: sub * fac]
    g_ref, a_ref, made_g, made_a, raw_ref, sems, out_sems = refs[-7:]
    size = raws[0].shape[0]
    copies = [
        pltpu.make_async_copy(ref, raw_ref.at[pl.ds(i * size, size), :], sems.at[i])
        for i, ref in enumerate(raws)
    ]
    for copy in copies:
        copy.start()
    here = []
    for s in range(sub):
        for f in range(fac):
            for k in range(tok):
                row = lax.rem(at_ref[0] + tok - k, tok) * sub + lax.rem(at_ref[1] + sub - s, sub)
                row = row * fac + lax.rem(at_ref[2] + fac - f, fac)
                here.append(slot_ref[pl.ds(row, 1), :])
    here = jnp.concatenate(here, axis=1)
    for copy in copies:
        copy.wait()
    outs = []
    for klass in range(2):
        table = lax.broadcasted_iota(I32, (slots, here.shape[1]), 0) + klass * slots == here
        table = table.astype(F32).astype(BF16)
        for side, (ref, made, begin) in enumerate(((g_ref, made_g, 0), (a_ref, made_a, room))):
            made[klass] = jnp.dot(
                table, raw_ref[:, begin : begin + ref.shape[2]], preferred_element_type=F32
            ).astype(BF16)
            out = pltpu.make_async_copy(made.at[klass], ref.at[klass], out_sems.at[klass, side])
            out.start()
            outs.append(out)
    for out in outs:
        out.wait()


def pack(counts, at, slot, raws, slots, deep_g, deep_a, after):
    size, width = raws[0].shape
    return pl.pallas_call(
        functools.partial(pack_kernel, counts, slots, up_to(deep_g, LANES)),
        in_specs=[SCALARS, WHOLE] + [ANYWHERE] * (len(raws) + len(after)),
        out_specs=[ANYWHERE, ANYWHERE],
        out_shape=[jax.ShapeDtypeStruct((2, slots, deep), BF16) for deep in (deep_g, deep_a)],
        scratch_shapes=[
            pltpu.VMEM((2, slots, deep_g), BF16),
            pltpu.VMEM((2, slots, deep_a), BF16),
            pltpu.VMEM((size * len(raws), width), BF16),
            pltpu.SemaphoreType.DMA((len(raws),)),
            pltpu.SemaphoreType.DMA((2, 2)),
        ],
        compiler_params=params(PACK_MIB, slots),
        name="pack_tokens",
    )(at, slot, *raws, *after)


def token_kernel(packed_ref, eigen_ref, basis_ref, *refs):
    high_ref, low_ref = refs[-2:]
    for klass in range(2):
        coords = (
            jnp.dot(packed_ref[klass], basis_ref[klass], preferred_element_type=F32)
            / (eigen_ref[klass : klass + 1, :] + DAMPING)
        )
        high = coords.astype(BF16)
        high_ref[klass] = high
        low_ref[klass] = (coords - high.astype(F32)).astype(BF16)


def token_coords(packed, eigen, basis, column, segment, after):
    slots = packed.shape[1]
    deep, width = basis.shape[1:]
    here = min(segment, width - column)
    tile = min(TILE, width)
    base = column // tile
    out = jax.ShapeDtypeStruct((2, slots, here), BF16)
    return pl.pallas_call(
        token_kernel,
        grid=(pl.cdiv(here, tile),),
        in_specs=[
            pl.BlockSpec((2, slots, deep), lambda i: (0, 0, 0)),
            pl.BlockSpec((2, tile), lambda i: (0, base + i)),
            pl.BlockSpec((2, deep, tile), lambda i: (0, 0, base + i)),
        ]
        + [ANYWHERE] * len(after),
        out_specs=[pl.BlockSpec((2, slots, tile), lambda i: (0, 0, i))] * 2,
        out_shape=[out, out],
        compiler_params=params(slots=slots),
        name="token_coords",
    )(packed, eigen, basis, *after)


def tiles_of(width):
    return [(begin, min(LANES, width - begin)) for begin in range(0, width, LANES)]


def scaled(x):
    top = jnp.max(jnp.abs(x), axis=1, keepdims=True)
    code = jnp.ceil(jnp.log(jnp.maximum(top, 1e-30)) * FINE)
    factor = LARGEST * jnp.exp(code * (-1.0 / FINE))
    return (x * factor + TO_WHOLE) - TO_WHOLE, code


def narrow(x):
    return x.astype(I32).astype(jnp.int16)


def wide(x):
    return x.astype(I32).astype(F32)


def steps_of(ref, tail):
    step = jnp.exp(wide(ref[:, tail : tail + LANES]) * (1.0 / FINE)) * (1.0 / LARGEST)
    shape = step.shape
    return (
        jnp.broadcast_to(step[:, 0:1], shape),
        jnp.broadcast_to(step[:, LANES - 1 : LANES], shape),
    )


def stage_kernel(row_at, gots, parts, after, at_ref, spot_ref, *refs):
    sources, refs = refs[:gots], refs[gots:]
    use = [k for k in range(2) if parts[k]]
    part = {k: (refs[2 * i], refs[2 * i + 1]) for i, k in enumerate(use)}
    refs = refs[2 * len(use) + after :]
    out_ref, refs = refs[0], refs[1:]
    held = {k: (refs[2 * i], refs[2 * i + 1]) for i, k in enumerate(use)}
    got_ref, made_ref, sems = refs[2 * len(use) :]
    chunk, which, heed = (at_ref[row_at + i] for i in range(3))
    size = ROWS
    blocks = out_ref.shape[0] // size
    per_unit = blocks // GROUP
    width_g, width_a = (ref.shape[1] for ref in part[use[0]])
    room = up_to(width_g, LANES)
    tail = room + up_to(width_a, LANES)

    def received(b, source):
        at = pl.ds(b * size, size)
        return pltpu.make_async_copy(source.at[at, :], got_ref.at[at, :], sems.at[b, 4])

    def each(b, act, first):
        if gots == 1 or (gots and not first):
            act(received(b, sources[0]))
        elif gots:
            for i in range(2):

                @pl.when(which == i)
                def _():
                    act(received(b, sources[i]))

        unit = chunk * GROUP + b // per_unit
        for k in use:
            row = pl.multiple_of(((unit - (0, LOW)[k]) * per_unit + b % per_unit) * size, size)

            def go():
                for side in range(2):
                    act(
                        pltpu.make_async_copy(
                            part[k][side].at[pl.ds(row, size), :],
                            held[k][side].at[pl.ds(b * size, size), :],
                            sems.at[b, 2 * k + side],
                        )
                    )

            if len(use) == 1:
                go()
            else:
                pl.when((unit < HIGH) if k == 0 else (unit >= LOW))(go)

    def sent(b):
        at = pl.ds(b * size, size)
        return pltpu.make_async_copy(made_ref.at[at, :], out_ref.at[at, :], sems.at[b, 5])

    for b in range(blocks):
        each(b, lambda copy: copy.start(), True)
    for b in range(blocks):
        each(b, lambda copy: copy.wait(), False)
        at = slice(b * size, (b + 1) * size)
        if len(use) == 1:
            x_g, x_a = (ref[at, :] for ref in held[use[0]])
        else:
            of_zero = spot_ref[at, :] > 0
            x_g, x_a = (jnp.where(of_zero, held[0][i][at, :], held[1][i][at, :]) for i in range(2))
        if gots:
            step = jnp.exp(wide(got_ref[at, tail : tail + LANES]) * (1.0 / FINE)) * (1.0 / LARGEST)
            step = jnp.where(heed > 0, step, 0.0)
            x_g = x_g + wide(got_ref[at, :width_g]) * step[:, 0:1]
            x_a = x_a + wide(got_ref[at, room : room + width_a]) * step[:, LANES - 1 : LANES]
        q_g, code_g = scaled(x_g)
        q_a, code_a = scaled(x_a)
        if room != width_g or tail != room + width_a:
            made_ref[at, :] = jnp.zeros((size, made_ref.shape[1]), jnp.int16)
        made_ref[at, :width_g] = narrow(q_g)
        made_ref[at, room : room + width_a] = narrow(q_a)
        lane = lax.broadcasted_iota(I32, (size, LANES), 1)
        made_ref[at, tail:] = narrow(jnp.where(lane < LANES // 2, code_g, code_a))
        sent(b).start()
    for b in range(blocks):
        sent(b).wait()


def stage(table, number, spot, got, parts, after):
    use = [part for part in parts if part is not None]
    width_g, width_a = use[0][0].shape[1], use[0][1].shape[1]
    unit = use[0][0].shape[0] // HIGH * GROUP
    packet = up_to(width_g, LANES) + up_to(width_a, LANES) + LANES
    flat = [array for part in use for array in part]
    row_at = 3 * number
    return pl.pallas_call(
        functools.partial(
            stage_kernel, row_at, len(got), tuple(part is not None for part in parts), len(after)
        ),
        grid_spec=pltpu.PrefetchScalarGridSpec(
            num_scalar_prefetch=1,
            grid=(1,),
            in_specs=[pl.BlockSpec((unit, 1), lambda i, c: (c[row_at], 0))]
            + [ANYWHERE] * len(got)
            + [IN_HBM] * len(flat)
            + [ANYWHERE] * len(after),
            out_specs=ANYWHERE,
            scratch_shapes=[pltpu.VMEM((unit, array.shape[1]), F32) for array in flat]
            + [pltpu.VMEM((unit, packet), jnp.int16)] * 2
            + [pltpu.SemaphoreType.DMA((unit // ROWS, 6))],
        ),
        out_shape=jax.ShapeDtypeStruct((unit, packet), jnp.int16),
        compiler_params=params(STAGE_MIB[0 if len(got) != 1 else 1]),
        name="running_sum",
    )(table, spot, *got, *flat, *after)


def side_kernel(plan, counts, z_ref, spot_ref, *refs):
    units, spans, hops, segments, after = plan
    tok, sub, fac = counts
    refs = list(refs)

    def take(n):
        out, refs[:n] = refs[:n], []
        return out

    chunks = sorted({u // GROUP for u in units})
    below = {c: take(hops) for c in chunks}
    above = {c: take(hops) for c in chunks}
    needs = {u: [k for k in (0, 1) if (u < HIGH, u >= LOW)[k]] for u in units}
    part = {k: take(2) for k in (0, 1) if any(k in needs[u] for u in units)}
    pieces = [take(2) for _ in segments]
    take(after)
    out_refs = take(sub)
    held_g, held_a, got, x_g, x_a, sums_ref = take(6)
    tables = take(len(segments))
    sems, piece_sems = take(2)
    held = (held_g, held_a)
    width_g, width_a = x_g.shape[1], x_a.shape[1]
    unit = got.shape[2]
    rows = unit // fac
    slots = pieces[0][0].shape[1]
    cap = slots // (tok * sub)
    room = up_to(width_g, LANES)
    tail = room + up_to(width_a, LANES)
    lanes = out_refs[0].shape[-1] // 2
    z, core, at_x = z_ref[2], z_ref[3], z_ref[4]
    spot_of = {}
    for u in units:
        for k in needs[u]:
            spot_of[u, k] = len(spot_of)

    def own(i, u):
        return [
            pltpu.make_async_copy(
                part[k][side].at[pl.ds((u - (0, LOW)[k]) * unit, unit), :],
                held[side].at[spot_of[u, k]],
                sems.at[i, 2 * k + side],
            )
            for k in needs[u]
            for side in range(2)
        ]

    def arrived(i, u, way, hop):
        source = (below, above)[way][u // GROUP][hop]
        return pltpu.make_async_copy(
            source.at[pl.ds(u % GROUP * unit, unit), :], got.at[way, i], sems.at[i, 4 + way]
        )

    for i, u in enumerate(units):
        for copy in own(i, u):
            copy.start()
        for way in range(2):
            for hop in range(hops):
                cut = (z_ref[way] <= 1) if hop == 0 else (z_ref[way] == hop + 1)

                @pl.when(cut)
                def _():
                    arrived(i, u, way, hop).start()

    copies = [
        pltpu.make_async_copy(
            pieces[s][half].at[klass],
            tables[s].at[c, pl.ds(half * slots, slots), :],
            piece_sems.at[s, 2 * c + half],
        )
        for c, (klass, _) in enumerate(spans)
        for s in range(len(segments))
        for half in range(2)
    ]
    for copy in copies:
        copy.start()
    for i, u in enumerate(units):
        for copy in own(i, u):
            copy.wait()
        for way in range(2):
            arrived(i, u, way, 0).wait()
        below_steps, above_steps = (
            tuple(jnp.where(z_ref[way] > 0, step, 0.0) for step in steps_of(got.at[way, i], tail))
            for way in range(2)
        )
        if len(needs[u]) == 2:
            of_zero = jnp.broadcast_to(spot_ref[u * unit : (u + 1) * unit, :], (unit, LANES)) > 0
        for side, (ref, own_ref) in enumerate(((x_g, held_g), (x_a, held_a))):
            for begin, wide_by in tiles_of(ref.shape[1]):
                cut = slice(begin, begin + wide_by)
                there = slice((0, room)[side] + begin, (0, room)[side] + begin + wide_by)
                full = own_ref[spot_of[u, needs[u][0]], :, cut]
                if len(needs[u]) == 2:
                    full = jnp.where(of_zero[:, :wide_by], full, own_ref[spot_of[u, 1], :, cut])
                full = full + wide(got[0, i, :, there]) * below_steps[side][:, :wide_by]
                full = full + wide(got[1, i, :, there]) * above_steps[side][:, :wide_by]
                high = full.astype(BF16)
                ref[2 * i * unit : (2 * i + 1) * unit, cut] = high
                ref[(2 * i + 1) * unit : (2 * i + 2) * unit, cut] = (full - high.astype(F32)).astype(BF16)

    for copy in copies:
        copy.wait()
    dims = (((1,), (1,)), ((), ()))
    lane = 0
    for c, (klass, members) in enumerate(spans):
        first = units.index(members[0])
        span = slice(2 * first * unit, 2 * (first + len(members)) * unit)
        total = [None, None]
        for s, (side, begin, width) in enumerate(segments):
            x = (x_g, x_a)[side]
            term = lax.dot_general(
                tables[s][c], x[span, begin : begin + width], dims, preferred_element_type=F32
            )
            total[side] = term if total[side] is None else total[side] + term
        for side in range(2):
            sums = total[side][:slots] + total[side][slots:]
            for i in range(len(members)):
                of_unit = (
                    sums[:, 2 * i * unit : (2 * i + 1) * unit] + sums[:, (2 * i + 1) * unit : (2 * i + 2) * unit]
                )
                sums_ref[...] = of_unit
                left = side * lanes + lane + i * rows
                for zz in range(tok):
                    to = lax.rem(zz + tok - z, tok)
                    for s in range(sub):
                        begin = (zz * sub + lax.rem(core + s, sub)) * cap
                        block = sums_ref[pl.ds(pl.multiple_of(begin, 8), cap), :]
                        for f in range(fac):
                            out_refs[s][lax.rem(f + fac - at_x, fac), to, :, left : left + rows] = block[
                                :, f * rows : (f + 1) * rows
                            ]
        lane += len(members) * rows


def sides(counts, where_z, spot, units, spans, parts, first_got, second_got, pieces, after):
    tok, sub, fac = counts
    hops = tok - 1
    packet = first_got[0].shape[1]
    unit = first_got[0].shape[0] // GROUP
    segments = tuple((side, begin, array[0].shape[2]) for side, begin, array in pieces)
    slots = pieces[0][2][0].shape[1]
    needs = [[k for k in (0, 1) if (u < HIGH, u >= LOW)[k]] for u in units]
    used = [array for k in (0, 1) if any(k in some for some in needs) for array in parts[k]]
    width_g, width_a = parts[0][0].shape[1], parts[0][1].shape[1]
    chunks = sorted({u // GROUP for u in units})
    near = [array for c in chunks for array in first_got[c : c + hops]]
    near += [array for c in chunks for array in second_got[c : c + hops]]
    flat = [array for _, _, pair in pieces for array in pair]
    lanes = sum(len(members) for _, members in spans) * (unit // fac)
    owns = sum(len(some) for some in needs)
    many = 2 * len(units) * unit
    return pl.pallas_call(
        functools.partial(side_kernel, (units, spans, hops, segments, len(after)), counts),
        in_specs=[SCALARS, WHOLE]
        + [ANYWHERE] * len(near)
        + [IN_HBM] * (len(used) + len(flat))
        + [ANYWHERE] * len(after),
        out_specs=[WHOLE] * sub,
        out_shape=[jax.ShapeDtypeStruct((fac, tok, slots // (tok * sub), 2 * lanes), F32)] * sub,
        scratch_shapes=[
            pltpu.VMEM((owns, unit, width_g), F32),
            pltpu.VMEM((owns, unit, width_a), F32),
            pltpu.VMEM((2, len(units), unit, packet), jnp.int16),
            pltpu.VMEM((many, width_g), BF16),
            pltpu.VMEM((many, width_a), BF16),
            pltpu.VMEM((slots, unit), F32),
        ]
        + [pltpu.VMEM((len(spans), 2 * slots, width), BF16) for _, _, width in segments]
        + [
            pltpu.SemaphoreType.DMA((len(units), 6)),
            pltpu.SemaphoreType.DMA((len(segments), 2 * len(spans))),
        ],
        compiler_params=params(SIDE_MIB[min(units[0] // 4, 1)], slots),
        name="side_sums",
    )(where_z, spot, *near, *used, *flat, *after)


def final_kernel(groups, hops, first_ref, place_ref, slot_ref, *refs):
    out_ref = refs[-1]
    columns = [[], []]
    for i, batches in enumerate(groups):
        total = refs[i * hops][...]
        for hop in range(1, hops):
            total = total + refs[i * hops + hop][...]
        at = 0
        for runs in batches:
            lanes = sum(run for _, run in runs)
            scores = total[:, at : at + lanes] * total[:, at + lanes : at + 2 * lanes]
            scores = scores * (1.0 / math.sqrt(FH * D))
            at += 2 * lanes
            here = 0
            for klass, run in runs:
                columns[klass].append(scores[:, here : here + run])
                here += run
    cap = columns[0][0].shape[0]
    half_rows, block = out_ref.shape
    result = jnp.zeros((half_rows, block), F32)
    for klass in range(2):
        scores = jnp.concatenate(columns[klass], axis=1)
        count = scores.shape[1]
        begin = (0, LOW * (count // HIGH))[klass]
        row = lax.broadcasted_iota(I32, (count, block), 0) + begin
        of_class = (row < first_ref[0]) if klass == 0 else (row >= first_ref[0])
        to_query = ((place_ref[...] == row) & of_class).astype(F32)
        to_token = (lax.broadcasted_iota(I32, (half_rows, cap), 1) + klass * cap == slot_ref[...]).astype(F32)
        by_query = jnp.dot(scores, to_query, precision=lax.Precision.HIGHEST, preferred_element_type=F32)
        result = result + jnp.dot(
            to_token, by_query, precision=lax.Precision.HIGHEST, preferred_element_type=F32
        )
    out_ref[...] = result


def final(groups, first, place, slot, sums):
    hops = len(sums[0])
    return pl.pallas_call(
        functools.partial(final_kernel, groups, hops),
        in_specs=[SCALARS] + [WHOLE] * (2 + hops * len(sums)),
        out_specs=WHOLE,
        out_shape=jax.ShapeDtypeStruct((slot.shape[0], place.shape[1]), F32),
        compiler_params=params(),
        name="place_scores",
    )(first, place, slot, *[array for arrays in sums for array in arrays])


def body(
    activations,
    gradients,
    tok_class,
    query_inputs,
    query_gradients,
    query_class,
    basis_a,
    basis_g,
    eigen_a,
    eigen_g,
):
    deep_g, width_g = basis_g.shape[1:]
    deep_a, width_a = basis_a.shape[1:]
    counts = tok_count, sub_count, fac_count = tuple(lax.axis_size(a) for a in ("tok", "sub", "fac"))
    z, core, x = (lax.axis_index(a) for a in ("tok", "sub", "fac"))
    block = query_inputs.shape[0] // fac_count
    rows = block // CHUNKS
    tok_rows = activations.shape[0]
    half_rows = tok_rows // sub_count
    slot_cap = 5 * half_rows // 8
    share = half_rows // fac_count
    halves = tok_count * sub_count
    slots = halves * slot_cap
    token_ids = tok_class[:, 0]
    query_ids = query_class[:, 0]

    at = (core * fac_count + x) * share
    room = up_to(deep_g, LANES)
    blocks = []
    for step in range(tok_count):
        to = lax.rem(z + step, tok_count)
        blocks.append(
            jnp.concatenate(
                [
                    lax.dynamic_slice(gradients, (at, to * deep_g), (share, deep_g)),
                    jnp.zeros((share, room - deep_g), BF16),
                    lax.dynamic_slice(activations, (at, to * deep_a), (share, deep_a)),
                ],
                axis=1,
            )
        )
    moved = [blocks[0]] + [
        lax.ppermute(blocks[step], "tok", turn(tok_count, step)) for step in range(1, tok_count)
    ]

    qids = query_ids.reshape(fac_count, block)
    key = qids * block + jnp.arange(block)
    place = jnp.sum((key[:, None, :] < key[:, :, None]).astype(I32), axis=2)
    first = jnp.sum((qids == 0).astype(I32), axis=1)
    spot = (jnp.arange(CHUNKS)[:, None, None] * rows + jnp.arange(rows)) < first[None, :, None]
    spot = spot.reshape(query_ids.shape[0], 1).astype(I32)
    features = (query_gradients, query_inputs, basis_g, basis_a, fac_count, rows)
    parts = [query_coords(0, place, *features, blocks[1:]), None]

    ids = token_ids.reshape(halves, half_rows)
    earlier = jnp.arange(half_rows)[None, :] < jnp.arange(half_rows)[:, None]
    rank = jnp.sum(((ids[:, None, :] == ids[:, :, None]) & earlier).astype(I32), axis=2)
    slot = ids * slots + jnp.arange(halves)[:, None] * slot_cap + rank
    slot = slot.reshape(halves * fac_count, share)
    own_slot = lax.dynamic_index_in_dim(ids * slot_cap + rank, z * sub_count + core, 0).reshape(half_rows, 1)
    places = jnp.stack([z, core, x]).astype(I32)
    last = tok_count - 1
    behinds = (jnp.where(core == 0, z, last - z), jnp.where(core == 0, last - z, z))
    where_z = jnp.stack([*behinds, z, core, x]).astype(I32)

    state = {"pieces": []}

    def second(after):
        parts[1] = query_coords(1, place, *features, after)
        return parts[1][1]

    def joined(after):
        mine = join(moved, after)
        raws = [mine]
        for step in range(1, fac_count):
            raws.append(lax.ppermute(mine, "fac", turn(fac_count, step)))
        for step in range(1, sub_count):
            raws += [lax.ppermute(raw, "sub", turn(sub_count, step)) for raw in raws[:fac_count]]
        state["raws"] = raws
        return mine

    def packed(after):
        state["packed"] = pack(counts, places, slot, state["raws"], slots, deep_g, deep_a, after)
        return state["packed"][0]

    def token(side, column):
        def run(after):
            eigen, basis = ((eigen_g, basis_g), (eigen_a, basis_a))[side]
            segment = SEGMENT if side == 0 else width_a
            pair = token_coords(state["packed"][side], eigen, basis, column, segment, after)
            state["pieces"].append((side, column, pair))
            return pair[0]

        return run

    first_got, second_got = [], []
    groups, sent = [], []

    def batch(units, spans):
        def run(after):
            out = sides(
                counts, where_z, spot, units, spans, parts, first_got, second_got, state["pieces"], after
            )
            groups.append(tuple((klass, len(members) * rows) for klass, members in spans))
            sent.append(out)
            return out[0]

        return run

    columns = list(range(0, width_g, SEGMENT))
    fillers = [[joined, second], [packed]]
    fillers += [[token(0, column)] for column in columns]
    fillers[-1].append(token(1, 0))
    needs = {}
    for units in (range(4), range(4, 6), range(6, 8)):
        spans = [(k, [u for u in units if (u < HIGH, u >= LOW)[k]]) for k in range(2)]
        needs[len(fillers)] = units[-1] // GROUP + tok_count - 2
        fillers.append([batch(list(units), [span for span in spans if span[1]])])

    def over_plane(batches):
        totals = []
        for own, *others in batches:
            for step, other in enumerate(others, 1):
                own = own + lax.ppermute(other, "sub", turn(sub_count, step))
            totals.append(own)
        whole = totals[0] if len(totals) == 1 else jnp.concatenate(totals, axis=-1)
        total = whole[0]
        for step in range(1, fac_count):
            total = total + lax.ppermute(whole[step], "fac", turn(fac_count, step))
        return total

    def over_line(totals):
        whole = jnp.concatenate(totals, axis=-1)
        return [whole[0]] + [
            lax.ppermute(whole[step], "tok", turn(tok_count, step)) for step in range(1, tok_count)
        ]

    at_of = lambda chip, half: chip * sub_count + half
    rounds = []
    for upward in range(2):
        other = 1 - upward
        pairs = [(at_of(i, upward), at_of(i + 1, upward)) for i in range(last)]
        pairs += [(at_of(i + 1, other), at_of(i, other)) for i in range(last)]
        rounds.append(pairs + [(at_of(last, upward), at_of(last, other)), (at_of(0, other), at_of(0, upward))])
    swap = [(0, 1), (1, 0), (last, last - 1), (last - 1, last)]
    after = []
    chunks = CHUNKS // GROUP
    steps = chunks + tok_count - 2
    done = 0
    near_end = jnp.minimum(z, last - z)
    from_upper = (z >= tok_count // 2) == (core == 0)
    table = []
    for step in range(steps):
        if step < 2:
            table += [jnp.clip(step - near_end, 0, chunks - 1), jnp.int32(0), near_end] * 2
        elif step == steps - 1:
            table += [jnp.int32(chunks - 1), jnp.where(from_upper, 0, 1), jnp.int32(1)] * 2
        else:
            for behind in behinds:
                table += [jnp.clip(step - behind, 0, chunks - 1), jnp.int32(0), behind]
    table = jnp.stack([jnp.asarray(entry).astype(I32) for entry in table])
    for step in range(steps):
        early, late = max(step - tok_count + 1, 0) * GROUP, min(step, chunks - 1) * GROUP + GROUP - 1
        wanted = [parts[0] if early < HIGH else None, parts[1] if late >= LOW else None]
        if step == 0:
            packet = stage(table, 0, spot, [], wanted, after)
            came = lax.ppermute(packet, "tok", swap)
            first_got.append(came)
            second_got.append(came)
            after = [packet]
        elif step == 1:
            packet = stage(table, 2, spot, [first_got[-1]], wanted, after)
            first_got.append(lax.ppermute(packet, ("tok", "sub"), rounds[0]))
            second_got.append(lax.ppermute(packet, ("tok", "sub"), rounds[1]))
            after = [packet]
        elif step == steps - 1:
            got = [first_got[-1], second_got[-1]]
            packet = stage(table, 2 * step, spot, got, [None, parts[1]], after)
            came = lax.ppermute(packet, "tok", swap)
            first_got.append(came)
            second_got.append(came)
            after = [packet]
        else:
            for way, (got, pairs) in enumerate(((first_got, rounds[0]), (second_got, rounds[1]))):
                packet = stage(table, 2 * step + way, spot, got[-1:], wanted, after)
                got.append(lax.ppermute(packet, ("tok", "sub"), pairs))
                after = [packet]
        if step < steps - 1 and needs.get(done, -1) < step:
            for item in fillers[done]:
                after = [item(after)]
            done += 1
    for items in fillers[done:]:
        for item in items:
            after = [item(after)]
    sums = [over_line([over_plane(sent[:2]), over_plane(sent[2:])])]

    own_place = lax.dynamic_index_in_dim(place, x, 0)
    own_first = lax.dynamic_index_in_dim(first, x, 0)
    return final([groups], own_first, own_place, own_slot, sums).T


def solution(mesh):
    placed = (
        P(("grp", "tok"), None),
        P(("grp", "tok"), None),
        P("grp", None),
        P("grp", "tok"),
        P("grp", "tok"),
        P("grp", None),
        P(None, "tok", ("fac", "sub")),
        P(None, "tok", ("fac", "sub")),
        P(None, ("fac", "sub")),
        P(None, ("fac", "sub")),
    )
    return jax.shard_map(
        body, mesh=mesh, in_specs=placed, out_specs=P("fac", ("grp", "tok", "sub")), check_vma=False
    )
```

```python
import functools
import math

import jax
import jax.numpy as jnp
from jax import lax
from jax.experimental import pallas as pl
from jax.experimental.pallas import tpu as pltpu
from jax.sharding import PartitionSpec as P

D = 5120
FH = 13824
DAMPING = 0.25
CHUNKS = 8
LOW, HIGH = 3 * CHUNKS // 8, 5 * CHUNKS // 8
LARGEST = 32760.0
TO_WHOLE = 1.5 * 2.0**23
LANES = 128
TILE = 512
SEGMENT = 4 * TILE
GROUP = 2
ROWS = 64
STAGE_MIB = (57, 57)
QUERY_MIB = (63, 63)
PACK_MIB = 63
SIDE_MIB = (63, 63)
MIB = 1 << 20
F32 = jnp.float32
BF16 = jnp.bfloat16
I32 = jnp.int32
FINE = 8.0 / math.log(2.0)
IN_HBM = pl.BlockSpec(memory_space=pltpu.HBM)
ANYWHERE = pl.BlockSpec(memory_space=pl.ANY)
SCALARS = pl.BlockSpec(memory_space=pltpu.SMEM)
WHOLE = pl.BlockSpec(memory_space=pltpu.VMEM)


def up_to(n, m):
    return -(-n // m) * m


def params(mib=63, slots=0):
    return pltpu.CompilerParams(vmem_limit_bytes=(mib if slots <= 512 else 63) * MIB)


def turn(count, step):
    return [(i, (i + step) % count) for i in range(count)]


def query_kernel(fac, rows, first, tiles, place_ref, feat_g_ref, feat_a_ref, basis_g_ref, basis_a_ref, *refs):
    out_g_ref, out_a_ref, sorted_g_ref, sorted_a_ref = refs[-4:]
    block = place_ref.shape[1]
    unit = fac * rows

    def put(feat_ref, sorted_ref):
        for f in range(fac):
            spots = lax.broadcasted_iota(I32, (HIGH * rows, block), 0) + first * rows
            order = (spots == place_ref[f : f + 1, :]).astype(F32).astype(BF16)
            moved = jnp.dot(
                order, feat_ref[f * block : (f + 1) * block, :], preferred_element_type=F32
            ).astype(BF16)
            for j in range(HIGH):
                sorted_ref[j * unit + f * rows : j * unit + (f + 1) * rows, :] = moved[
                    j * rows : (j + 1) * rows, :
                ]

    step = pl.program_id(0)

    @pl.when(step == 0)
    def _():
        put(feat_g_ref, sorted_g_ref)

    @pl.when(step == tiles)
    def _():
        put(feat_a_ref, sorted_a_ref)

    @pl.when(step < tiles)
    def _():
        out_g_ref[...] = jnp.dot(sorted_g_ref[...], basis_g_ref[0], preferred_element_type=F32)

    @pl.when(step >= tiles)
    def _():
        out_a_ref[...] = jnp.dot(sorted_a_ref[...], basis_a_ref[0], preferred_element_type=F32)


def query_coords(klass, place, feat_g, feat_a, basis_g, basis_a, fac, rows, after=()):
    queries, deep_g = feat_g.shape
    deep_a = feat_a.shape[1]
    width_g, width_a = basis_g.shape[2], basis_a.shape[2]
    tile_g, tile_a = min(TILE, width_g), min(TILE, width_a)
    tiles_g, tiles_a = pl.cdiv(width_g, tile_g), pl.cdiv(width_a, tile_a)
    count = HIGH * fac * rows
    at_g = lambda i: jnp.minimum(i, tiles_g - 1)
    at_a = lambda i: jnp.maximum(i - tiles_g, 0)
    return pl.pallas_call(
        functools.partial(query_kernel, fac, rows, (0, LOW)[klass], tiles_g),
        grid=(tiles_g + tiles_a,),
        in_specs=[
            pl.BlockSpec(place.shape, lambda i: (0, 0)),
            pl.BlockSpec((queries, deep_g), lambda i: (0, 0)),
            pl.BlockSpec((queries, deep_a), lambda i: (0, 0)),
            pl.BlockSpec((1, deep_g, tile_g), lambda i: (klass, 0, at_g(i))),
            pl.BlockSpec((1, deep_a, tile_a), lambda i: (klass, 0, at_a(i))),
        ]
        + [ANYWHERE] * len(after),
        out_specs=[
            pl.BlockSpec((count, tile_g), lambda i: (0, at_g(i))),
            pl.BlockSpec((count, tile_a), lambda i: (0, at_a(i))),
        ],
        out_shape=[jax.ShapeDtypeStruct((count, width), F32) for width in (width_g, width_a)],
        scratch_shapes=[pltpu.VMEM((count, deep), BF16) for deep in (deep_g, deep_a)],
        compiler_params=params(QUERY_MIB[klass]),
        name="query_coords",
    )(place, feat_g, feat_a, basis_g, basis_a, *after)


def join_kernel(count, *refs):
    sources, out_ref, sems = refs[:count], refs[-2], refs[-1]
    size = sources[0].shape[0]
    copies = [
        pltpu.make_async_copy(ref, out_ref.at[pl.ds(i * size, size), :], sems.at[i])
        for i, ref in enumerate(sources)
    ]
    for copy in copies:
        copy.start()
    for copy in copies:
        copy.wait()


def join(blocks, after):
    size, width = blocks[0].shape
    return pl.pallas_call(
        functools.partial(join_kernel, len(blocks)),
        in_specs=[ANYWHERE] * (len(blocks) + len(after)),
        out_specs=WHOLE,
        out_shape=jax.ShapeDtypeStruct((size * len(blocks), width), BF16),
        scratch_shapes=[pltpu.SemaphoreType.DMA((len(blocks),))],
        compiler_params=params(),
        name="join_tokens",
    )(*blocks, *after)


def pack_kernel(counts, slots, room, at_ref, slot_ref, *refs):
    tok, sub, fac = counts
    raws = refs[: sub * fac]
    g_ref, a_ref, made_g, made_a, raw_ref, sems, out_sems = refs[-7:]
    size = raws[0].shape[0]
    copies = [
        pltpu.make_async_copy(ref, raw_ref.at[pl.ds(i * size, size), :], sems.at[i])
        for i, ref in enumerate(raws)
    ]
    for copy in copies:
        copy.start()
    here = []
    for s in range(sub):
        for f in range(fac):
            for k in range(tok):
                row = lax.rem(at_ref[0] + tok - k, tok) * sub + lax.rem(at_ref[1] + sub - s, sub)
                row = row * fac + lax.rem(at_ref[2] + fac - f, fac)
                here.append(slot_ref[pl.ds(row, 1), :])
    here = jnp.concatenate(here, axis=1)
    for copy in copies:
        copy.wait()
    outs = []
    for klass in range(2):
        table = lax.broadcasted_iota(I32, (slots, here.shape[1]), 0) + klass * slots == here
        table = table.astype(F32).astype(BF16)
        for side, (ref, made, begin) in enumerate(((g_ref, made_g, 0), (a_ref, made_a, room))):
            made[klass] = jnp.dot(
                table, raw_ref[:, begin : begin + ref.shape[2]], preferred_element_type=F32
            ).astype(BF16)
            out = pltpu.make_async_copy(made.at[klass], ref.at[klass], out_sems.at[klass, side])
            out.start()
            outs.append(out)
    for out in outs:
        out.wait()


def pack(counts, at, slot, raws, slots, deep_g, deep_a, after):
    size, width = raws[0].shape
    return pl.pallas_call(
        functools.partial(pack_kernel, counts, slots, up_to(deep_g, LANES)),
        in_specs=[SCALARS, WHOLE] + [ANYWHERE] * (len(raws) + len(after)),
        out_specs=[ANYWHERE, ANYWHERE],
        out_shape=[jax.ShapeDtypeStruct((2, slots, deep), BF16) for deep in (deep_g, deep_a)],
        scratch_shapes=[
            pltpu.VMEM((2, slots, deep_g), BF16),
            pltpu.VMEM((2, slots, deep_a), BF16),
            pltpu.VMEM((size * len(raws), width), BF16),
            pltpu.SemaphoreType.DMA((len(raws),)),
            pltpu.SemaphoreType.DMA((2, 2)),
        ],
        compiler_params=params(PACK_MIB, slots),
        name="pack_tokens",
    )(at, slot, *raws, *after)


def token_kernel(packed_ref, eigen_ref, basis_ref, *refs):
    high_ref, low_ref = refs[-2:]
    for klass in range(2):
        coords = (
            jnp.dot(packed_ref[klass], basis_ref[klass], preferred_element_type=F32)
            / (eigen_ref[klass : klass + 1, :] + DAMPING)
        )
        high = coords.astype(BF16)
        high_ref[klass] = high
        low_ref[klass] = (coords - high.astype(F32)).astype(BF16)


def token_coords(packed, eigen, basis, column, segment, after):
    slots = packed.shape[1]
    deep, width = basis.shape[1:]
    here = min(segment, width - column)
    tile = min(TILE, width)
    base = column // tile
    out = jax.ShapeDtypeStruct((2, slots, here), BF16)
    return pl.pallas_call(
        token_kernel,
        grid=(pl.cdiv(here, tile),),
        in_specs=[
            pl.BlockSpec((2, slots, deep), lambda i: (0, 0, 0)),
            pl.BlockSpec((2, tile), lambda i: (0, base + i)),
            pl.BlockSpec((2, deep, tile), lambda i: (0, 0, base + i)),
        ]
        + [ANYWHERE] * len(after),
        out_specs=[pl.BlockSpec((2, slots, tile), lambda i: (0, 0, i))] * 2,
        out_shape=[out, out],
        compiler_params=params(slots=slots),
        name="token_coords",
    )(packed, eigen, basis, *after)


def tiles_of(width):
    return [(begin, min(LANES, width - begin)) for begin in range(0, width, LANES)]


def scaled(x):
    top = jnp.max(jnp.abs(x), axis=1, keepdims=True)
    code = jnp.ceil(jnp.log(jnp.maximum(top, 1e-30)) * FINE)
    factor = LARGEST * jnp.exp(code * (-1.0 / FINE))
    return (x * factor + TO_WHOLE) - TO_WHOLE, code


def narrow(x):
    return x.astype(I32).astype(jnp.int16)


def wide(x):
    return x.astype(I32).astype(F32)


def steps_of(ref, tail):
    step = jnp.exp(wide(ref[:, tail : tail + LANES]) * (1.0 / FINE)) * (1.0 / LARGEST)
    shape = step.shape
    return (
        jnp.broadcast_to(step[:, 0:1], shape),
        jnp.broadcast_to(step[:, LANES - 1 : LANES], shape),
    )


def stage_kernel(row_at, gots, parts, after, at_ref, spot_ref, *refs):
    sources, refs = refs[:gots], refs[gots:]
    use = [k for k in range(2) if parts[k]]
    part = {k: (refs[2 * i], refs[2 * i + 1]) for i, k in enumerate(use)}
    refs = refs[2 * len(use) + after :]
    out_ref, refs = refs[0], refs[1:]
    held = {k: (refs[2 * i], refs[2 * i + 1]) for i, k in enumerate(use)}
    got_ref, made_ref, sems = refs[2 * len(use) :]
    chunk, which, heed = (at_ref[row_at + i] for i in range(3))
    size = ROWS
    blocks = out_ref.shape[0] // size
    per_unit = blocks // GROUP
    width_g, width_a = (ref.shape[1] for ref in part[use[0]])
    room = up_to(width_g, LANES)
    tail = room + up_to(width_a, LANES)

    def received(b, source):
        at = pl.ds(b * size, size)
        return pltpu.make_async_copy(source.at[at, :], got_ref.at[at, :], sems.at[b, 4])

    def each(b, act, first):
        if gots == 1 or (gots and not first):
            act(received(b, sources[0]))
        elif gots:
            for i in range(2):

                @pl.when(which == i)
                def _():
                    act(received(b, sources[i]))

        unit = chunk * GROUP + b // per_unit
        for k in use:
            row = pl.multiple_of(((unit - (0, LOW)[k]) * per_unit + b % per_unit) * size, size)

            def go():
                for side in range(2):
                    act(
                        pltpu.make_async_copy(
                            part[k][side].at[pl.ds(row, size), :],
                            held[k][side].at[pl.ds(b * size, size), :],
                            sems.at[b, 2 * k + side],
                        )
                    )

            if len(use) == 1:
                go()
            else:
                pl.when((unit < HIGH) if k == 0 else (unit >= LOW))(go)

    def sent(b):
        at = pl.ds(b * size, size)
        return pltpu.make_async_copy(made_ref.at[at, :], out_ref.at[at, :], sems.at[b, 5])

    for b in range(blocks):
        each(b, lambda copy: copy.start(), True)
    for b in range(blocks):
        each(b, lambda copy: copy.wait(), False)
        at = slice(b * size, (b + 1) * size)
        if len(use) == 1:
            x_g, x_a = (ref[at, :] for ref in held[use[0]])
        else:
            of_zero = spot_ref[at, :] > 0
            x_g, x_a = (jnp.where(of_zero, held[0][i][at, :], held[1][i][at, :]) for i in range(2))
        if gots:
            step = jnp.exp(wide(got_ref[at, tail : tail + LANES]) * (1.0 / FINE)) * (1.0 / LARGEST)
            step = jnp.where(heed > 0, step, 0.0)
            x_g = x_g + wide(got_ref[at, :width_g]) * step[:, 0:1]
            x_a = x_a + wide(got_ref[at, room : room + width_a]) * step[:, LANES - 1 : LANES]
        q_g, code_g = scaled(x_g)
        q_a, code_a = scaled(x_a)
        if room != width_g or tail != room + width_a:
            made_ref[at, :] = jnp.zeros((size, made_ref.shape[1]), jnp.int16)
        made_ref[at, :width_g] = narrow(q_g)
        made_ref[at, room : room + width_a] = narrow(q_a)
        lane = lax.broadcasted_iota(I32, (size, LANES), 1)
        made_ref[at, tail:] = narrow(jnp.where(lane < LANES // 2, code_g, code_a))
        sent(b).start()
    for b in range(blocks):
        sent(b).wait()


def stage(table, number, spot, got, parts, after):
    use = [part for part in parts if part is not None]
    width_g, width_a = use[0][0].shape[1], use[0][1].shape[1]
    unit = use[0][0].shape[0] // HIGH * GROUP
    packet = up_to(width_g, LANES) + up_to(width_a, LANES) + LANES
    flat = [array for part in use for array in part]
    row_at = 3 * number
    return pl.pallas_call(
        functools.partial(
            stage_kernel, row_at, len(got), tuple(part is not None for part in parts), len(after)
        ),
        grid_spec=pltpu.PrefetchScalarGridSpec(
            num_scalar_prefetch=1,
            grid=(1,),
            in_specs=[pl.BlockSpec((unit, 1), lambda i, c: (c[row_at], 0))]
            + [ANYWHERE] * len(got)
            + [IN_HBM] * len(flat)
            + [ANYWHERE] * len(after),
            out_specs=ANYWHERE,
            scratch_shapes=[pltpu.VMEM((unit, array.shape[1]), F32) for array in flat]
            + [pltpu.VMEM((unit, packet), jnp.int16)] * 2
            + [pltpu.SemaphoreType.DMA((unit // ROWS, 6))],
        ),
        out_shape=jax.ShapeDtypeStruct((unit, packet), jnp.int16),
        compiler_params=params(STAGE_MIB[min(number, 1)]),
        name="running_sum",
    )(table, spot, *got, *flat, *after)


def side_kernel(plan, counts, z_ref, spot_ref, *refs):
    units, spans, hops, segments, after = plan
    tok, sub, fac = counts
    refs = list(refs)

    def take(n):
        out, refs[:n] = refs[:n], []
        return out

    chunks = sorted({u // GROUP for u in units})
    below = {c: take(hops) for c in chunks}
    above = {c: take(hops) for c in chunks}
    needs = {u: [k for k in (0, 1) if (u < HIGH, u >= LOW)[k]] for u in units}
    part = {k: take(2) for k in (0, 1) if any(k in needs[u] for u in units)}
    pieces = [take(2) for _ in segments]
    take(after)
    out_refs = take(sub)
    held_g, held_a, got, x_g, x_a, sums_ref = take(6)
    tables = take(len(segments))
    sems, piece_sems = take(2)
    held = (held_g, held_a)
    width_g, width_a = x_g.shape[1], x_a.shape[1]
    unit = got.shape[2]
    rows = unit // fac
    slots = pieces[0][0].shape[1]
    cap = slots // (tok * sub)
    room = up_to(width_g, LANES)
    tail = room + up_to(width_a, LANES)
    lanes = out_refs[0].shape[-1] // 2
    z, core, at_x = z_ref[2], z_ref[3], z_ref[4]
    spot_of = {}
    for u in units:
        for k in needs[u]:
            spot_of[u, k] = len(spot_of)

    def own(i, u):
        return [
            pltpu.make_async_copy(
                part[k][side].at[pl.ds((u - (0, LOW)[k]) * unit, unit), :],
                held[side].at[spot_of[u, k]],
                sems.at[i, 2 * k + side],
            )
            for k in needs[u]
            for side in range(2)
        ]

    def arrived(i, u, way, hop):
        source = (below, above)[way][u // GROUP][hop]
        return pltpu.make_async_copy(
            source.at[pl.ds(u % GROUP * unit, unit), :], got.at[way, i], sems.at[i, 4 + way]
        )

    for i, u in enumerate(units):
        for copy in own(i, u):
            copy.start()
        for way in range(2):
            for hop in range(hops):
                cut = (z_ref[way] <= 1) if hop == 0 else (z_ref[way] == hop + 1)

                @pl.when(cut)
                def _():
                    arrived(i, u, way, hop).start()

    copies = [
        pltpu.make_async_copy(
            pieces[s][half].at[klass],
            tables[s].at[c, pl.ds(half * slots, slots), :],
            piece_sems.at[s, 2 * c + half],
        )
        for c, (klass, _) in enumerate(spans)
        for s in range(len(segments))
        for half in range(2)
    ]
    for copy in copies:
        copy.start()
    for i, u in enumerate(units):
        for copy in own(i, u):
            copy.wait()
        for way in range(2):
            arrived(i, u, way, 0).wait()
        below_steps, above_steps = (
            tuple(jnp.where(z_ref[way] > 0, step, 0.0) for step in steps_of(got.at[way, i], tail))
            for way in range(2)
        )
        if len(needs[u]) == 2:
            of_zero = jnp.broadcast_to(spot_ref[u * unit : (u + 1) * unit, :], (unit, LANES)) > 0
        for side, (ref, own_ref) in enumerate(((x_g, held_g), (x_a, held_a))):
            for begin, wide_by in tiles_of(ref.shape[1]):
                cut = slice(begin, begin + wide_by)
                there = slice((0, room)[side] + begin, (0, room)[side] + begin + wide_by)
                full = own_ref[spot_of[u, needs[u][0]], :, cut]
                if len(needs[u]) == 2:
                    full = jnp.where(of_zero[:, :wide_by], full, own_ref[spot_of[u, 1], :, cut])
                full = full + wide(got[0, i, :, there]) * below_steps[side][:, :wide_by]
                full = full + wide(got[1, i, :, there]) * above_steps[side][:, :wide_by]
                high = full.astype(BF16)
                ref[2 * i * unit : (2 * i + 1) * unit, cut] = high
                ref[(2 * i + 1) * unit : (2 * i + 2) * unit, cut] = (full - high.astype(F32)).astype(BF16)

    for copy in copies:
        copy.wait()
    dims = (((1,), (1,)), ((), ()))
    lane = 0
    for c, (klass, members) in enumerate(spans):
        first = units.index(members[0])
        span = slice(2 * first * unit, 2 * (first + len(members)) * unit)
        total = [None, None]
        for s, (side, begin, width) in enumerate(segments):
            x = (x_g, x_a)[side]
            term = lax.dot_general(
                tables[s][c], x[span, begin : begin + width], dims, preferred_element_type=F32
            )
            total[side] = term if total[side] is None else total[side] + term
        for side in range(2):
            sums = total[side][:slots] + total[side][slots:]
            for i in range(len(members)):
                of_unit = (
                    sums[:, 2 * i * unit : (2 * i + 1) * unit] + sums[:, (2 * i + 1) * unit : (2 * i + 2) * unit]
                )
                sums_ref[...] = of_unit
                left = side * lanes + lane + i * rows
                for zz in range(tok):
                    to = lax.rem(zz + tok - z, tok)
                    for s in range(sub):
                        begin = (zz * sub + lax.rem(core + s, sub)) * cap
                        block = sums_ref[pl.ds(pl.multiple_of(begin, 8), cap), :]
                        for f in range(fac):
                            out_refs[s][lax.rem(f + fac - at_x, fac), to, :, left : left + rows] = block[
                                :, f * rows : (f + 1) * rows
                            ]
        lane += len(members) * rows


def sides(counts, where_z, spot, units, spans, parts, first_got, second_got, pieces, after):
    tok, sub, fac = counts
    hops = tok - 1
    packet = first_got[0].shape[1]
    unit = first_got[0].shape[0] // GROUP
    segments = tuple((side, begin, array[0].shape[2]) for side, begin, array in pieces)
    slots = pieces[0][2][0].shape[1]
    needs = [[k for k in (0, 1) if (u < HIGH, u >= LOW)[k]] for u in units]
    used = [array for k in (0, 1) if any(k in some for some in needs) for array in parts[k]]
    width_g, width_a = parts[0][0].shape[1], parts[0][1].shape[1]
    chunks = sorted({u // GROUP for u in units})
    near = [array for c in chunks for array in first_got[c : c + hops]]
    near += [array for c in chunks for array in second_got[c : c + hops]]
    flat = [array for _, _, pair in pieces for array in pair]
    lanes = sum(len(members) for _, members in spans) * (unit // fac)
    owns = sum(len(some) for some in needs)
    many = 2 * len(units) * unit
    return pl.pallas_call(
        functools.partial(side_kernel, (units, spans, hops, segments, len(after)), counts),
        in_specs=[SCALARS, WHOLE]
        + [ANYWHERE] * len(near)
        + [IN_HBM] * (len(used) + len(flat))
        + [ANYWHERE] * len(after),
        out_specs=[WHOLE] * sub,
        out_shape=[jax.ShapeDtypeStruct((fac, tok, slots // (tok * sub), 2 * lanes), F32)] * sub,
        scratch_shapes=[
            pltpu.VMEM((owns, unit, width_g), F32),
            pltpu.VMEM((owns, unit, width_a), F32),
            pltpu.VMEM((2, len(units), unit, packet), jnp.int16),
            pltpu.VMEM((many, width_g), BF16),
            pltpu.VMEM((many, width_a), BF16),
            pltpu.VMEM((slots, unit), F32),
        ]
        + [pltpu.VMEM((len(spans), 2 * slots, width), BF16) for _, _, width in segments]
        + [
            pltpu.SemaphoreType.DMA((len(units), 6)),
            pltpu.SemaphoreType.DMA((len(segments), 2 * len(spans))),
        ],
        compiler_params=params(SIDE_MIB[min(units[0] // 4, 1)], slots),
        name="side_sums",
    )(where_z, spot, *near, *used, *flat, *after)


def final_kernel(groups, hops, first_ref, place_ref, slot_ref, *refs):
    out_ref = refs[-1]
    columns = [[], []]
    for i, batches in enumerate(groups):
        total = refs[i * hops][...]
        for hop in range(1, hops):
            total = total + refs[i * hops + hop][...]
        at = 0
        for runs in batches:
            lanes = sum(run for _, run in runs)
            scores = total[:, at : at + lanes] * total[:, at + lanes : at + 2 * lanes]
            scores = scores * (1.0 / math.sqrt(FH * D))
            at += 2 * lanes
            here = 0
            for klass, run in runs:
                columns[klass].append(scores[:, here : here + run])
                here += run
    cap = columns[0][0].shape[0]
    half_rows, block = out_ref.shape
    result = jnp.zeros((half_rows, block), F32)
    for klass in range(2):
        scores = jnp.concatenate(columns[klass], axis=1)
        count = scores.shape[1]
        begin = (0, LOW * (count // HIGH))[klass]
        row = lax.broadcasted_iota(I32, (count, block), 0) + begin
        of_class = (row < first_ref[0]) if klass == 0 else (row >= first_ref[0])
        to_query = ((place_ref[...] == row) & of_class).astype(F32)
        to_token = (lax.broadcasted_iota(I32, (half_rows, cap), 1) + klass * cap == slot_ref[...]).astype(F32)
        by_query = jnp.dot(scores, to_query, precision=lax.Precision.HIGHEST, preferred_element_type=F32)
        result = result + jnp.dot(
            to_token, by_query, precision=lax.Precision.HIGHEST, preferred_element_type=F32
        )
    out_ref[...] = result


def final(groups, first, place, slot, sums):
    hops = len(sums[0])
    return pl.pallas_call(
        functools.partial(final_kernel, groups, hops),
        in_specs=[SCALARS] + [WHOLE] * (2 + hops * len(sums)),
        out_specs=WHOLE,
        out_shape=jax.ShapeDtypeStruct((slot.shape[0], place.shape[1]), F32),
        compiler_params=params(),
        name="place_scores",
    )(first, place, slot, *[array for arrays in sums for array in arrays])


def body(
    activations,
    gradients,
    tok_class,
    query_inputs,
    query_gradients,
    query_class,
    basis_a,
    basis_g,
    eigen_a,
    eigen_g,
):
    deep_g, width_g = basis_g.shape[1:]
    deep_a, width_a = basis_a.shape[1:]
    counts = tok_count, sub_count, fac_count = tuple(lax.axis_size(a) for a in ("tok", "sub", "fac"))
    z, core, x = (lax.axis_index(a) for a in ("tok", "sub", "fac"))
    block = query_inputs.shape[0] // fac_count
    rows = block // CHUNKS
    tok_rows = activations.shape[0]
    half_rows = tok_rows // sub_count
    slot_cap = 5 * half_rows // 8
    share = half_rows // fac_count
    halves = tok_count * sub_count
    slots = halves * slot_cap
    token_ids = tok_class[:, 0]
    query_ids = query_class[:, 0]

    at = (core * fac_count + x) * share
    room = up_to(deep_g, LANES)
    blocks = []
    for step in range(tok_count):
        to = lax.rem(z + step, tok_count)
        blocks.append(
            jnp.concatenate(
                [
                    lax.dynamic_slice(gradients, (at, to * deep_g), (share, deep_g)),
                    jnp.zeros((share, room - deep_g), BF16),
                    lax.dynamic_slice(activations, (at, to * deep_a), (share, deep_a)),
                ],
                axis=1,
            )
        )
    moved = [blocks[0]] + [
        lax.ppermute(blocks[step], "tok", turn(tok_count, step)) for step in range(1, tok_count)
    ]

    qids = query_ids.reshape(fac_count, block)
    key = qids * block + jnp.arange(block)
    place = jnp.sum((key[:, None, :] < key[:, :, None]).astype(I32), axis=2)
    first = jnp.sum((qids == 0).astype(I32), axis=1)
    spot = (jnp.arange(CHUNKS)[:, None, None] * rows + jnp.arange(rows)) < first[None, :, None]
    spot = spot.reshape(query_ids.shape[0], 1).astype(I32)
    features = (query_gradients, query_inputs, basis_g, basis_a, fac_count, rows)
    parts = [query_coords(0, place, *features, blocks[1:]), None]

    ids = token_ids.reshape(halves, half_rows)
    earlier = jnp.arange(half_rows)[None, :] < jnp.arange(half_rows)[:, None]
    rank = jnp.sum(((ids[:, None, :] == ids[:, :, None]) & earlier).astype(I32), axis=2)
    slot = ids * slots + jnp.arange(halves)[:, None] * slot_cap + rank
    slot = slot.reshape(halves * fac_count, share)
    own_slot = lax.dynamic_index_in_dim(ids * slot_cap + rank, z * sub_count + core, 0).reshape(half_rows, 1)
    places = jnp.stack([z, core, x]).astype(I32)
    last = tok_count - 1
    behinds = (jnp.where(core == 0, z, last - z), jnp.where(core == 0, last - z, z))
    where_z = jnp.stack([*behinds, z, core, x]).astype(I32)

    state = {"pieces": []}

    def second(after):
        parts[1] = query_coords(1, place, *features, after)
        return parts[1][1]

    def joined(after):
        mine = join(moved, after)
        raws = [mine]
        for step in range(1, fac_count):
            raws.append(lax.ppermute(mine, "fac", turn(fac_count, step)))
        for step in range(1, sub_count):
            raws += [lax.ppermute(raw, "sub", turn(sub_count, step)) for raw in raws[:fac_count]]
        state["raws"] = raws
        return mine

    def packed(after):
        state["packed"] = pack(counts, places, slot, state["raws"], slots, deep_g, deep_a, after)
        return state["packed"][0]

    def token(side, column):
        def run(after):
            eigen, basis = ((eigen_g, basis_g), (eigen_a, basis_a))[side]
            segment = SEGMENT if side == 0 else width_a
            pair = token_coords(state["packed"][side], eigen, basis, column, segment, after)
            state["pieces"].append((side, column, pair))
            return pair[0]

        return run

    first_got, second_got = [], []
    groups, sent = [], []

    def batch(units, spans):
        def run(after):
            out = sides(
                counts, where_z, spot, units, spans, parts, first_got, second_got, state["pieces"], after
            )
            groups.append(tuple((klass, len(members) * rows) for klass, members in spans))
            sent.append(out)
            return out[0]

        return run

    columns = list(range(0, width_g, SEGMENT))
    fillers = [[joined, second], [packed, token(1, 0)]]
    fillers += [[token(0, column)] for column in columns]
    needs = {}
    for units in (range(4), range(4, 6), range(6, 8)):
        spans = [(k, [u for u in units if (u < HIGH, u >= LOW)[k]]) for k in range(2)]
        needs[len(fillers)] = units[-1] // GROUP + tok_count - 2
        fillers.append([batch(list(units), [span for span in spans if span[1]])])

    def over_plane(batches):
        totals = []
        for own, *others in batches:
            for step, other in enumerate(others, 1):
                own = own + lax.ppermute(other, "sub", turn(sub_count, step))
            totals.append(own)
        whole = totals[0] if len(totals) == 1 else jnp.concatenate(totals, axis=-1)
        total = whole[0]
        for step in range(1, fac_count):
            total = total + lax.ppermute(whole[step], "fac", turn(fac_count, step))
        return total

    def over_line(totals):
        whole = jnp.concatenate(totals, axis=-1)
        return [whole[0]] + [
            lax.ppermute(whole[step], "tok", turn(tok_count, step)) for step in range(1, tok_count)
        ]

    at_of = lambda chip, half: chip * sub_count + half
    rounds = []
    for upward in range(2):
        other = 1 - upward
        pairs = [(at_of(i, upward), at_of(i + 1, upward)) for i in range(last)]
        pairs += [(at_of(i + 1, other), at_of(i, other)) for i in range(last)]
        rounds.append(pairs + [(at_of(last, upward), at_of(last, other)), (at_of(0, other), at_of(0, upward))])
    swap = [(0, 1), (1, 0), (last, last - 1), (last - 1, last)]
    after = []
    chunks = CHUNKS // GROUP
    steps = chunks + tok_count - 2
    done = 0
    near_end = jnp.minimum(z, last - z)
    from_upper = (z >= tok_count // 2) == (core == 0)
    table = []
    for step in range(steps):
        if step < 2:
            table += [jnp.clip(step - near_end, 0, chunks - 1), jnp.int32(0), near_end] * 2
        elif step == steps - 1:
            table += [jnp.int32(chunks - 1), jnp.where(from_upper, 0, 1), jnp.int32(1)] * 2
        else:
            for behind in behinds:
                table += [jnp.clip(step - behind, 0, chunks - 1), jnp.int32(0), behind]
    table = jnp.stack([jnp.asarray(entry).astype(I32) for entry in table])
    for step in range(steps):
        early, late = max(step - tok_count + 1, 0) * GROUP, min(step, chunks - 1) * GROUP + GROUP - 1
        wanted = [parts[0] if early < HIGH else None, parts[1] if late >= LOW else None]
        if step == 0:
            packet = stage(table, 0, spot, [], wanted, after)
            came = lax.ppermute(packet, "tok", swap)
            first_got.append(came)
            second_got.append(came)
            after = [packet]
        elif step == 1:
            packet = stage(table, 2, spot, [first_got[-1]], wanted, after)
            first_got.append(lax.ppermute(packet, ("tok", "sub"), rounds[0]))
            second_got.append(lax.ppermute(packet, ("tok", "sub"), rounds[1]))
            after = [packet]
        elif step == steps - 1:
            got = [first_got[-1], second_got[-1]]
            packet = stage(table, 2 * step, spot, got, [None, parts[1]], after)
            came = lax.ppermute(packet, "tok", swap)
            first_got.append(came)
            second_got.append(came)
            after = [packet]
        else:
            for way, (got, pairs) in enumerate(((first_got, rounds[0]), (second_got, rounds[1]))):
                packet = stage(table, 2 * step + way, spot, got[-1:], wanted, after)
                got.append(lax.ppermute(packet, ("tok", "sub"), pairs))
                after = [packet]
        if step < steps - 1 and needs.get(done, -1) < step:
            for item in fillers[done]:
                after = [item(after)]
            done += 1
    for items in fillers[done:]:
        for item in items:
            after = [item(after)]
    sums = [over_line([over_plane(sent[:2]), over_plane(sent[2:])])]

    own_place = lax.dynamic_index_in_dim(place, x, 0)
    own_first = lax.dynamic_index_in_dim(first, x, 0)
    return final([groups], own_first, own_place, own_slot, sums).T


def solution(mesh):
    placed = (
        P(("grp", "tok"), None),
        P(("grp", "tok"), None),
        P("grp", None),
        P("grp", "tok"),
        P("grp", "tok"),
        P("grp", None),
        P(None, "tok", ("fac", "sub")),
        P(None, "tok", ("fac", "sub")),
        P(None, ("fac", "sub")),
        P(None, ("fac", "sub")),
    )
    return jax.shard_map(
        body, mesh=mesh, in_specs=placed, out_specs=P("fac", ("grp", "tok", "sub")), check_vma=False
    )
```

```python
import functools
import math

import jax
import jax.numpy as jnp
from jax import lax
from jax.experimental import pallas as pl
from jax.experimental.pallas import tpu as pltpu
from jax.sharding import PartitionSpec as P

D = 5120
FH = 13824
DAMPING = 0.25
CHUNKS = 8
LOW, HIGH = 3 * CHUNKS // 8, 5 * CHUNKS // 8
LARGEST = 32760.0
TO_WHOLE = 1.5 * 2.0**23
LANES = 128
TILE = 512
SEGMENT = 4 * TILE
GROUP = 2
ROWS = 64
STAGE_MIB = (57, 20)
QUERY_MIB = (63, 34)
PACK_MIB = 34
SIDE_MIB = (63, 63)
MIB = 1 << 20
F32 = jnp.float32
BF16 = jnp.bfloat16
I32 = jnp.int32
FINE = 8.0 / math.log(2.0)
IN_HBM = pl.BlockSpec(memory_space=pltpu.HBM)
ANYWHERE = pl.BlockSpec(memory_space=pl.ANY)
SCALARS = pl.BlockSpec(memory_space=pltpu.SMEM)
WHOLE = pl.BlockSpec(memory_space=pltpu.VMEM)


def up_to(n, m):
    return -(-n // m) * m


def params(mib=34, slots=0):
    return pltpu.CompilerParams(vmem_limit_bytes=(mib if slots <= 512 else 63) * MIB)


def turn(count, step):
    return [(i, (i + step) % count) for i in range(count)]


def query_kernel(fac, rows, first, tiles, place_ref, feat_g_ref, feat_a_ref, basis_g_ref, basis_a_ref, *refs):
    out_g_ref, out_a_ref, sorted_g_ref, sorted_a_ref = refs[-4:]
    block = place_ref.shape[1]
    unit = fac * rows

    def put(feat_ref, sorted_ref):
        for f in range(fac):
            spots = lax.broadcasted_iota(I32, (HIGH * rows, block), 0) + first * rows
            order = (spots == place_ref[f : f + 1, :]).astype(F32).astype(BF16)
            moved = jnp.dot(
                order, feat_ref[f * block : (f + 1) * block, :], preferred_element_type=F32
            ).astype(BF16)
            for j in range(HIGH):
                sorted_ref[j * unit + f * rows : j * unit + (f + 1) * rows, :] = moved[
                    j * rows : (j + 1) * rows, :
                ]

    step = pl.program_id(0)

    @pl.when(step == 0)
    def _():
        put(feat_g_ref, sorted_g_ref)

    @pl.when(step == tiles)
    def _():
        put(feat_a_ref, sorted_a_ref)

    @pl.when(step < tiles)
    def _():
        out_g_ref[...] = jnp.dot(sorted_g_ref[...], basis_g_ref[0], preferred_element_type=F32)

    @pl.when(step >= tiles)
    def _():
        out_a_ref[...] = jnp.dot(sorted_a_ref[...], basis_a_ref[0], preferred_element_type=F32)


def query_coords(klass, place, feat_g, feat_a, basis_g, basis_a, fac, rows, after=()):
    queries, deep_g = feat_g.shape
    deep_a = feat_a.shape[1]
    width_g, width_a = basis_g.shape[2], basis_a.shape[2]
    tile_g, tile_a = min(TILE, width_g), min(TILE, width_a)
    tiles_g, tiles_a = pl.cdiv(width_g, tile_g), pl.cdiv(width_a, tile_a)
    count = HIGH * fac * rows
    at_g = lambda i: jnp.minimum(i, tiles_g - 1)
    at_a = lambda i: jnp.maximum(i - tiles_g, 0)
    return pl.pallas_call(
        functools.partial(query_kernel, fac, rows, (0, LOW)[klass], tiles_g),
        grid=(tiles_g + tiles_a,),
        in_specs=[
            pl.BlockSpec(place.shape, lambda i: (0, 0)),
            pl.BlockSpec((queries, deep_g), lambda i: (0, 0)),
            pl.BlockSpec((queries, deep_a), lambda i: (0, 0)),
            pl.BlockSpec((1, deep_g, tile_g), lambda i: (klass, 0, at_g(i))),
            pl.BlockSpec((1, deep_a, tile_a), lambda i: (klass, 0, at_a(i))),
        ]
        + [ANYWHERE] * len(after),
        out_specs=[
            pl.BlockSpec((count, tile_g), lambda i: (0, at_g(i))),
            pl.BlockSpec((count, tile_a), lambda i: (0, at_a(i))),
        ],
        out_shape=[jax.ShapeDtypeStruct((count, width), F32) for width in (width_g, width_a)],
        scratch_shapes=[pltpu.VMEM((count, deep), BF16) for deep in (deep_g, deep_a)],
        compiler_params=params(QUERY_MIB[klass]),
        name="query_coords",
    )(place, feat_g, feat_a, basis_g, basis_a, *after)


def join_kernel(count, *refs):
    sources, out_ref, sems = refs[:count], refs[-2], refs[-1]
    size = sources[0].shape[0]
    copies = [
        pltpu.make_async_copy(ref, out_ref.at[pl.ds(i * size, size), :], sems.at[i])
        for i, ref in enumerate(sources)
    ]
    for copy in copies:
        copy.start()
    for copy in copies:
        copy.wait()


def join(blocks, after):
    size, width = blocks[0].shape
    return pl.pallas_call(
        functools.partial(join_kernel, len(blocks)),
        in_specs=[ANYWHERE] * (len(blocks) + len(after)),
        out_specs=WHOLE,
        out_shape=jax.ShapeDtypeStruct((size * len(blocks), width), BF16),
        scratch_shapes=[pltpu.SemaphoreType.DMA((len(blocks),))],
        compiler_params=params(),
        name="join_tokens",
    )(*blocks, *after)


def pack_kernel(counts, slots, room, at_ref, slot_ref, *refs):
    tok, sub, fac = counts
    raws = refs[: sub * fac]
    g_ref, a_ref, made_g, made_a, raw_ref, sems, out_sems = refs[-7:]
    size = raws[0].shape[0]
    copies = [
        pltpu.make_async_copy(ref, raw_ref.at[pl.ds(i * size, size), :], sems.at[i])
        for i, ref in enumerate(raws)
    ]
    for copy in copies:
        copy.start()
    here = []
    for s in range(sub):
        for f in range(fac):
            for k in range(tok):
                row = lax.rem(at_ref[0] + tok - k, tok) * sub + lax.rem(at_ref[1] + sub - s, sub)
                row = row * fac + lax.rem(at_ref[2] + fac - f, fac)
                here.append(slot_ref[pl.ds(row, 1), :])
    here = jnp.concatenate(here, axis=1)
    for copy in copies:
        copy.wait()
    outs = []
    for klass in range(2):
        table = lax.broadcasted_iota(I32, (slots, here.shape[1]), 0) + klass * slots == here
        table = table.astype(F32).astype(BF16)
        for side, (ref, made, begin) in enumerate(((g_ref, made_g, 0), (a_ref, made_a, room))):
            made[klass] = jnp.dot(
                table, raw_ref[:, begin : begin + ref.shape[2]], preferred_element_type=F32
            ).astype(BF16)
            out = pltpu.make_async_copy(made.at[klass], ref.at[klass], out_sems.at[klass, side])
            out.start()
            outs.append(out)
    for out in outs:
        out.wait()


def pack(counts, at, slot, raws, slots, deep_g, deep_a, after):
    size, width = raws[0].shape
    return pl.pallas_call(
        functools.partial(pack_kernel, counts, slots, up_to(deep_g, LANES)),
        in_specs=[SCALARS, WHOLE] + [ANYWHERE] * (len(raws) + len(after)),
        out_specs=[ANYWHERE, ANYWHERE],
        out_shape=[jax.ShapeDtypeStruct((2, slots, deep), BF16) for deep in (deep_g, deep_a)],
        scratch_shapes=[
            pltpu.VMEM((2, slots, deep_g), BF16),
            pltpu.VMEM((2, slots, deep_a), BF16),
            pltpu.VMEM((size * len(raws), width), BF16),
            pltpu.SemaphoreType.DMA((len(raws),)),
            pltpu.SemaphoreType.DMA((2, 2)),
        ],
        compiler_params=params(PACK_MIB, slots),
        name="pack_tokens",
    )(at, slot, *raws, *after)


def token_kernel(packed_ref, eigen_ref, basis_ref, *refs):
    high_ref, low_ref = refs[-2:]
    for klass in range(2):
        coords = (
            jnp.dot(packed_ref[klass], basis_ref[klass], preferred_element_type=F32)
            / (eigen_ref[klass : klass + 1, :] + DAMPING)
        )
        high = coords.astype(BF16)
        high_ref[klass] = high
        low_ref[klass] = (coords - high.astype(F32)).astype(BF16)


def token_coords(packed, eigen, basis, column, segment, after):
    slots = packed.shape[1]
    deep, width = basis.shape[1:]
    here = min(segment, width - column)
    tile = min(TILE, width)
    base = column // tile
    out = jax.ShapeDtypeStruct((2, slots, here), BF16)
    return pl.pallas_call(
        token_kernel,
        grid=(pl.cdiv(here, tile),),
        in_specs=[
            pl.BlockSpec((2, slots, deep), lambda i: (0, 0, 0)),
            pl.BlockSpec((2, tile), lambda i: (0, base + i)),
            pl.BlockSpec((2, deep, tile), lambda i: (0, 0, base + i)),
        ]
        + [ANYWHERE] * len(after),
        out_specs=[pl.BlockSpec((2, slots, tile), lambda i: (0, 0, i))] * 2,
        out_shape=[out, out],
        compiler_params=params(slots=slots),
        name="token_coords",
    )(packed, eigen, basis, *after)


def tiles_of(width):
    return [(begin, min(LANES, width - begin)) for begin in range(0, width, LANES)]


def scaled(x):
    top = jnp.max(jnp.abs(x), axis=1, keepdims=True)
    code = jnp.ceil(jnp.log(jnp.maximum(top, 1e-30)) * FINE)
    factor = LARGEST * jnp.exp(code * (-1.0 / FINE))
    return (x * factor + TO_WHOLE) - TO_WHOLE, code


def narrow(x):
    return x.astype(I32).astype(jnp.int16)


def wide(x):
    return x.astype(I32).astype(F32)


def steps_of(ref, tail):
    step = jnp.exp(wide(ref[:, tail : tail + LANES]) * (1.0 / FINE)) * (1.0 / LARGEST)
    shape = step.shape
    return (
        jnp.broadcast_to(step[:, 0:1], shape),
        jnp.broadcast_to(step[:, LANES - 1 : LANES], shape),
    )


def stage_kernel(row_at, gots, parts, after, at_ref, spot_ref, *refs):
    sources, refs = refs[:gots], refs[gots:]
    use = [k for k in range(2) if parts[k]]
    part = {k: (refs[2 * i], refs[2 * i + 1]) for i, k in enumerate(use)}
    refs = refs[2 * len(use) + after :]
    out_ref, refs = refs[0], refs[1:]
    held = {k: (refs[2 * i], refs[2 * i + 1]) for i, k in enumerate(use)}
    got_ref, made_ref, sems = refs[2 * len(use) :]
    chunk, which, heed = (at_ref[row_at + i] for i in range(3))
    size = ROWS
    blocks = out_ref.shape[0] // size
    per_unit = blocks // GROUP
    width_g, width_a = (ref.shape[1] for ref in part[use[0]])
    room = up_to(width_g, LANES)
    tail = room + up_to(width_a, LANES)

    def received(b, source):
        at = pl.ds(b * size, size)
        return pltpu.make_async_copy(source.at[at, :], got_ref.at[at, :], sems.at[b, 4])

    def each(b, act, first):
        if gots == 1 or (gots and not first):
            act(received(b, sources[0]))
        elif gots:
            for i in range(2):

                @pl.when(which == i)
                def _():
                    act(received(b, sources[i]))

        unit = chunk * GROUP + b // per_unit
        for k in use:
            row = pl.multiple_of(((unit - (0, LOW)[k]) * per_unit + b % per_unit) * size, size)

            def go():
                for side in range(2):
                    act(
                        pltpu.make_async_copy(
                            part[k][side].at[pl.ds(row, size), :],
                            held[k][side].at[pl.ds(b * size, size), :],
                            sems.at[b, 2 * k + side],
                        )
                    )

            if len(use) == 1:
                go()
            else:
                pl.when((unit < HIGH) if k == 0 else (unit >= LOW))(go)

    def sent(b):
        at = pl.ds(b * size, size)
        return pltpu.make_async_copy(made_ref.at[at, :], out_ref.at[at, :], sems.at[b, 5])

    for b in range(blocks):
        each(b, lambda copy: copy.start(), True)
    for b in range(blocks):
        each(b, lambda copy: copy.wait(), False)
        at = slice(b * size, (b + 1) * size)
        if len(use) == 1:
            x_g, x_a = (ref[at, :] for ref in held[use[0]])
        else:
            of_zero = spot_ref[at, :] > 0
            x_g, x_a = (jnp.where(of_zero, held[0][i][at, :], held[1][i][at, :]) for i in range(2))
        if gots:
            step = jnp.exp(wide(got_ref[at, tail : tail + LANES]) * (1.0 / FINE)) * (1.0 / LARGEST)
            step = jnp.where(heed > 0, step, 0.0)
            x_g = x_g + wide(got_ref[at, :width_g]) * step[:, 0:1]
            x_a = x_a + wide(got_ref[at, room : room + width_a]) * step[:, LANES - 1 : LANES]
        q_g, code_g = scaled(x_g)
        q_a, code_a = scaled(x_a)
        if room != width_g or tail != room + width_a:
            made_ref[at, :] = jnp.zeros((size, made_ref.shape[1]), jnp.int16)
        made_ref[at, :width_g] = narrow(q_g)
        made_ref[at, room : room + width_a] = narrow(q_a)
        lane = lax.broadcasted_iota(I32, (size, LANES), 1)
        made_ref[at, tail:] = narrow(jnp.where(lane < LANES // 2, code_g, code_a))
        sent(b).start()
    for b in range(blocks):
        sent(b).wait()


def stage(table, number, spot, got, parts, after):
    use = [part for part in parts if part is not None]
    width_g, width_a = use[0][0].shape[1], use[0][1].shape[1]
    unit = use[0][0].shape[0] // HIGH * GROUP
    packet = up_to(width_g, LANES) + up_to(width_a, LANES) + LANES
    flat = [array for part in use for array in part]
    row_at = 3 * number
    return pl.pallas_call(
        functools.partial(
            stage_kernel, row_at, len(got), tuple(part is not None for part in parts), len(after)
        ),
        grid_spec=pltpu.PrefetchScalarGridSpec(
            num_scalar_prefetch=1,
            grid=(1,),
            in_specs=[pl.BlockSpec((unit, 1), lambda i, c: (c[row_at], 0))]
            + [ANYWHERE] * len(got)
            + [IN_HBM] * len(flat)
            + [ANYWHERE] * len(after),
            out_specs=ANYWHERE,
            scratch_shapes=[pltpu.VMEM((unit, array.shape[1]), F32) for array in flat]
            + [pltpu.VMEM((unit, packet), jnp.int16)] * 2
            + [pltpu.SemaphoreType.DMA((unit // ROWS, 6))],
        ),
        out_shape=jax.ShapeDtypeStruct((unit, packet), jnp.int16),
        compiler_params=params(STAGE_MIB[0 if len(got) != 1 else 1]),
        name="running_sum",
    )(table, spot, *got, *flat, *after)


def side_kernel(plan, counts, z_ref, spot_ref, *refs):
    units, spans, hops, segments, after = plan
    tok, sub, fac = counts
    refs = list(refs)

    def take(n):
        out, refs[:n] = refs[:n], []
        return out

    chunks = sorted({u // GROUP for u in units})
    below = {c: take(hops) for c in chunks}
    above = {c: take(hops) for c in chunks}
    needs = {u: [k for k in (0, 1) if (u < HIGH, u >= LOW)[k]] for u in units}
    part = {k: take(2) for k in (0, 1) if any(k in needs[u] for u in units)}
    pieces = [take(2) for _ in segments]
    take(after)
    out_refs = take(sub)
    held_g, held_a, got, x_g, x_a, sums_ref = take(6)
    tables = take(len(segments))
    sems, piece_sems = take(2)
    held = (held_g, held_a)
    width_g, width_a = x_g.shape[1], x_a.shape[1]
    unit = got.shape[2]
    rows = unit // fac
    slots = pieces[0][0].shape[1]
    cap = slots // (tok * sub)
    room = up_to(width_g, LANES)
    tail = room + up_to(width_a, LANES)
    lanes = out_refs[0].shape[-1] // 2
    z, core, at_x = z_ref[2], z_ref[3], z_ref[4]
    spot_of = {}
    for u in units:
        for k in needs[u]:
            spot_of[u, k] = len(spot_of)

    def own(i, u):
        return [
            pltpu.make_async_copy(
                part[k][side].at[pl.ds((u - (0, LOW)[k]) * unit, unit), :],
                held[side].at[spot_of[u, k]],
                sems.at[i, 2 * k + side],
            )
            for k in needs[u]
            for side in range(2)
        ]

    def arrived(i, u, way, hop):
        source = (below, above)[way][u // GROUP][hop]
        return pltpu.make_async_copy(
            source.at[pl.ds(u % GROUP * unit, unit), :], got.at[way, i], sems.at[i, 4 + way]
        )

    for i, u in enumerate(units):
        for copy in own(i, u):
            copy.start()
        for way in range(2):
            for hop in range(hops):
                cut = (z_ref[way] <= 1) if hop == 0 else (z_ref[way] == hop + 1)

                @pl.when(cut)
                def _():
                    arrived(i, u, way, hop).start()

    copies = [
        pltpu.make_async_copy(
            pieces[s][half].at[klass],
            tables[s].at[c, pl.ds(half * slots, slots), :],
            piece_sems.at[s, 2 * c + half],
        )
        for c, (klass, _) in enumerate(spans)
        for s in range(len(segments))
        for half in range(2)
    ]
    for copy in copies:
        copy.start()
    for i, u in enumerate(units):
        for copy in own(i, u):
            copy.wait()
        for way in range(2):
            arrived(i, u, way, 0).wait()
        below_steps, above_steps = (
            tuple(jnp.where(z_ref[way] > 0, step, 0.0) for step in steps_of(got.at[way, i], tail))
            for way in range(2)
        )
        if len(needs[u]) == 2:
            of_zero = jnp.broadcast_to(spot_ref[u * unit : (u + 1) * unit, :], (unit, LANES)) > 0
        for side, (ref, own_ref) in enumerate(((x_g, held_g), (x_a, held_a))):
            for begin, wide_by in tiles_of(ref.shape[1]):
                cut = slice(begin, begin + wide_by)
                there = slice((0, room)[side] + begin, (0, room)[side] + begin + wide_by)
                full = own_ref[spot_of[u, needs[u][0]], :, cut]
                if len(needs[u]) == 2:
                    full = jnp.where(of_zero[:, :wide_by], full, own_ref[spot_of[u, 1], :, cut])
                full = full + wide(got[0, i, :, there]) * below_steps[side][:, :wide_by]
                full = full + wide(got[1, i, :, there]) * above_steps[side][:, :wide_by]
                high = full.astype(BF16)
                ref[2 * i * unit : (2 * i + 1) * unit, cut] = high
                ref[(2 * i + 1) * unit : (2 * i + 2) * unit, cut] = (full - high.astype(F32)).astype(BF16)

    for copy in copies:
        copy.wait()
    dims = (((1,), (1,)), ((), ()))
    lane = 0
    for c, (klass, members) in enumerate(spans):
        first = units.index(members[0])
        span = slice(2 * first * unit, 2 * (first + len(members)) * unit)
        total = [None, None]
        for s, (side, begin, width) in enumerate(segments):
            x = (x_g, x_a)[side]
            term = lax.dot_general(
                tables[s][c], x[span, begin : begin + width], dims, preferred_element_type=F32
            )
            total[side] = term if total[side] is None else total[side] + term
        for side in range(2):
            sums = total[side][:slots] + total[side][slots:]
            for i in range(len(members)):
                of_unit = (
                    sums[:, 2 * i * unit : (2 * i + 1) * unit] + sums[:, (2 * i + 1) * unit : (2 * i + 2) * unit]
                )
                sums_ref[...] = of_unit
                left = side * lanes + lane + i * rows
                for zz in range(tok):
                    to = lax.rem(zz + tok - z, tok)
                    for s in range(sub):
                        begin = (zz * sub + lax.rem(core + s, sub)) * cap
                        block = sums_ref[pl.ds(pl.multiple_of(begin, 8), cap), :]
                        for f in range(fac):
                            out_refs[s][lax.rem(f + fac - at_x, fac), to, :, left : left + rows] = block[
                                :, f * rows : (f + 1) * rows
                            ]
        lane += len(members) * rows


def sides(counts, where_z, spot, units, spans, parts, first_got, second_got, pieces, after):
    tok, sub, fac = counts
    hops = tok - 1
    packet = first_got[0].shape[1]
    unit = first_got[0].shape[0] // GROUP
    segments = tuple((side, begin, array[0].shape[2]) for side, begin, array in pieces)
    slots = pieces[0][2][0].shape[1]
    needs = [[k for k in (0, 1) if (u < HIGH, u >= LOW)[k]] for u in units]
    used = [array for k in (0, 1) if any(k in some for some in needs) for array in parts[k]]
    width_g, width_a = parts[0][0].shape[1], parts[0][1].shape[1]
    chunks = sorted({u // GROUP for u in units})
    near = [array for c in chunks for array in first_got[c : c + hops]]
    near += [array for c in chunks for array in second_got[c : c + hops]]
    flat = [array for _, _, pair in pieces for array in pair]
    lanes = sum(len(members) for _, members in spans) * (unit // fac)
    owns = sum(len(some) for some in needs)
    many = 2 * len(units) * unit
    return pl.pallas_call(
        functools.partial(side_kernel, (units, spans, hops, segments, len(after)), counts),
        in_specs=[SCALARS, WHOLE]
        + [ANYWHERE] * len(near)
        + [IN_HBM] * (len(used) + len(flat))
        + [ANYWHERE] * len(after),
        out_specs=[WHOLE] * sub,
        out_shape=[jax.ShapeDtypeStruct((fac, tok, slots // (tok * sub), 2 * lanes), F32)] * sub,
        scratch_shapes=[
            pltpu.VMEM((owns, unit, width_g), F32),
            pltpu.VMEM((owns, unit, width_a), F32),
            pltpu.VMEM((2, len(units), unit, packet), jnp.int16),
            pltpu.VMEM((many, width_g), BF16),
            pltpu.VMEM((many, width_a), BF16),
            pltpu.VMEM((slots, unit), F32),
        ]
        + [pltpu.VMEM((len(spans), 2 * slots, width), BF16) for _, _, width in segments]
        + [
            pltpu.SemaphoreType.DMA((len(units), 6)),
            pltpu.SemaphoreType.DMA((len(segments), 2 * len(spans))),
        ],
        compiler_params=params(SIDE_MIB[min(units[0] // 4, 1)], slots),
        name="side_sums",
    )(where_z, spot, *near, *used, *flat, *after)


def final_kernel(groups, hops, first_ref, place_ref, slot_ref, *refs):
    out_ref = refs[-1]
    columns = [[], []]
    for i, batches in enumerate(groups):
        total = refs[i * hops][...]
        for hop in range(1, hops):
            total = total + refs[i * hops + hop][...]
        at = 0
        for runs in batches:
            lanes = sum(run for _, run in runs)
            scores = total[:, at : at + lanes] * total[:, at + lanes : at + 2 * lanes]
            scores = scores * (1.0 / math.sqrt(FH * D))
            at += 2 * lanes
            here = 0
            for klass, run in runs:
                columns[klass].append(scores[:, here : here + run])
                here += run
    cap = columns[0][0].shape[0]
    half_rows, block = out_ref.shape
    result = jnp.zeros((half_rows, block), F32)
    for klass in range(2):
        scores = jnp.concatenate(columns[klass], axis=1)
        count = scores.shape[1]
        begin = (0, LOW * (count // HIGH))[klass]
        row = lax.broadcasted_iota(I32, (count, block), 0) + begin
        of_class = (row < first_ref[0]) if klass == 0 else (row >= first_ref[0])
        to_query = ((place_ref[...] == row) & of_class).astype(F32)
        to_token = (lax.broadcasted_iota(I32, (half_rows, cap), 1) + klass * cap == slot_ref[...]).astype(F32)
        by_query = jnp.dot(scores, to_query, precision=lax.Precision.HIGHEST, preferred_element_type=F32)
        result = result + jnp.dot(
            to_token, by_query, precision=lax.Precision.HIGHEST, preferred_element_type=F32
        )
    out_ref[...] = result


def final(groups, first, place, slot, sums):
    hops = len(sums[0])
    return pl.pallas_call(
        functools.partial(final_kernel, groups, hops),
        in_specs=[SCALARS] + [WHOLE] * (2 + hops * len(sums)),
        out_specs=WHOLE,
        out_shape=jax.ShapeDtypeStruct((slot.shape[0], place.shape[1]), F32),
        compiler_params=params(),
        name="place_scores",
    )(first, place, slot, *[array for arrays in sums for array in arrays])


def body(
    activations,
    gradients,
    tok_class,
    query_inputs,
    query_gradients,
    query_class,
    basis_a,
    basis_g,
    eigen_a,
    eigen_g,
):
    deep_g, width_g = basis_g.shape[1:]
    deep_a, width_a = basis_a.shape[1:]
    counts = tok_count, sub_count, fac_count = tuple(lax.axis_size(a) for a in ("tok", "sub", "fac"))
    z, core, x = (lax.axis_index(a) for a in ("tok", "sub", "fac"))
    block = query_inputs.shape[0] // fac_count
    rows = block // CHUNKS
    tok_rows = activations.shape[0]
    half_rows = tok_rows // sub_count
    slot_cap = 5 * half_rows // 8
    share = half_rows // fac_count
    halves = tok_count * sub_count
    slots = halves * slot_cap
    token_ids = tok_class[:, 0]
    query_ids = query_class[:, 0]

    at = (core * fac_count + x) * share
    room = up_to(deep_g, LANES)
    blocks = []
    for step in range(tok_count):
        to = lax.rem(z + step, tok_count)
        blocks.append(
            jnp.concatenate(
                [
                    lax.dynamic_slice(gradients, (at, to * deep_g), (share, deep_g)),
                    jnp.zeros((share, room - deep_g), BF16),
                    lax.dynamic_slice(activations, (at, to * deep_a), (share, deep_a)),
                ],
                axis=1,
            )
        )
    moved = [blocks[0]] + [
        lax.ppermute(blocks[step], "tok", turn(tok_count, step)) for step in range(1, tok_count)
    ]

    qids = query_ids.reshape(fac_count, block)
    key = qids * block + jnp.arange(block)
    place = jnp.sum((key[:, None, :] < key[:, :, None]).astype(I32), axis=2)
    first = jnp.sum((qids == 0).astype(I32), axis=1)
    spot = (jnp.arange(CHUNKS)[:, None, None] * rows + jnp.arange(rows)) < first[None, :, None]
    spot = spot.reshape(query_ids.shape[0], 1).astype(I32)
    features = (query_gradients, query_inputs, basis_g, basis_a, fac_count, rows)
    parts = [query_coords(0, place, *features, blocks[1:]), None]

    ids = token_ids.reshape(halves, half_rows)
    earlier = jnp.arange(half_rows)[None, :] < jnp.arange(half_rows)[:, None]
    rank = jnp.sum(((ids[:, None, :] == ids[:, :, None]) & earlier).astype(I32), axis=2)
    slot = ids * slots + jnp.arange(halves)[:, None] * slot_cap + rank
    slot = slot.reshape(halves * fac_count, share)
    own_slot = lax.dynamic_index_in_dim(ids * slot_cap + rank, z * sub_count + core, 0).reshape(half_rows, 1)
    places = jnp.stack([z, core, x]).astype(I32)
    last = tok_count - 1
    behinds = (jnp.where(core == 0, z, last - z), jnp.where(core == 0, last - z, z))
    where_z = jnp.stack([*behinds, z, core, x]).astype(I32)

    state = {"pieces": []}

    def second(after):
        parts[1] = query_coords(1, place, *features, after)
        return parts[1][1]

    def joined(after):
        mine = join(moved, after)
        raws = [mine]
        for step in range(1, fac_count):
            raws.append(lax.ppermute(mine, "fac", turn(fac_count, step)))
        for step in range(1, sub_count):
            raws += [lax.ppermute(raw, "sub", turn(sub_count, step)) for raw in raws[:fac_count]]
        state["raws"] = raws
        return mine

    def packed(after):
        state["packed"] = pack(counts, places, slot, state["raws"], slots, deep_g, deep_a, after)
        return state["packed"][0]

    def token(side, column):
        def run(after):
            eigen, basis = ((eigen_g, basis_g), (eigen_a, basis_a))[side]
            segment = SEGMENT if side == 0 else width_a
            pair = token_coords(state["packed"][side], eigen, basis, column, segment, after)
            state["pieces"].append((side, column, pair))
            return pair[0]

        return run

    first_got, second_got = [], []
    groups, sent = [], []

    def batch(units, spans):
        def run(after):
            out = sides(
                counts, where_z, spot, units, spans, parts, first_got, second_got, state["pieces"], after
            )
            groups.append(tuple((klass, len(members) * rows) for klass, members in spans))
            sent.append(out)
            return out[0]

        return run

    columns = list(range(0, width_g, SEGMENT))
    fillers = [[joined, second], [packed, token(1, 0)]]
    fillers += [[token(0, column)] for column in columns]
    needs = {}
    for units in (range(4), range(4, 6), range(6, 8)):
        spans = [(k, [u for u in units if (u < HIGH, u >= LOW)[k]]) for k in range(2)]
        needs[len(fillers)] = units[-1] // GROUP + tok_count - 2
        fillers.append([batch(list(units), [span for span in spans if span[1]])])

    def over_plane(batches):
        totals = []
        for own, *others in batches:
            for step, other in enumerate(others, 1):
                own = own + lax.ppermute(other, "sub", turn(sub_count, step))
            totals.append(own)
        whole = totals[0] if len(totals) == 1 else jnp.concatenate(totals, axis=-1)
        total = whole[0]
        for step in range(1, fac_count):
            total = total + lax.ppermute(whole[step], "fac", turn(fac_count, step))
        return total

    def over_line(totals):
        whole = jnp.concatenate(totals, axis=-1)
        return [whole[0]] + [
            lax.ppermute(whole[step], "tok", turn(tok_count, step)) for step in range(1, tok_count)
        ]

    at_of = lambda chip, half: chip * sub_count + half
    rounds = []
    for upward in range(2):
        other = 1 - upward
        pairs = [(at_of(i, upward), at_of(i + 1, upward)) for i in range(last)]
        pairs += [(at_of(i + 1, other), at_of(i, other)) for i in range(last)]
        rounds.append(pairs + [(at_of(last, upward), at_of(last, other)), (at_of(0, other), at_of(0, upward))])
    swap = [(0, 1), (1, 0), (last, last - 1), (last - 1, last)]
    after = []
    chunks = CHUNKS // GROUP
    steps = chunks + tok_count - 2
    done = 0
    near_end = jnp.minimum(z, last - z)
    from_upper = (z >= tok_count // 2) == (core == 0)
    table = []
    for step in range(steps):
        if step < 2:
            table += [jnp.clip(step - near_end, 0, chunks - 1), jnp.int32(0), near_end] * 2
        elif step == steps - 1:
            table += [jnp.int32(chunks - 1), jnp.where(from_upper, 0, 1), jnp.int32(1)] * 2
        else:
            for behind in behinds:
                table += [jnp.clip(step - behind, 0, chunks - 1), jnp.int32(0), behind]
    table = jnp.stack([jnp.asarray(entry).astype(I32) for entry in table])
    for step in range(steps):
        early, late = max(step - tok_count + 1, 0) * GROUP, min(step, chunks - 1) * GROUP + GROUP - 1
        wanted = [parts[0] if early < HIGH else None, parts[1] if late >= LOW else None]
        if step == 0:
            packet = stage(table, 0, spot, [], wanted, after)
            came = lax.ppermute(packet, "tok", swap)
            first_got.append(came)
            second_got.append(came)
            after = [packet]
        elif step == 1:
            packet = stage(table, 2, spot, [first_got[-1]], wanted, after)
            first_got.append(lax.ppermute(packet, ("tok", "sub"), rounds[0]))
            second_got.append(lax.ppermute(packet, ("tok", "sub"), rounds[1]))
            after = [packet]
        elif step == steps - 1:
            got = [first_got[-1], second_got[-1]]
            packet = stage(table, 2 * step, spot, got, [None, parts[1]], after)
            came = lax.ppermute(packet, "tok", swap)
            first_got.append(came)
            second_got.append(came)
            after = [packet]
        else:
            for way, (got, pairs) in enumerate(((first_got, rounds[0]), (second_got, rounds[1]))):
                packet = stage(table, 2 * step + way, spot, got[-1:], wanted, after)
                got.append(lax.ppermute(packet, ("tok", "sub"), pairs))
                after = [packet]
        if step < steps - 1 and needs.get(done, -1) < step:
            for item in fillers[done]:
                after = [item(after)]
            done += 1
    for items in fillers[done:]:
        for item in items:
            after = [item(after)]
    sums = [over_line([over_plane(sent[:2]), over_plane(sent[2:])])]

    own_place = lax.dynamic_index_in_dim(place, x, 0)
    own_first = lax.dynamic_index_in_dim(first, x, 0)
    return final([groups], own_first, own_place, own_slot, sums).T


def solution(mesh):
    placed = (
        P(("grp", "tok"), None),
        P(("grp", "tok"), None),
        P("grp", None),
        P("grp", "tok"),
        P("grp", "tok"),
        P("grp", None),
        P(None, "tok", ("fac", "sub")),
        P(None, "tok", ("fac", "sub")),
        P(None, ("fac", "sub")),
        P(None, ("fac", "sub")),
    )
    return jax.shard_map(
        body, mesh=mesh, in_specs=placed, out_specs=P("fac", ("grp", "tok", "sub")), check_vma=False
    )
```
